128 devices in a mesh: doc: 2 (over core), head: 2 (over y_lo), seq: 32 (over x, z, y_hi).
Axes of the slice: x: 4, y: 4 (y_hi: 2, y_lo: 2; y = y_hi * 2 + y_lo), z: 4, core: 2. Of those that a mesh axis runs over, the one named last changes fastest.
Arguments:
- token_ids: int32 [2, 16384], P('doc', 'seq'), may hold values from 0 to 152063, as said below
- teacher_query: bfloat16 [2, 16384, 8192], P('doc', 'seq', 'head'), may hold values from -4.5 to 4.5
- teacher_value: bfloat16 [2, 16384, 1024], P('doc', 'seq', 'head'), may hold values from -4.5 to 4.5
- student_query: bfloat16 [2, 16384, 3584], P('doc', 'seq'), may hold values from -4.5 to 4.5
- student_value: bfloat16 [2, 16384, 512], P('doc', 'seq'), may hold values from -4.5 to 4.5
- teacher_pick: int32 [4], replicated, may hold values from 0 to 127
- student_pick: int32 [4], replicated, may hold values from 0 to 55
Outputs:
- grad_query: float32 [2, 16384, 256], P('doc', 'seq', 'head')
- grad_value: float32 [2, 16384, 256], P('doc', 'seq', 'head')
- loss: float32 [2], P('doc')
The draws below stay inside these ranges and needn't reach their ends.
Inputs may be any that keep to these rules, and one draw needn't show every extreme that they name: `token_ids`: 0 marks padding, which fills the tail of each document and is present in every document; at least half of a document's 16384 tokens are not padding; the first token of every document is the id 152064 - 1.
All inputs are finite; a program needn't handle non-finite values.
Results may differ from the reference program's by a relative error of at most 0.0023.
Values may be sent and summed in bfloat16 or wider, within the bound.
A program may use at most 128 MiB of HBM per device.

```python
import math
import jax
import jax.numpy as jnp
from jax import lax

T_HEADS = 64
T_KV = 8
S_HEADS = 28
S_KV = 4
HEAD_DIM = 128
VOCAB = 152064
REL_HEADS = 4
REL_WIDTH = 64
DOC_LEN = 16384
DOCS = 2


def rough_rows(key, shape, low, high, limit):
    key_norm, key_scale = jax.random.split(key)
    base = jax.random.normal(key_norm, shape, jnp.float32)
    scales = jnp.exp(jax.random.uniform(key_scale, shape[:-1] + (1,), jnp.float32, math.log(low), math.log(high)))
    return jnp.clip(base * scales, -limit, limit)


def draw_token_ids(key, part):
    key = jax.random.fold_in(key, 7)
    key_len, key_ids = jax.random.split(key)
    lengths = jax.random.randint(key_len, (DOCS, 1), DOC_LEN // 2, DOC_LEN)
    values = jax.random.randint(key_ids, (DOCS, DOC_LEN), 1, VOCAB)
    position = jnp.arange(DOC_LEN, dtype=jnp.int32)[None, :]
    values = jnp.where(position == 0, VOCAB - 1, values)
    return jnp.where(position < lengths, values, 0).astype(jnp.int32)


def draw_teacher_query(key, part):
    key = jax.random.fold_in(key, 3)
    shape = (DOCS, DOC_LEN, T_HEADS * HEAD_DIM)
    values = rough_rows(key, shape, 0.6, 1.6, 4.5)
    return values.astype(jnp.bfloat16)


def draw_teacher_value(key, part):
    key = jax.random.fold_in(key, 4)
    shape = (DOCS, DOC_LEN, T_KV * HEAD_DIM)
    values = rough_rows(key, shape, 0.6, 1.6, 4.5)
    return values.astype(jnp.bfloat16)


def draw_student_query(key, part):
    key = jax.random.fold_in(key, 5)
    shape = (DOCS, DOC_LEN, S_HEADS * HEAD_DIM)
    values = rough_rows(key, shape, 0.6, 1.6, 4.5)
    return values.astype(jnp.bfloat16)


def draw_student_value(key, part):
    key = jax.random.fold_in(key, 6)
    shape = (DOCS, DOC_LEN, S_KV * HEAD_DIM)
    values = rough_rows(key, shape, 0.6, 1.6, 4.5)
    return values.astype(jnp.bfloat16)


def place_ends(entries, key, low, high):
    shape = entries.shape
    spot = [jax.random.randint(jax.random.fold_in(key, axis), (), 0, shape[axis]) for axis in range(len(shape))]
    entries = entries.at[tuple(spot)].set(low)
    longest = shape.index(max(shape))
    spot[longest] = (spot[longest] + 1) % shape[longest]
    return entries.at[tuple(spot)].set(high)


def setup_inputs(seed: int = 0) -> dict:
    splits = jax.random.split(jax.random.key(seed), 8)
    return {
        "token_ids": draw_token_ids(jax.random.fold_in(splits[7], 71), 0),
        "teacher_query": draw_teacher_query(jax.random.fold_in(splits[7], 71), 0),
        "teacher_value": draw_teacher_value(jax.random.fold_in(splits[7], 71), 0),
        "student_query": draw_student_query(jax.random.fold_in(splits[7], 71), 0),
        "student_value": draw_student_value(jax.random.fold_in(splits[7], 71), 0),
        "teacher_pick": place_ends(jax.random.randint(splits[5], (REL_HEADS,), 0, T_HEADS * (HEAD_DIM // REL_WIDTH)), jax.random.fold_in(splits[5], 1), 0, (T_HEADS * (HEAD_DIM // REL_WIDTH)) - 1).astype(jnp.int32),
        "student_pick": place_ends(jax.random.randint(splits[6], (REL_HEADS,), 0, S_HEADS * (HEAD_DIM // REL_WIDTH)), jax.random.fold_in(splits[6], 1), 0, (S_HEADS * (HEAD_DIM // REL_WIDTH)) - 1).astype(jnp.int32),
    }


def pick_columns(array, block):
    return lax.dynamic_slice_in_dim(array, (block * REL_WIDTH).astype(jnp.int32), REL_WIDTH, 1)


def value_block(block, group):
    per_head = HEAD_DIM // REL_WIDTH
    return (block // per_head) // group * per_head + block % per_head


def relation(teach, stud, live):
    scale = REL_WIDTH ** -0.5
    length = teach.shape[0]
    width = math.gcd(length, 1024)
    count_blocks = length // width

    def scores(rows_x, all_x):
        return jnp.dot(rows_x, all_x.T, preferred_element_type=jnp.float32) * scale

    def log_sums(block_idx):
        start_row = (block_idx * width).astype(jnp.int32)
        outs = []
        for feats in (teach, stud):
            tile = scores(lax.dynamic_slice_in_dim(feats, start_row, width, 0), feats)
            masked = jnp.where(live[None, :], tile, -1e30)
            top = jnp.max(masked, axis=1)
            total = jnp.sum(jnp.where(live[None, :], jnp.exp(tile - top[:, None]), 0.0), axis=1)
            outs.append(top + jnp.log(total))
        return jnp.stack(outs, 0)

    stats = lax.map(log_sums, jnp.arange(count_blocks))
    lse_t = stats[:, 0].reshape(length)
    lse_s = stats[:, 1].reshape(length)

    def grads(block_idx):
        start_row = (block_idx * width).astype(jnp.int32)
        rows_t = lax.dynamic_slice_in_dim(teach, start_row, width, 0)
        rows_s = lax.dynamic_slice_in_dim(stud, start_row, width, 0)
        lt_rows = lax.dynamic_slice_in_dim(lse_t, start_row, width, 0)[:, None]
        ls_rows = lax.dynamic_slice_in_dim(lse_s, start_row, width, 0)[:, None]
        live_rows = lax.dynamic_slice_in_dim(live, start_row, width, 0)
        tile_t = scores(rows_t, teach)
        tile_s = scores(rows_s, stud)
        both = live_rows[:, None] & live[None, :]
        diff_rows = jnp.where(both, jnp.exp(tile_s - ls_rows) - jnp.exp(tile_t - lt_rows), 0.0)
        diff_cols = jnp.where(both, jnp.exp(tile_s - lse_s[None, :]) - jnp.exp(tile_t - lse_t[None, :]), 0.0)
        weights = (diff_rows + diff_cols).astype(jnp.bfloat16)
        grad = jnp.dot(weights, stud, preferred_element_type=jnp.float32) * scale
        kl_rows = jnp.sum(jnp.where(both, jnp.exp(tile_t - lt_rows) * (tile_t - tile_s), 0.0), axis=1)
        kl_sum = jnp.sum(jnp.where(live_rows, kl_rows - lt_rows[:, 0] + ls_rows[:, 0], 0.0))
        return grad, kl_sum

    grad_blocks, kl_blocks = lax.map(grads, jnp.arange(count_blocks))
    return grad_blocks.reshape(length, REL_WIDTH), jnp.sum(kl_blocks)


def reference(token_ids, teacher_query, teacher_value, student_query, student_value, teacher_pick, student_pick):
    query_out = []
    value_out = []
    losses = []
    for doc_idx in range(DOCS):
        live = token_ids[doc_idx] != 0
        count = jnp.sum(live.astype(jnp.float32))
        total = jnp.float32(0.0)
        query_parts = []
        value_parts = []
        for rel in range(REL_HEADS):
            t_block = teacher_pick[rel]
            s_block = student_pick[rel]
            t_vblock = value_block(t_block, T_HEADS // T_KV)
            s_vblock = value_block(s_block, S_HEADS // S_KV)
            grad_q, kl_q = relation(pick_columns(teacher_query[doc_idx], t_block), pick_columns(student_query[doc_idx], s_block), live)
            grad_v, kl_v = relation(pick_columns(teacher_value[doc_idx], t_vblock), pick_columns(student_value[doc_idx], s_vblock), live)
            query_parts.append(grad_q)
            value_parts.append(grad_v)
            total = total + kl_q + kl_v
        query_out.append(jnp.concatenate(query_parts, 1))
        value_out.append(jnp.concatenate(value_parts, 1))
        losses.append(total / (2.0 * REL_HEADS * count))
    return jnp.stack(query_out, 0), jnp.stack(value_out, 0), jnp.stack(losses, 0)
```

```python
import functools

import jax
import jax.numpy as jnp
from jax import lax
from jax.experimental import pallas as pl
from jax.experimental.pallas import tpu as pltpu
from jax.sharding import PartitionSpec as P

HEAD_DIM = 128
W = 64
PER_HEAD = HEAD_DIM // W
T_GROUP = 8
S_GROUP = 7
REL_HEADS = 4
LEN = 16384
ROWS = 512
PIECE = ROWS + 16
OWN = 2048
TOP_BOUND = 162.0
LN2 = 0.6931471805599453
SHIFT = 74.0
FAST_TOP = 130.0
BJ = 1024
F32 = jnp.float32
BF16 = jnp.bfloat16
MESH = pl.DeviceIdType.MESH
VMEM = pltpu.VMEM
ANY = pl.ANY


def coords():
    doc = lax.axis_index("doc")
    head = lax.axis_index("head")
    seq = lax.axis_index("seq")
    return doc, head, seq // 8, (seq // 2) % 4, seq % 2


def device(doc, head, x, z, yh):
    return (doc, head, (x * 4 + z) * 2 + yh)


def same(a, b):
    return (a[0] == b[0]) & (a[1] == b[1]) & (a[2] == b[2])


def params(**kw):
    return pltpu.CompilerParams(vmem_limit_bytes=56 * 2**20, **kw)


def pick_kernel(tp, sp, ids, tq, tv, sq, sv, msg_a, msg_b, tw, sw, sem):
    head = lax.axis_index("head")
    copies = []

    def fetch(src, block, dst):
        start = pl.multiple_of((block // 2) * 128, 128)
        copy = pltpu.make_async_copy(src.at[:, pl.ds(start, 128)], dst, sem.at[len(copies)])
        copy.start()
        copies.append(copy)

    q_blocks = tq.shape[1] // W
    v_blocks = tv.shape[1] // W
    for r in range(REL_HEADS):
        b = tp[r]
        vb = (b // PER_HEAD) // T_GROUP * PER_HEAD + b % PER_HEAD
        fetch(tq, b % q_blocks, tw.at[0, r])
        fetch(tv, vb % v_blocks, tw.at[1, r])
    for e in range(2):
        b = sp[head * 2 + e]
        vb = (b // PER_HEAD) // S_GROUP * PER_HEAD + b % PER_HEAD
        fetch(sq, b, sw.at[0, e])
        fetch(sv, vb, sw.at[1, e])
    for copy in copies:
        copy.wait()

    def half(w, b):
        return jnp.where(b % 2 == 0, w[:, :W], w[:, W:])

    live = (ids[...] != 0).astype(F32)
    tail = jnp.concatenate([live, jnp.zeros((12, 128), F32)], axis=0).astype(BF16)
    for k in range(2):
        for e in range(2):
            r = head * 2 + e
            t = half(tw[k, r], tp[r])
            s = half(sw[k, e], sp[r])
            msg_a[k, e, 0:ROWS, :] = jnp.concatenate([t, s], axis=1)
            msg_a[k, e, ROWS:PIECE, :] = tail
            r = (1 - head) * 2 + e
            t = half(tw[k, r], tp[r])
            msg_b[k, e] = jnp.concatenate([t[: ROWS // 2], t[ROWS // 2 :]], axis=1)


def pick(tp, sp, ids, tq, tv, sq, sv):
    smem = pl.BlockSpec(memory_space=pltpu.SMEM)
    vmem = pl.BlockSpec(memory_space=VMEM)
    hbm = pl.BlockSpec(memory_space=ANY)
    return pl.pallas_call(
        pick_kernel,
        out_shape=(
            jax.ShapeDtypeStruct((2, 2, PIECE, 128), BF16),
            jax.ShapeDtypeStruct((2, 2, ROWS // 2, 128), BF16),
        ),
        in_specs=[smem, smem, vmem, hbm, hbm, hbm, hbm],
        out_specs=(vmem, vmem),
        scratch_shapes=[
            VMEM((2, 4, ROWS, 128), BF16),
            VMEM((2, 2, ROWS, 128), BF16),
            pltpu.SemaphoreType.DMA((12,)),
        ],
        compiler_params=params(),
    )(tp, sp, ids, tq, tv, sq, sv)


def greet(peers, me):
    barrier = pltpu.get_barrier_semaphore()
    count = 0
    for peer in peers:
        other = jnp.logical_not(same(peer, me))

        @pl.when(other)
        def _():
            pl.semaphore_signal(barrier, inc=1, device_id=peer, device_id_type=MESH)

        count = count + other.astype(jnp.int32)
    pl.semaphore_wait(barrier, count)


def gather_kernel(
    tp, msg_a, msg_b, out, got_a, got_b, chunk,
    sa, sb, ra, rb, s_own, s_core, s_up, s_dn, r_core, r_up, r_dn,
):
    doc, head, x, z, yh = coords()
    me = device(doc, head, x, z, yh)
    core = device(1 - doc, head, x, z, yh)
    up = device(doc, head, x, (z + 1) % 4, yh)
    down = device(doc, head, x, (z + 3) % 4, yh)
    to_a = [[device(yh, head, 2 * doc + k, z, e) for e in range(2)] for k in range(2)]
    to_b = [[device(yh, 1 - head, 2 * doc + k, z, e) for e in range(2)] for k in range(2)]
    from_doc = x // 2
    sources = [device(from_doc, h, xs, z, doc) for h in range(2) for xs in range(4)]
    greet(to_a[0] + to_a[1] + to_b[0] + to_b[1] + sources + [core, up, down], me)

    for k in range(2):
        for e in range(2):
            mine = same(to_a[k][e], me)

            @pl.when(mine)
            def _():
                pltpu.make_async_copy(msg_a.at[k, e], got_a.at[x], ra.at[x]).start()

            @pl.when(jnp.logical_not(mine))
            def _():
                pltpu.make_async_remote_copy(
                    msg_a.at[k, e], got_a.at[x], sa.at[k, e], ra.at[x],
                    device_id=to_a[k][e], device_id_type=MESH,
                ).start()

            pltpu.make_async_remote_copy(
                msg_b.at[k, e], got_b.at[x], sb.at[k, e], rb.at[x],
                device_id=to_b[k][e], device_id_type=MESH,
            ).start()

    own = tp[head * 2 + yh] // (REL_HEADS * 16) == head

    def remote(src, dst, send, recv, to):
        return pltpu.make_async_remote_copy(
            src, dst, send, recv, device_id=to, device_id_type=MESH
        )

    def place(i, zz, c):
        return out.at[i, zz, c]

    sends = []
    lane = lax.broadcasted_iota(jnp.int32, (ROWS // 2, 128), 1)
    for i in range(4):
        pltpu.make_async_copy(msg_a.at[0, 0], got_a.at[i], ra.at[i]).wait()
        pltpu.make_async_copy(msg_b.at[0, 0], got_b.at[i], rb.at[i]).wait()
        b = got_b[i]
        b_roll = jnp.concatenate([b[:, W:], b[:, :W]], axis=1)
        keep = jnp.logical_or(own, lane >= W)
        chunk[i, 0 : ROWS // 2] = jnp.where(keep, got_a[i, 0 : ROWS // 2], b)
        chunk[i, ROWS // 2 : ROWS] = jnp.where(keep, got_a[i, ROWS // 2 : ROWS], b_roll)
        chunk[i, ROWS:PIECE] = got_a[i, ROWS:PIECE]
        for copy in (
            remote(chunk.at[i], place(i, z, doc), s_up.at[i], r_dn.at[i], up),
            remote(chunk.at[i], place(i, z, doc), s_dn.at[i], r_up.at[i], down),
            remote(chunk.at[i], place(i, z, doc), s_core.at[i], r_core.at[i], core),
        ):
            copy.start()
            sends.append(copy)
        local = pltpu.make_async_copy(chunk.at[i], place(i, z, doc), s_own.at[i])
        local.start()
        sends.append(local)

    below, above, across = (z + 3) % 4, (z + 1) % 4, (z + 2) % 4

    def forward(src, send, recv, to):
        copy = remote(src, src, send, recv, to)
        copy.start()
        sends.append(copy)

    def arrived(ref, sem):
        pltpu.make_async_copy(ref, ref, sem).wait()

    for i in range(4):
        lo = place(i, below, doc)
        arrived(lo, r_dn.at[i])
        if i < 2:
            forward(lo, s_up.at[4 + i], r_dn.at[4 + i], up)
        forward(lo, s_core.at[4 + i], r_core.at[4 + i], core)
        hi = place(i, above, doc)
        arrived(hi, r_up.at[i])
        if i >= 2:
            forward(hi, s_dn.at[2 + i], r_up.at[2 + i], down)
        forward(hi, s_core.at[8 + i], r_core.at[8 + i], core)
    for i in range(4):
        far = place(i, across, doc)
        arrived(far, r_dn.at[4 + i] if i < 2 else r_up.at[2 + i])
        forward(far, s_core.at[12 + i], r_core.at[12 + i], core)
    for i in range(4):
        arrived(place(i, z, 1 - doc), r_core.at[i])
        arrived(place(i, below, 1 - doc), r_core.at[4 + i])
        arrived(place(i, above, 1 - doc), r_core.at[8 + i])
        arrived(place(i, across, 1 - doc), r_core.at[12 + i])
    for copy in sends:
        if hasattr(copy, "wait_send") and copy.is_remote:
            copy.wait_send()
        else:
            copy.wait()
    for k in range(2):
        for e in range(2):

            @pl.when(jnp.logical_not(same(to_a[k][e], me)))
            def _():
                remote(msg_a.at[k, e], got_a.at[x], sa.at[k, e], ra.at[x], to_a[k][e]).wait_send()

            remote(msg_b.at[k, e], got_b.at[x], sb.at[k, e], rb.at[x], to_b[k][e]).wait_send()


def gather(tp, msg_a, msg_b):
    dma = pltpu.SemaphoreType.DMA
    vmem = pl.BlockSpec(memory_space=VMEM)
    return pl.pallas_call(
        gather_kernel,
        out_shape=jax.ShapeDtypeStruct((4, 4, 2, PIECE, 128), BF16),
        in_specs=[pl.BlockSpec(memory_space=pltpu.SMEM), vmem, vmem],
        out_specs=pl.BlockSpec(memory_space=ANY),
        scratch_shapes=[
            VMEM((4, PIECE, 128), BF16),
            VMEM((4, ROWS // 2, 128), BF16),
            VMEM((4, PIECE, 128), BF16),
            dma((2, 2)), dma((2, 2)), dma((4,)), dma((4,)),
            dma((4,)), dma((16,)), dma((6,)), dma((6,)), dma((16,)), dma((6,)), dma((6,)),
        ],
        compiler_params=params(collective_id=0, has_side_effects=True),
    )(tp, msg_a, msg_b)


def live_count(feats):
    total = jnp.zeros((16, 128), F32)
    for i in range(4):
        for zz in range(4):
            for c in range(2):
                total = total + feats[i, zz, c, ROWS:PIECE, :].astype(F32)
    return jnp.sum(total).astype(jnp.int32)


def fill_columns(feats, n, xa, ya):
    lane = lax.broadcasted_iota(jnp.int32, (ROWS, 128), 1)
    row = lax.broadcasted_iota(jnp.int32, (ROWS, 128), 0)
    ones = jnp.where((lane >= W) & (lane < W + 3), 1.0, 0.0)

    def one(b, _):
        f = feats[b // 8, (b // 2) % 4, b % 2, 0:ROWS, :]
        rest = jnp.where((lane == W + 3) & (row + b * ROWS >= n), -30000.0, ones).astype(BF16)
        at = pl.ds(pl.multiple_of(b * ROWS, ROWS), ROWS)
        xa[at, :] = jnp.where(lane < W, f, rest)
        turned = jnp.concatenate([f[:, W:], f[:, :W]], axis=1)
        ya[at, :] = jnp.where(lane < W, turned, rest)
        return 0

    lax.fori_loop(0, (n + ROWS - 1) // ROWS, one, 0)
    b = jnp.minimum((n + ROWS - 1) // ROWS, LEN // ROWS - 1)

    @pl.when(b * ROWS >= n)
    def _():
        one(b, 0)


def own_rows(feats, d, own):
    for m in range(16):
        b = 2 * m + d // 4
        part = feats[b // 8, (b // 2) % 4, b % 2, pl.ds(pl.multiple_of((d % 4) * 128, 128), 128), :]
        own[:, m * 128 : (m + 1) * 128] = part.T


def self_scores(feat):
    f = feat.astype(F32)
    return jnp.sum(f * f, axis=0, keepdims=True) * 0.125


def row_shift(own_score):
    room = 75.0 - (jnp.sqrt(own_score * TOP_BOUND) - own_score)
    k = jnp.floor(jnp.maximum(jnp.minimum(room, own_score), 0.0) * (1.0 / LN2))
    return own_score - k * LN2, k


def fill_rows(own, xi, yi):
    for ref, lo in ((xi, 0), (yi, W)):
        feat = own[lo : lo + W, :]
        shift, _ = row_shift(self_scores(feat))
        one = shift.astype(BF16).astype(F32)
        two = (shift - one).astype(BF16).astype(F32)
        three = shift - one - two
        at = lax.broadcasted_iota(jnp.int32, (16, OWN), 0)
        rest = jnp.where(at == 0, -one, jnp.where(at == 1, -two, jnp.where(at == 2, -three, jnp.where(at == 3, 1.0, 0.0))))
        ref[0:W, :] = feat * jnp.asarray(0.125, BF16)
        ref[W : W + 16, :] = rest.astype(BF16)
        ref[W + 16 :, :] = jnp.zeros((128 - W - 16, OWN), BF16)


def own_live(n, d):
    lane = lax.broadcasted_iota(jnp.int32, (1, OWN), 1)
    token = ((lane // 128) * 8 + d) * 128 + lane % 128
    return token < n


def row_tiles(n, d, tile):
    blocks = jnp.clip((n - d * 128 + 1023) // 1024, 0, 16)
    quarters = (blocks + 1) // 2
    full = quarters // 4

    def big(b, _):
        tile(pl.multiple_of(b * 1024, 1024), 1024)
        return 0

    lax.fori_loop(0, full, big, 0)
    rest = quarters % 4

    @pl.when(rest == 3)
    def _():
        tile(pl.multiple_of(full * 1024, 1024), 1024)

    @pl.when(rest == 2)
    def _():
        tile(pl.multiple_of(full * 1024, 1024), 512)

    @pl.when(rest == 1)
    def _():
        tile(pl.multiple_of(full * 1024, 1024), 256)


def sums_kernel(feats, out, own, xa, ya, xi, yi, sums):
    doc, _, _, z, _ = coords()
    d = z * 2 + doc
    n = live_count(feats)
    fill_columns(feats, n, xa, ya)
    own_rows(feats, d, own)
    fill_rows(own, xi, yi)
    sums[...] = jnp.ones_like(sums)
    steps = (n + BJ - 1) // BJ

    def tile(start, width):
        at = pl.ds(start, width)

        def step(j, carry):
            js = pl.ds(pl.multiple_of(j * BJ, BJ), BJ)
            t = jnp.exp(jnp.dot(xa[js, :], xi[:, at], preferred_element_type=F32))
            s = jnp.exp(jnp.dot(ya[js, :], yi[:, at], preferred_element_type=F32))
            add_t = jnp.sum(t.reshape(BJ // 8, 8, width), axis=0)
            add_s = jnp.sum(s.reshape(BJ // 8, 8, width), axis=0)
            return carry[0] + add_t, carry[1] + add_s

        zero = jnp.zeros((8, width), F32)
        t, s = lax.fori_loop(0, steps, step, (zero, zero))
        sums[0:1, at] = jnp.sum(t, axis=0, keepdims=True)
        sums[1:2, at] = jnp.sum(s, axis=0, keepdims=True)

    row_tiles(n, d, tile)
    live = own_live(n, d)
    st = self_scores(own[0:W, :])
    ss = self_scores(own[W:, :])
    lt = row_shift(st)[0] + jnp.log(sums[0:1, :])
    ls = row_shift(ss)[0] + jnp.log(sums[1:2, :])
    top = jnp.max(jnp.where(live, jnp.maximum(st, ss), 0.0))
    out[0:1, :] = jnp.where(live, lt, 0.0)
    out[1:2, :] = jnp.where(live, ls, 0.0)
    out[2:3, :] = jnp.full((1, OWN), top)
    out[3:4, :] = jnp.full((1, OWN), n.astype(F32))
    out[4:8, :] = jnp.zeros((4, OWN), F32)


def sums(feats):
    return pl.pallas_call(
        sums_kernel,
        out_shape=jax.ShapeDtypeStruct((8, OWN), F32),
        in_specs=[pl.BlockSpec(memory_space=VMEM)],
        out_specs=pl.BlockSpec(memory_space=VMEM),
        scratch_shapes=[
            VMEM((128, OWN), BF16),
            VMEM((LEN, 128), BF16),
            VMEM((LEN, 128), BF16),
            VMEM((128, OWN), BF16),
            VMEM((128, OWN), BF16),
            VMEM((8, OWN), F32),
        ],
        compiler_params=params(),
    )(feats)


def share_kernel(mine, out, s_own, send, recv):
    doc, head, x, z, yh = coords()
    me = device(doc, head, x, z, yh)
    d = z * 2 + doc
    peers = []
    for step in range(1, 8):
        p = (d + step) % 8
        peers.append(device(p % 2, head, x, p // 2, yh))
    greet(peers, me)
    copies = []
    for step in range(1, 8):
        copy = pltpu.make_async_remote_copy(
            mine, out.at[d], send.at[step - 1], recv.at[step - 1],
            device_id=peers[step - 1], device_id_type=MESH,
        )
        copy.start()
        copies.append(copy)
    local = pltpu.make_async_copy(mine, out.at[d], s_own)
    local.start()
    for step in range(1, 8):
        p = (d + 8 - step) % 8
        pltpu.make_async_copy(mine, out.at[p], recv.at[step - 1]).wait()
    for copy in copies:
        copy.wait_send()
    local.wait()


def share(mine):
    dma = pltpu.SemaphoreType.DMA
    vmem = pl.BlockSpec(memory_space=VMEM)
    return pl.pallas_call(
        share_kernel,
        out_shape=jax.ShapeDtypeStruct((8, 8, OWN), F32),
        in_specs=[vmem],
        out_specs=vmem,
        scratch_shapes=[dma, dma((7,)), dma((7,))],
        compiler_params=params(collective_id=1, has_side_effects=True),
    )(mine)


def grads_kernel(feats, lse, grad, kl, own, xa, ya, xi, yi, vt, vs, ot, os_):
    doc, _, _, z, _ = coords()
    d = z * 2 + doc
    n = live_count(feats)
    fill_columns(feats, n, xa, ya)
    own_rows(feats, d, own)
    fill_rows(own, xi, yi)
    steps = (n + BJ - 1) // BJ

    def weigh(b, _):
        f = feats[b // 8, (b // 2) % 4, b % 2, 0:ROWS, :].T
        x, y = f[:W, :], f[W:, :]
        yf = y.astype(F32)
        at = pl.ds(pl.multiple_of(b * ROWS, ROWS), ROWS)
        lt, ls = [], []
        for q in range(4):
            m = (b * 4 + q) // 8
            dd = (b * 4 + q) % 8
            ms = pl.ds(pl.multiple_of(m * 128, 128), 128)
            lt.append(lse[dd, 0:1, ms])
            ls.append(lse[dd, 1:2, ms])
        lane = lax.broadcasted_iota(jnp.int32, (1, ROWS), 1) + b * ROWS
        wt = jnp.where(lane < n, jnp.exp(SHIFT - jnp.concatenate(lt, axis=1)), 0.0)
        ws = jnp.where(lane < n, jnp.exp(SHIFT - jnp.concatenate(ls, axis=1)), 0.0)
        vt[0:W, at] = y
        vt[W : 2 * W, at] = (yf * wt).astype(BF16)
        vt[2 * W :, at] = x
        vs[0:W, at] = y
        vs[W:, at] = (yf * ws).astype(BF16)
        return 0

    lax.fori_loop(0, steps * (BJ // ROWS), weigh, 0)
    ot[...] = jnp.zeros_like(ot)
    os_[...] = jnp.zeros_like(os_)

    def tile(start, width):
        at = pl.ds(start, width)

        def step(j, _):
            js = pl.ds(pl.multiple_of(j * BJ, BJ), BJ)
            t = jnp.exp(jnp.dot(xa[js, :], xi[:, at], preferred_element_type=F32)).astype(BF16)
            s = jnp.exp(jnp.dot(ya[js, :], yi[:, at], preferred_element_type=F32)).astype(BF16)
            ot[:, at] += jnp.dot(vt[:, js], t, preferred_element_type=F32)
            os_[:, at] += jnp.dot(vs[:, js], s, preferred_element_type=F32)
            return 0

        lax.fori_loop(0, steps, step, 0)

    row_tiles(n, d, tile)
    live = own_live(n, d)
    x = own[0:W, :].astype(F32)
    y = own[W:, :].astype(F32)
    lt = lse[d, 0:1, :]
    ls = lse[d, 1:2, :]

    def finish(acc, feat, l):
        shift, k = row_shift(self_scores(feat))
        by_row = jnp.exp(shift - l)
        by_col = jnp.exp((shift - SHIFT) * 0.5)
        exact = y * jnp.exp(SHIFT - l)
        missing = (exact - exact.astype(BF16).astype(F32)) * jnp.exp2(k)
        return acc[0:W, :] * by_row + (acc[W : 2 * W, :] + missing) * by_col * by_col, by_row

    gs, _ = finish(os_, own[W:, :], ls)
    gt, by_row = finish(ot, own[0:W, :], lt)
    grad[...] = jnp.where(live, (gs - gt) * 0.125, 0.0)
    moved = jnp.sum(x * ot[2 * W :, :] - y * ot[0:W, :], axis=0, keepdims=True)
    rows = jnp.where(live, moved * by_row * 0.125 - lt + ls, 0.0)
    acc = rows[:, 0:128]
    for m in range(1, 16):
        acc = acc + rows[:, m * 128 : (m + 1) * 128]
    at = lax.broadcasted_iota(jnp.int32, (8, 128), 0)
    kl[...] = jnp.where(at == 0, acc, jnp.where(at == 1, n.astype(F32), 0.0))


def grads(feats, lse):
    vmem = pl.BlockSpec(memory_space=VMEM)
    return pl.pallas_call(
        grads_kernel,
        out_shape=(jax.ShapeDtypeStruct((W, OWN), F32), jax.ShapeDtypeStruct((8, 128), F32)),
        in_specs=[vmem, vmem],
        out_specs=(vmem, vmem),
        scratch_shapes=[
            VMEM((128, OWN), BF16),
            VMEM((LEN, 128), BF16),
            VMEM((LEN, 128), BF16),
            VMEM((128, OWN), BF16),
            VMEM((128, OWN), BF16),
            VMEM((3 * W, LEN), BF16),
            VMEM((2 * W, LEN), BF16),
            VMEM((3 * W, OWN), F32),
            VMEM((2 * W, OWN), F32),
        ],
        compiler_params=params(),
    )(feats, lse)


def grads_wide(feats, lse):
    doc, _, _, z, _ = coords()
    d = z * 2 + doc
    n = lse[0, 3, 0].astype(jnp.int32)
    f = feats[:, :, :, :ROWS, :].reshape(LEN // 1024, 8, 128, 128)
    mine = lax.dynamic_index_in_dim(f, d, 1, keepdims=False).reshape(OWN, 128)
    cols = f.reshape(LEN // 1024, 1024, 128)
    col_lse = jnp.transpose(lse[:, :2].reshape(8, 2, 16, 128), (2, 1, 0, 3)).reshape(16, 2, 1024)
    own_lse = lax.dynamic_index_in_dim(lse, d, 0, keepdims=False)
    lt, ls = own_lse[0][:, None], own_lse[1][:, None]
    lane = jnp.arange(OWN)
    live = (((lane // 128) * 8 + d) * 128 + lane % 128 < n)[:, None]

    def step(j, carry):
        grad, kl = carry
        c = lax.dynamic_index_in_dim(cols, j, 0, keepdims=False)
        cl = lax.dynamic_index_in_dim(col_lse, j, 0, keepdims=False)
        both = live & (j * 1024 + jnp.arange(1024) < n)[None, :]
        t = jnp.dot(mine[:, :W], c[:, :W].T, preferred_element_type=F32) * 0.125
        s = jnp.dot(mine[:, W:], c[:, W:].T, preferred_element_type=F32) * 0.125
        pt = jnp.where(both, jnp.exp(t - lt), 0.0)
        rows = jnp.where(both, jnp.exp(s - ls), 0.0) - pt
        columns = jnp.where(both, jnp.exp(s - cl[1:2]) - jnp.exp(t - cl[0:1]), 0.0)
        w = (rows + columns).astype(BF16)
        grad = grad + jnp.dot(w, c[:, W:], preferred_element_type=F32) * 0.125
        return grad, kl + jnp.sum(pt * (t - s), axis=1, keepdims=True)

    zero = (jnp.zeros((OWN, W), F32), jnp.zeros((OWN, 1), F32))
    grad, kl = lax.fori_loop(0, 16, step, zero)
    rows = jnp.where(live, kl - lt + ls, 0.0).reshape(16, 128)
    tile = jnp.concatenate(
        [jnp.sum(rows, axis=0, keepdims=True), jnp.full((1, 128), n.astype(F32)), jnp.zeros((6, 128), F32)]
    )
    return grad.T, tile


def give_kernel(grad, kl, gq, gv, loss, got, got_kl, sums, got_sum, sg, rg, sk, rk, ss, rs):
    doc, head, x, z, yh = coords()
    me = device(doc, head, x, z, yh)
    d = z * 2 + doc
    to = [device(x // 2, head, m // 4, m % 4, z // 2) for m in range(16)]
    sources = []
    for k in range(2):
        for e in range(2):
            for q in range(4):
                sources.append(device(q % 2, head, 2 * doc + k, 2 * yh + q // 2, e))
    ring = [device(doc, 1 - head, x, z, yh), device(doc, head, x, z, 1 - yh), device(doc, 1 - head, x, z, 1 - yh)]
    greet(to + sources + ring, me)
    kind, part, q = x % 2, yh, d % 4
    slot = (kind * 2 + part) * 4 + q
    where = pl.ds(pl.multiple_of(part * W, W), W)
    for m in range(16):
        mine = same(to[m], me)
        src = grad.at[:, m * 128 : (m + 1) * 128]

        @pl.when(mine)
        def _():
            pltpu.make_async_copy(src, got.at[kind, q, where], rg.at[slot]).start()
            pltpu.make_async_copy(kl, got_kl.at[slot], rk.at[slot]).start()

        @pl.when(jnp.logical_not(mine))
        def _():
            pltpu.make_async_remote_copy(
                src, got.at[kind, q, where], sg.at[m], rg.at[slot], device_id=to[m], device_id_type=MESH
            ).start()
            pltpu.make_async_remote_copy(
                kl, got_kl.at[slot], sk.at[m], rk.at[slot], device_id=to[m], device_id_type=MESH
            ).start()

    total = jnp.zeros((8, 128), F32)
    for i in range(16):
        pltpu.make_async_copy(kl, got_kl.at[i], rk.at[i]).wait()
        total = total + got_kl[i]
    sums[...] = total
    swaps = []
    for i in range(3):
        copy = pltpu.make_async_remote_copy(
            sums, got_sum.at[i], ss.at[i], rs.at[i], device_id=ring[i], device_id_type=MESH
        )
        copy.start()
        swaps.append(copy)
    for k, out in ((0, gq), (1, gv)):
        for q_ in range(4):
            for e in range(2):
                part_ref = got.at[k, q_, pl.ds(e * W, W)]
                pltpu.make_async_copy(part_ref, part_ref, rg.at[(k * 2 + e) * 4 + q_]).wait()
            out[q_ * 128 : (q_ + 1) * 128, :] = got[k, q_].T
    for i in range(3):
        swaps[i].wait_recv()
        total = total + got_sum[i]
    for i in range(3):
        swaps[i].wait_send()
    kl_sum = jnp.sum(total[0:1, :], axis=1, keepdims=True)
    count = total[1:2, 0:1] * (1.0 / 64.0)
    loss[...] = jnp.broadcast_to(kl_sum / (count * (2.0 * REL_HEADS)), (8, 128))
    for m in range(16):
        src = grad.at[:, m * 128 : (m + 1) * 128]

        @pl.when(jnp.logical_not(same(to[m], me)))
        def _():
            pltpu.make_async_remote_copy(
                src, got.at[kind, q, where], sg.at[m], rg.at[slot], device_id=to[m], device_id_type=MESH
            ).wait_send()
            pltpu.make_async_remote_copy(
                kl, got_kl.at[slot], sk.at[m], rk.at[slot], device_id=to[m], device_id_type=MESH
            ).wait_send()


def give(grad, kl):
    dma = pltpu.SemaphoreType.DMA
    vmem = pl.BlockSpec(memory_space=VMEM)
    out = jax.ShapeDtypeStruct((ROWS, 128), F32)
    return pl.pallas_call(
        give_kernel,
        out_shape=(out, out, jax.ShapeDtypeStruct((8, 128), F32)),
        in_specs=[vmem, vmem],
        out_specs=(vmem, vmem, vmem),
        scratch_shapes=[
            VMEM((2, 4, 128, 128), F32),
            VMEM((16, 8, 128), F32),
            VMEM((8, 128), F32),
            VMEM((3, 8, 128), F32),
            dma((16,)), dma((16,)), dma((16,)), dma((16,)), dma((3,)), dma((3,)),
        ],
        compiler_params=params(collective_id=2, has_side_effects=True),
    )(grad, kl)


def shards(token_ids, teacher_query, teacher_value, student_query, student_value, teacher_pick, student_pick):
    msg_a, msg_b = pick(
        teacher_pick, student_pick, token_ids.reshape(4, 128),
        teacher_query[0], teacher_value[0], student_query[0], student_value[0],
    )
    feats = gather(teacher_pick, msg_a, msg_b)
    lse = share(sums(feats))
    fast = jnp.max(lse[:, 2, 0]) <= FAST_TOP
    grad, kl = lax.cond(fast, grads, grads_wide, feats, lse)
    gq, gv, loss = give(grad, kl)
    return gq[None], gv[None], loss[0, :1]


def solution(mesh):
    return jax.shard_map(
        shards,
        mesh=mesh,
        in_specs=(
            P("doc", "seq"),
            P("doc", "seq", "head"),
            P("doc", "seq", "head"),
            P("doc", "seq", None),
            P("doc", "seq", None),
            P(),
            P(),
        ),
        out_specs=(P("doc", "seq", "head"), P("doc", "seq", "head"), P("doc")),
        check_vma=False,
    )
```

```python
import functools

import jax
import jax.numpy as jnp
from jax import lax
from jax.experimental import pallas as pl
from jax.experimental.pallas import tpu as pltpu
from jax.sharding import PartitionSpec as P

HEAD_DIM = 128
W = 64
PER_HEAD = HEAD_DIM // W
T_GROUP = 8
S_GROUP = 7
REL_HEADS = 4
LEN = 16384
ROWS = 512
PIECE = ROWS + 16
OWN = 2048
TOP_BOUND = 162.0
LN2 = 0.6931471805599453
LOG2E = 1.4426950408889634
SHIFT = 74.0
FAST_TOP = 130.0
BJ = 1024
F32 = jnp.float32
BF16 = jnp.bfloat16
MESH = pl.DeviceIdType.MESH
VMEM = pltpu.VMEM
ANY = pl.ANY


def coords():
    doc = lax.axis_index("doc")
    head = lax.axis_index("head")
    seq = lax.axis_index("seq")
    return doc, head, seq // 8, (seq // 2) % 4, seq % 2


def device(doc, head, x, z, yh):
    return (doc, head, (x * 4 + z) * 2 + yh)


def same(a, b):
    return (a[0] == b[0]) & (a[1] == b[1]) & (a[2] == b[2])


def params(**kw):
    return pltpu.CompilerParams(vmem_limit_bytes=56 * 2**20, **kw)


def pick_kernel(tp, sp, ids, tq, tv, sq, sv, msg_a, msg_b, tw, sw, sem):
    head = lax.axis_index("head")
    copies = []

    def fetch(src, block, dst):
        start = pl.multiple_of((block // 2) * 128, 128)
        copy = pltpu.make_async_copy(src.at[:, pl.ds(start, 128)], dst, sem.at[len(copies)])
        copy.start()
        copies.append(copy)

    q_blocks = tq.shape[1] // W
    v_blocks = tv.shape[1] // W
    for r in range(REL_HEADS):
        b = tp[r]
        vb = (b // PER_HEAD) // T_GROUP * PER_HEAD + b % PER_HEAD
        fetch(tq, b % q_blocks, tw.at[0, r])
        fetch(tv, vb % v_blocks, tw.at[1, r])
    for e in range(2):
        b = sp[head * 2 + e]
        vb = (b // PER_HEAD) // S_GROUP * PER_HEAD + b % PER_HEAD
        fetch(sq, b, sw.at[0, e])
        fetch(sv, vb, sw.at[1, e])
    for copy in copies:
        copy.wait()

    def half(w, b):
        return jnp.where(b % 2 == 0, w[:, :W], w[:, W:])

    live = (ids[...] != 0).astype(F32)
    tail = jnp.concatenate([live, jnp.zeros((12, 128), F32)], axis=0).astype(BF16)
    for k in range(2):
        for e in range(2):
            r = head * 2 + e
            t = half(tw[k, r], tp[r])
            s = half(sw[k, e], sp[r])
            msg_a[k, e, 0:ROWS, :] = jnp.concatenate([t, s], axis=1)
            msg_a[k, e, ROWS:PIECE, :] = tail
            r = (1 - head) * 2 + e
            t = half(tw[k, r], tp[r])
            msg_b[k, e] = jnp.concatenate([t[: ROWS // 2], t[ROWS // 2 :]], axis=1)


def pick(tp, sp, ids, tq, tv, sq, sv):
    smem = pl.BlockSpec(memory_space=pltpu.SMEM)
    vmem = pl.BlockSpec(memory_space=VMEM)
    hbm = pl.BlockSpec(memory_space=ANY)
    return pl.pallas_call(
        pick_kernel,
        out_shape=(
            jax.ShapeDtypeStruct((2, 2, PIECE, 128), BF16),
            jax.ShapeDtypeStruct((2, 2, ROWS // 2, 128), BF16),
        ),
        in_specs=[smem, smem, vmem, hbm, hbm, hbm, hbm],
        out_specs=(vmem, vmem),
        scratch_shapes=[
            VMEM((2, 4, ROWS, 128), BF16),
            VMEM((2, 2, ROWS, 128), BF16),
            pltpu.SemaphoreType.DMA((12,)),
        ],
        compiler_params=params(),
    )(tp, sp, ids, tq, tv, sq, sv)


def greet(peers, me):
    barrier = pltpu.get_barrier_semaphore()
    count = 0
    for peer in peers:
        other = jnp.logical_not(same(peer, me))

        @pl.when(other)
        def _():
            pl.semaphore_signal(barrier, inc=1, device_id=peer, device_id_type=MESH)

        count = count + other.astype(jnp.int32)
    pl.semaphore_wait(barrier, count)


def gather_kernel(
    tp, msg_a, msg_b, out, got_a, got_b, chunk,
    sa, sb, ra, rb, s_own, s_core, s_up, s_dn, r_core, r_up, r_dn,
):
    doc, head, x, z, yh = coords()
    me = device(doc, head, x, z, yh)
    core = device(1 - doc, head, x, z, yh)
    up = device(doc, head, x, (z + 1) % 4, yh)
    down = device(doc, head, x, (z + 3) % 4, yh)
    to_a = [[device(yh, head, 2 * doc + k, z, e) for e in range(2)] for k in range(2)]
    to_b = [[device(yh, 1 - head, 2 * doc + k, z, e) for e in range(2)] for k in range(2)]
    from_doc = x // 2
    sources = [device(from_doc, h, xs, z, doc) for h in range(2) for xs in range(4)]
    greet(to_a[0] + to_a[1] + to_b[0] + to_b[1] + sources + [core, up, down], me)

    for k in range(2):
        for e in range(2):
            mine = same(to_a[k][e], me)

            @pl.when(mine)
            def _():
                pltpu.make_async_copy(msg_a.at[k, e], got_a.at[x], ra.at[x]).start()

            @pl.when(jnp.logical_not(mine))
            def _():
                pltpu.make_async_remote_copy(
                    msg_a.at[k, e], got_a.at[x], sa.at[k, e], ra.at[x],
                    device_id=to_a[k][e], device_id_type=MESH,
                ).start()

            pltpu.make_async_remote_copy(
                msg_b.at[k, e], got_b.at[x], sb.at[k, e], rb.at[x],
                device_id=to_b[k][e], device_id_type=MESH,
            ).start()

    own = tp[head * 2 + yh] // (REL_HEADS * 16) == head

    def remote(src, dst, send, recv, to):
        return pltpu.make_async_remote_copy(
            src, dst, send, recv, device_id=to, device_id_type=MESH
        )

    def place(i, zz, c):
        return out.at[order[i], zz, c]

    sends = []
    lane = lax.broadcasted_iota(jnp.int32, (ROWS // 2, 128), 1)
    order = [x, (x + 1) % 4, (x + 3) % 4, (x + 2) % 4]
    for i, xs in enumerate(order):
        pltpu.make_async_copy(msg_a.at[0, 0], got_a.at[xs], ra.at[xs]).wait()
        pltpu.make_async_copy(msg_b.at[0, 0], got_b.at[xs], rb.at[xs]).wait()
        b = got_b[xs]
        b_roll = jnp.concatenate([b[:, W:], b[:, :W]], axis=1)
        keep = jnp.logical_or(own, lane >= W)
        chunk[i, 0 : ROWS // 2] = jnp.where(keep, got_a[xs, 0 : ROWS // 2], b)
        chunk[i, ROWS // 2 : ROWS] = jnp.where(keep, got_a[xs, ROWS // 2 : ROWS], b_roll)
        chunk[i, ROWS:PIECE] = got_a[xs, ROWS:PIECE]
        for copy in (
            remote(chunk.at[i], place(i, z, doc), s_up.at[i], r_dn.at[i], up),
            remote(chunk.at[i], place(i, z, doc), s_dn.at[i], r_up.at[i], down),
            remote(chunk.at[i], place(i, z, doc), s_core.at[i], r_core.at[i], core),
        ):
            copy.start()
            sends.append(copy)
        local = pltpu.make_async_copy(chunk.at[i], place(i, z, doc), s_own.at[i])
        local.start()
        sends.append(local)

    below, above, across = (z + 3) % 4, (z + 1) % 4, (z + 2) % 4

    def forward(src, send, recv, to):
        copy = remote(src, src, send, recv, to)
        copy.start()
        sends.append(copy)

    def arrived(ref, sem):
        pltpu.make_async_copy(ref, ref, sem).wait()

    for i in range(4):
        lo = place(i, below, doc)
        arrived(lo, r_dn.at[i])
        if i < 2:
            forward(lo, s_up.at[4 + i], r_dn.at[4 + i], up)
        forward(lo, s_core.at[4 + i], r_core.at[4 + i], core)
        hi = place(i, above, doc)
        arrived(hi, r_up.at[i])
        if i >= 2:
            forward(hi, s_dn.at[2 + i], r_up.at[2 + i], down)
        forward(hi, s_core.at[8 + i], r_core.at[8 + i], core)
    for i in range(4):
        far = place(i, across, doc)
        arrived(far, r_dn.at[4 + i] if i < 2 else r_up.at[2 + i])
        forward(far, s_core.at[12 + i], r_core.at[12 + i], core)
    for i in range(4):
        arrived(place(i, z, 1 - doc), r_core.at[i])
        arrived(place(i, below, 1 - doc), r_core.at[4 + i])
        arrived(place(i, above, 1 - doc), r_core.at[8 + i])
        arrived(place(i, across, 1 - doc), r_core.at[12 + i])
    for copy in sends:
        if hasattr(copy, "wait_send") and copy.is_remote:
            copy.wait_send()
        else:
            copy.wait()
    for k in range(2):
        for e in range(2):

            @pl.when(jnp.logical_not(same(to_a[k][e], me)))
            def _():
                remote(msg_a.at[k, e], got_a.at[x], sa.at[k, e], ra.at[x], to_a[k][e]).wait_send()

            remote(msg_b.at[k, e], got_b.at[x], sb.at[k, e], rb.at[x], to_b[k][e]).wait_send()


def gather(tp, msg_a, msg_b):
    dma = pltpu.SemaphoreType.DMA
    vmem = pl.BlockSpec(memory_space=VMEM)
    return pl.pallas_call(
        gather_kernel,
        out_shape=jax.ShapeDtypeStruct((4, 4, 2, PIECE, 128), BF16),
        in_specs=[pl.BlockSpec(memory_space=pltpu.SMEM), vmem, vmem],
        out_specs=pl.BlockSpec(memory_space=ANY),
        scratch_shapes=[
            VMEM((4, PIECE, 128), BF16),
            VMEM((4, ROWS // 2, 128), BF16),
            VMEM((4, PIECE, 128), BF16),
            dma((2, 2)), dma((2, 2)), dma((4,)), dma((4,)),
            dma((4,)), dma((16,)), dma((6,)), dma((6,)), dma((16,)), dma((6,)), dma((6,)),
        ],
        compiler_params=params(collective_id=0, has_side_effects=True),
    )(tp, msg_a, msg_b)


def live_count(feats):
    total = jnp.zeros((16, 128), F32)
    for i in range(4):
        for zz in range(4):
            for c in range(2):
                total = total + feats[i, zz, c, ROWS:PIECE, :].astype(F32)
    return jnp.sum(total).astype(jnp.int32)


def block(feats, b):
    return feats[b // 8, (b // 2) % 4, b % 2, 0:ROWS, :]


def tile_scores(feats, j, rows):
    parts = []
    for half in range(BJ // ROWS):
        parts.append(jnp.dot(block(feats, j * (BJ // ROWS) + half), rows, preferred_element_type=F32))
    return jnp.concatenate(parts, axis=0)


def own_rows(feats, d, own):
    for m in range(16):
        b = 2 * m + d // 4
        part = feats[b // 8, (b // 2) % 4, b % 2, pl.ds(pl.multiple_of((d % 4) * 128, 128), 128), :]
        own[:, m * 128 : (m + 1) * 128] = part.T


def self_scores(feat):
    f = feat.astype(F32)
    return jnp.sum(f * f, axis=0, keepdims=True) * 0.125


def row_shift(own_score):
    room = 75.0 - (jnp.sqrt(own_score * TOP_BOUND) - own_score)
    k = jnp.floor(jnp.maximum(jnp.minimum(room, own_score), 0.0) * LOG2E)
    return own_score * LOG2E - k, k


def fill_rows(own, xi, yi, shifts):
    zero = jnp.zeros((W, OWN), BF16)
    xi[0:W, :] = own[0:W, :] * jnp.asarray(0.125, BF16)
    xi[W:, :] = zero
    yi[0:W, :] = zero
    yi[W:, :] = own[W:, :] * jnp.asarray(0.125, BF16)
    shifts[0:1, :] = row_shift(self_scores(own[0:W, :]))[0]
    shifts[1:2, :] = row_shift(self_scores(own[W:, :]))[0]


def own_live(n, d):
    lane = lax.broadcasted_iota(jnp.int32, (1, OWN), 1)
    token = ((lane // 128) * 8 + d) * 128 + lane % 128
    return token < n


def row_tiles(n, d, tile):
    blocks = jnp.clip((n - d * 128 + 1023) // 1024, 0, 16)
    quarters = (blocks + 1) // 2
    full = quarters // 4

    def big(b, _):
        tile(pl.multiple_of(b * 1024, 1024), 1024)
        return 0

    lax.fori_loop(0, full, big, 0)
    rest = quarters % 4

    @pl.when(rest == 3)
    def _():
        tile(pl.multiple_of(full * 1024, 1024), 1024)

    @pl.when(rest == 2)
    def _():
        tile(pl.multiple_of(full * 1024, 1024), 512)

    @pl.when(rest == 1)
    def _():
        tile(pl.multiple_of(full * 1024, 1024), 256)


def sums_kernel(feats, out, own, xi, yi, shifts, acc_t, acc_s):
    doc, _, _, z, _ = coords()
    d = doc * 4 + z
    n = live_count(feats)
    own_rows(feats, d, own)
    fill_rows(own, xi, yi, shifts)
    acc_t[...] = jnp.ones_like(acc_t)
    acc_s[...] = jnp.ones_like(acc_s)
    steps = n // BJ

    def tile(start, width):
        at = pl.ds(start, width)

        def step(j, carry, mask=False):
            t = jnp.exp2(tile_scores(feats, j, xi[:, at]) * LOG2E - shifts[0:1, at])
            s = jnp.exp2(tile_scores(feats, j, yi[:, at]) * LOG2E - shifts[1:2, at])
            if mask:
                alive = lax.broadcasted_iota(jnp.int32, (BJ, width), 0) + j * BJ < n
                t = jnp.where(alive, t, 0.0)
                s = jnp.where(alive, s, 0.0)
            add_t = jnp.sum(t.reshape(BJ // 8, 8, width), axis=0)
            add_s = jnp.sum(s.reshape(BJ // 8, 8, width), axis=0)
            return carry[0] + add_t, carry[1] + add_s

        zero = jnp.zeros((8, width), F32)
        t, s = lax.fori_loop(0, steps, step, (zero, zero))
        acc_t[:, at] = t
        acc_s[:, at] = s

        @pl.when(steps * BJ < n)
        def _():
            t, s = step(steps, (acc_t[:, at], acc_s[:, at]), True)
            acc_t[:, at] = t
            acc_s[:, at] = s

    row_tiles(n, d, tile)
    live = own_live(n, d)
    st = self_scores(own[0:W, :])
    ss = self_scores(own[W:, :])
    lt = shifts[0:1, :] * LN2 + jnp.log(jnp.sum(acc_t[...], axis=0, keepdims=True))
    ls = shifts[1:2, :] * LN2 + jnp.log(jnp.sum(acc_s[...], axis=0, keepdims=True))
    top = jnp.max(jnp.where(live, jnp.maximum(st, ss), 0.0))
    lt = jnp.where(live, lt, 0.0)
    ls = jnp.where(live, ls, 0.0)
    for m in range(16):
        out[m : m + 1, :] = lt[:, m * 128 : (m + 1) * 128]
        out[16 + m : 17 + m, :] = ls[:, m * 128 : (m + 1) * 128]
    at = lax.broadcasted_iota(jnp.int32, (8, 128), 0)
    out[32:40, :] = jnp.where(at == 0, top, jnp.where(at == 1, n.astype(F32), 0.0))


def sums(feats):
    return pl.pallas_call(
        sums_kernel,
        out_shape=jax.ShapeDtypeStruct((40, 128), F32),
        in_specs=[pl.BlockSpec(memory_space=VMEM)],
        out_specs=pl.BlockSpec(memory_space=VMEM),
        scratch_shapes=[
            VMEM((128, OWN), BF16),
            VMEM((128, OWN), BF16),
            VMEM((128, OWN), BF16),
            VMEM((8, OWN), F32),
            VMEM((8, OWN), F32),
            VMEM((8, OWN), F32),
        ],
        compiler_params=params(),
    )(feats)


def share_kernel(mine, out, s_own, send, recv):
    doc, head, x, z, yh = coords()
    me = device(doc, head, x, z, yh)
    d = doc * 4 + z
    peers = []
    for step in range(1, 8):
        p = (d + step) % 8
        peers.append(device(p // 4, head, x, p % 4, yh))
    greet(peers, me)
    copies = []
    for step in range(1, 8):
        copy = pltpu.make_async_remote_copy(
            mine, out.at[d], send.at[step - 1], recv.at[step - 1],
            device_id=peers[step - 1], device_id_type=MESH,
        )
        copy.start()
        copies.append(copy)
    local = pltpu.make_async_copy(mine, out.at[d], s_own)
    local.start()
    for step in range(1, 8):
        p = (d + 8 - step) % 8
        pltpu.make_async_copy(mine, out.at[p], recv.at[step - 1]).wait()
    for copy in copies:
        copy.wait_send()
    local.wait()


def share(mine):
    dma = pltpu.SemaphoreType.DMA
    vmem = pl.BlockSpec(memory_space=VMEM)
    return pl.pallas_call(
        share_kernel,
        out_shape=jax.ShapeDtypeStruct((8, 40, 128), F32),
        in_specs=[vmem],
        out_specs=vmem,
        scratch_shapes=[dma, dma((7,)), dma((7,))],
        compiler_params=params(collective_id=1, has_side_effects=True),
    )(mine)


def grads_kernel(feats, lse, grad, kl, own, xi, yi, shifts, v, ot, os_):
    doc, _, _, z, _ = coords()
    d = doc * 4 + z
    n = jnp.max(lse[0, 33:34, :]).astype(jnp.int32)
    own_rows(feats, d, own)
    fill_rows(own, xi, yi, shifts)
    steps = (n + BJ - 1) // BJ

    def weigh(b, _):
        f = block(feats, b).T
        x, y = f[:W, :], f[W:, :]
        yf = y.astype(F32)
        at = pl.ds(pl.multiple_of(b * ROWS, ROWS), ROWS)
        lt, ls = [], []
        for q in range(4):
            m = (b * 4 + q) // 8
            dd = (b * 4 + q) % 8
            lt.append(lse[dd, pl.ds(m, 1), :])
            ls.append(lse[dd, pl.ds(16 + m, 1), :])
        live = lax.broadcasted_iota(jnp.int32, (1, ROWS), 1) + b * ROWS < n
        wt = jnp.where(live, jnp.exp(SHIFT - jnp.concatenate(lt, axis=1)), 0.0)
        ws = jnp.where(live, jnp.exp(SHIFT - jnp.concatenate(ls, axis=1)), 0.0)
        keep = jnp.where(live, 1.0, 0.0).astype(BF16)
        v[0:W, at] = x * keep
        v[W : 2 * W, at] = (yf * wt).astype(BF16)
        v[2 * W : 3 * W, at] = y * keep
        v[3 * W :, at] = (yf * ws).astype(BF16)
        return 0

    lax.fori_loop(0, steps * (BJ // ROWS), weigh, 0)
    ot[...] = jnp.zeros_like(ot)
    os_[...] = jnp.zeros_like(os_)

    def tile(start, width):
        at = pl.ds(start, width)

        def step(j, _):
            js = pl.ds(pl.multiple_of(j * BJ, BJ), BJ)
            t = jnp.exp2(tile_scores(feats, j, xi[:, at]) * LOG2E - shifts[0:1, at]).astype(BF16)
            s = jnp.exp2(tile_scores(feats, j, yi[:, at]) * LOG2E - shifts[1:2, at]).astype(BF16)
            ot[:, at] += jnp.dot(v[0 : 3 * W, js], t, preferred_element_type=F32)
            os_[:, at] += jnp.dot(v[2 * W :, js], s, preferred_element_type=F32)
            return 0

        lax.fori_loop(0, steps, step, 0)

    row_tiles(n, d, tile)
    live = own_live(n, d)
    x = own[0:W, :].astype(F32)
    y = own[W:, :].astype(F32)
    mine = lse[d]
    lt = jnp.concatenate([mine[m : m + 1, :] for m in range(16)], axis=1)
    ls = jnp.concatenate([mine[16 + m : 17 + m, :] for m in range(16)], axis=1)

    def finish(by_row_sum, by_col_sum, feat, l):
        shift, k = row_shift(self_scores(feat))
        by_row = jnp.exp(shift * LN2 - l)
        by_col = jnp.exp((shift * LN2 - SHIFT) * 0.5)
        exact = y * jnp.exp(SHIFT - l)
        missing = (exact - exact.astype(BF16).astype(F32)) * jnp.exp2(k)
        return by_row_sum * by_row + (by_col_sum + missing) * by_col * by_col, by_row

    gs, _ = finish(os_[0:W, :], os_[W:, :], own[W:, :], ls)
    gt, by_row = finish(ot[2 * W :, :], ot[W : 2 * W, :], own[0:W, :], lt)
    grad[...] = jnp.where(live, (gs - gt) * 0.125, 0.0)
    moved = jnp.sum(x * ot[0:W, :] - y * ot[2 * W :, :], axis=0, keepdims=True)
    rows = jnp.where(live, moved * by_row * 0.125 - lt + ls, 0.0)
    acc = rows[:, 0:128]
    for m in range(1, 16):
        acc = acc + rows[:, m * 128 : (m + 1) * 128]
    at = lax.broadcasted_iota(jnp.int32, (8, 128), 0)
    kl[...] = jnp.where(at == 0, acc, jnp.where(at == 1, n.astype(F32), 0.0))


def grads(feats, lse):
    vmem = pl.BlockSpec(memory_space=VMEM)
    return pl.pallas_call(
        grads_kernel,
        out_shape=(jax.ShapeDtypeStruct((W, OWN), F32), jax.ShapeDtypeStruct((8, 128), F32)),
        in_specs=[vmem, vmem],
        out_specs=(vmem, vmem),
        scratch_shapes=[
            VMEM((128, OWN), BF16),
            VMEM((128, OWN), BF16),
            VMEM((128, OWN), BF16),
            VMEM((8, OWN), F32),
            VMEM((4 * W, LEN), BF16),
            VMEM((3 * W, OWN), F32),
            VMEM((2 * W, OWN), F32),
        ],
        compiler_params=params(),
    )(feats, lse)


def grads_wide(feats, lse):
    doc, _, _, z, _ = coords()
    d = doc * 4 + z
    n = lse[0, 33, 0].astype(jnp.int32)
    f = feats[:, :, :, :ROWS, :].reshape(LEN // 1024, 8, 128, 128)
    mine = lax.dynamic_index_in_dim(f, d, 1, keepdims=False).reshape(OWN, 128)
    cols = f.reshape(LEN // 1024, 1024, 128)
    col_lse = jnp.transpose(lse[:, :32].reshape(8, 2, 16, 128), (2, 1, 0, 3)).reshape(16, 2, 1024)
    own_lse = lax.dynamic_index_in_dim(lse, d, 0, keepdims=False)[:32].reshape(2, OWN)
    lt, ls = own_lse[0][:, None], own_lse[1][:, None]
    lane = jnp.arange(OWN)
    live = (((lane // 128) * 8 + d) * 128 + lane % 128 < n)[:, None]

    def step(j, carry):
        grad, kl = carry
        c = lax.dynamic_index_in_dim(cols, j, 0, keepdims=False)
        cl = lax.dynamic_index_in_dim(col_lse, j, 0, keepdims=False)
        both = live & (j * 1024 + jnp.arange(1024) < n)[None, :]
        t = jnp.dot(mine[:, :W], c[:, :W].T, preferred_element_type=F32) * 0.125
        s = jnp.dot(mine[:, W:], c[:, W:].T, preferred_element_type=F32) * 0.125
        pt = jnp.where(both, jnp.exp(t - lt), 0.0)
        rows = jnp.where(both, jnp.exp(s - ls), 0.0) - pt
        columns = jnp.where(both, jnp.exp(s - cl[1:2]) - jnp.exp(t - cl[0:1]), 0.0)
        w = (rows + columns).astype(BF16)
        grad = grad + jnp.dot(w, c[:, W:], preferred_element_type=F32) * 0.125
        return grad, kl + jnp.sum(pt * (t - s), axis=1, keepdims=True)

    zero = (jnp.zeros((OWN, W), F32), jnp.zeros((OWN, 1), F32))
    grad, kl = lax.fori_loop(0, 16, step, zero)
    rows = jnp.where(live, kl - lt + ls, 0.0).reshape(16, 128)
    tile = jnp.concatenate(
        [jnp.sum(rows, axis=0, keepdims=True), jnp.full((1, 128), n.astype(F32)), jnp.zeros((6, 128), F32)]
    )
    return grad.T, tile


def give_kernel(grad, kl, got, loss, got_kl, sums, got_sum, sg, rg, sk, rk, ss, rs):
    doc, head, x, z, yh = coords()
    me = device(doc, head, x, z, yh)
    to = [device(x // 2, head, m // 4, m % 4, doc) for m in range(16)]
    sources = [device(yh, head, 2 * doc + k, q, e) for k in range(2) for e in range(2) for q in range(4)]
    ring = [device(doc, 1 - head, x, z, yh), device(doc, head, x, z, 1 - yh), device(doc, 1 - head, x, z, 1 - yh)]
    greet(to + sources + ring, me)
    kind, part, q = x % 2, yh, z
    slot = (kind * 2 + part) * 4 + q
    where = pl.ds(pl.multiple_of(part * W, W), W)
    for m in range(16):
        mine = same(to[m], me)
        src = grad.at[:, m * 128 : (m + 1) * 128]

        @pl.when(mine)
        def _():
            pltpu.make_async_copy(src, got.at[kind, q, where], rg.at[slot]).start()
            pltpu.make_async_copy(kl, got_kl.at[slot], rk.at[slot]).start()

        @pl.when(jnp.logical_not(mine))
        def _():
            pltpu.make_async_remote_copy(
                src, got.at[kind, q, where], sg.at[m], rg.at[slot], device_id=to[m], device_id_type=MESH
            ).start()
            pltpu.make_async_remote_copy(
                kl, got_kl.at[slot], sk.at[m], rk.at[slot], device_id=to[m], device_id_type=MESH
            ).start()

    total = jnp.zeros((8, 128), F32)
    for i in range(16):
        pltpu.make_async_copy(kl, got_kl.at[i], rk.at[i]).wait()
        total = total + got_kl[i]
    sums[...] = total
    swaps = []
    for i in range(3):
        copy = pltpu.make_async_remote_copy(
            sums, got_sum.at[i], ss.at[i], rs.at[i], device_id=ring[i], device_id_type=MESH
        )
        copy.start()
        swaps.append(copy)
    for i in range(3):
        swaps[i].wait_recv()
        total = total + got_sum[i]
    for i in range(3):
        swaps[i].wait_send()
    kl_sum = jnp.sum(total[0:1, :], axis=1, keepdims=True)
    count = total[1:2, 0:1] * (1.0 / 64.0)
    loss[...] = jnp.broadcast_to(kl_sum / (count * (2.0 * REL_HEADS)), (8, 128))
    for k in range(2):
        for q_ in range(4):
            for e in range(2):
                part_ref = got.at[k, q_, pl.ds(e * W, W)]
                pltpu.make_async_copy(part_ref, part_ref, rg.at[(k * 2 + e) * 4 + q_]).wait()
    for m in range(16):
        src = grad.at[:, m * 128 : (m + 1) * 128]

        @pl.when(jnp.logical_not(same(to[m], me)))
        def _():
            pltpu.make_async_remote_copy(
                src, got.at[kind, q, where], sg.at[m], rg.at[slot], device_id=to[m], device_id_type=MESH
            ).wait_send()
            pltpu.make_async_remote_copy(
                kl, got_kl.at[slot], sk.at[m], rk.at[slot], device_id=to[m], device_id_type=MESH
            ).wait_send()


def give(grad, kl):
    dma = pltpu.SemaphoreType.DMA
    vmem = pl.BlockSpec(memory_space=VMEM)
    return pl.pallas_call(
        give_kernel,
        out_shape=(jax.ShapeDtypeStruct((2, 4, 128, 128), F32), jax.ShapeDtypeStruct((8, 128), F32)),
        in_specs=[vmem, vmem],
        out_specs=(vmem, vmem),
        scratch_shapes=[
            VMEM((16, 8, 128), F32),
            VMEM((8, 128), F32),
            VMEM((3, 8, 128), F32),
            dma((16,)), dma((16,)), dma((16,)), dma((16,)), dma((3,)), dma((3,)),
        ],
        compiler_params=params(collective_id=2, has_side_effects=True),
    )(grad, kl)


def turn_kernel(got, tile, gq, gv, loss):
    for k, out in ((0, gq), (1, gv)):
        for q in range(4):
            out[0, q * 128 : (q + 1) * 128, :] = got[k, q].T
    loss[0] = jnp.max(tile[...])


def turn(got, tile):
    vmem = pl.BlockSpec(memory_space=VMEM)
    out = jax.ShapeDtypeStruct((1, ROWS, 128), F32)
    return pl.pallas_call(
        turn_kernel,
        out_shape=(out, out, jax.ShapeDtypeStruct((1,), F32)),
        in_specs=[vmem, vmem],
        out_specs=(vmem, vmem, pl.BlockSpec(memory_space=pltpu.SMEM)),
        compiler_params=params(),
    )(got, tile)


def shards(token_ids, teacher_query, teacher_value, student_query, student_value, teacher_pick, student_pick):
    msg_a, msg_b = pick(
        teacher_pick, student_pick, token_ids.reshape(4, 128),
        teacher_query[0], teacher_value[0], student_query[0], student_value[0],
    )
    feats = gather(teacher_pick, msg_a, msg_b)
    lse = share(sums(feats))
    fast = jnp.max(lse[:, 32, 0]) <= FAST_TOP
    grad, kl = lax.cond(fast, grads, grads_wide, feats, lse)
    return turn(*give(grad, kl))


def solution(mesh):
    return jax.shard_map(
        shards,
        mesh=mesh,
        in_specs=(
            P("doc", "seq"),
            P("doc", "seq", "head"),
            P("doc", "seq", "head"),
            P("doc", "seq", None),
            P("doc", "seq", None),
            P(),
            P(),
        ),
        out_specs=(P("doc", "seq", "head"), P("doc", "seq", "head"), P("doc")),
        check_vma=False,
    )
```

```python
import functools

import jax
import jax.numpy as jnp
from jax import lax
from jax.experimental import pallas as pl
from jax.experimental.pallas import tpu as pltpu
from jax.sharding import PartitionSpec as P

HEAD_DIM = 128
W = 64
PER_HEAD = HEAD_DIM // W
T_GROUP = 8
S_GROUP = 7
REL_HEADS = 4
LEN = 16384
ROWS = 512
PIECE = ROWS + 16
OWN = 2048
TOP_BOUND = 162.0
LN2 = 0.6931471805599453
LOG2E = 1.4426950408889634
SHIFT = 74.0
FAST_TOP = 130.0
STEP = 2048
F32 = jnp.float32
BF16 = jnp.bfloat16
MESH = pl.DeviceIdType.MESH
VMEM = pltpu.VMEM
ANY = pl.ANY


def coords():
    doc = lax.axis_index("doc")
    head = lax.axis_index("head")
    seq = lax.axis_index("seq")
    return doc, head, seq // 8, (seq // 2) % 4, seq % 2


def device(doc, head, x, z, yh):
    return (doc, head, (x * 4 + z) * 2 + yh)


def same(a, b):
    return (a[0] == b[0]) & (a[1] == b[1]) & (a[2] == b[2])


def params(**kw):
    return pltpu.CompilerParams(vmem_limit_bytes=56 * 2**20, **kw)


def pick_kernel(tp, sp, ids, tq, tv, sq, sv, msg_a, msg_b, tw, sw, sem):
    head = lax.axis_index("head")
    copies = []

    def fetch(src, block, dst):
        start = pl.multiple_of((block // 2) * 128, 128)
        copy = pltpu.make_async_copy(src.at[:, pl.ds(start, 128)], dst, sem.at[len(copies)])
        copy.start()
        copies.append(copy)

    q_blocks = tq.shape[1] // W
    v_blocks = tv.shape[1] // W
    for r in range(REL_HEADS):
        b = tp[r]
        vb = (b // PER_HEAD) // T_GROUP * PER_HEAD + b % PER_HEAD
        fetch(tq, b % q_blocks, tw.at[0, r])
        fetch(tv, vb % v_blocks, tw.at[1, r])
    for e in range(2):
        b = sp[head * 2 + e]
        vb = (b // PER_HEAD) // S_GROUP * PER_HEAD + b % PER_HEAD
        fetch(sq, b, sw.at[0, e])
        fetch(sv, vb, sw.at[1, e])
    for copy in copies:
        copy.wait()

    def half(w, b):
        return jnp.where(b % 2 == 0, w[:, :W], w[:, W:])

    live = (ids[...] != 0).astype(F32)
    tail = jnp.concatenate([live, jnp.zeros((12, 128), F32)], axis=0).astype(BF16)
    for k in range(2):
        for e in range(2):
            r = head * 2 + e
            t = half(tw[k, r], tp[r])
            s = half(sw[k, e], sp[r])
            msg_a[k, e, 0:ROWS, :] = jnp.concatenate([t, s], axis=1)
            msg_a[k, e, ROWS:PIECE, :] = tail
            r = (1 - head) * 2 + e
            t = half(tw[k, r], tp[r])
            msg_b[k, e] = jnp.concatenate([t[: ROWS // 2], t[ROWS // 2 :]], axis=1)


def pick(tp, sp, ids, tq, tv, sq, sv):
    smem = pl.BlockSpec(memory_space=pltpu.SMEM)
    vmem = pl.BlockSpec(memory_space=VMEM)
    hbm = pl.BlockSpec(memory_space=ANY)
    return pl.pallas_call(
        pick_kernel,
        out_shape=(
            jax.ShapeDtypeStruct((2, 2, PIECE, 128), BF16),
            jax.ShapeDtypeStruct((2, 2, ROWS // 2, 128), BF16),
        ),
        in_specs=[smem, smem, vmem, hbm, hbm, hbm, hbm],
        out_specs=(vmem, vmem),
        scratch_shapes=[
            VMEM((2, 4, ROWS, 128), BF16),
            VMEM((2, 2, ROWS, 128), BF16),
            pltpu.SemaphoreType.DMA((12,)),
        ],
        compiler_params=params(),
    )(tp, sp, ids, tq, tv, sq, sv)


def greet(peers, me):
    barrier = pltpu.get_barrier_semaphore()
    count = 0
    for peer in peers:
        other = jnp.logical_not(same(peer, me))

        @pl.when(other)
        def _():
            pl.semaphore_signal(barrier, inc=1, device_id=peer, device_id_type=MESH)

        count = count + other.astype(jnp.int32)
    pl.semaphore_wait(barrier, count)


def gather_kernel(
    tp, msg_a, msg_b, out, got_a, got_b, chunk,
    sa, sb, ra, rb, s_own, s_core, s_up, s_dn, r_core, r_up, r_dn,
):
    doc, head, x, z, yh = coords()
    me = device(doc, head, x, z, yh)
    core = device(1 - doc, head, x, z, yh)
    up = device(doc, head, x, (z + 1) % 4, yh)
    down = device(doc, head, x, (z + 3) % 4, yh)
    kinds = [((x == 2 * doc + 1) | (x == (2 * doc + 2) % 4)).astype(jnp.int32)]
    kinds.append(1 - kinds[0])
    to_a = [[device(yh, head, 2 * doc + k, z, e) for e in range(2)] for k in kinds]
    to_b = [[device(yh, 1 - head, 2 * doc + k, z, e) for e in range(2)] for k in kinds]
    from_doc = x // 2
    sources = [device(from_doc, h, xs, z, doc) for h in range(2) for xs in range(4)]
    greet(to_a[0] + to_a[1] + to_b[0] + to_b[1] + sources + [core, up, down], me)

    for i, k in enumerate(kinds):
        for e in range(2):
            mine = same(to_a[i][e], me)

            @pl.when(mine)
            def _():
                pltpu.make_async_copy(msg_a.at[k, e], got_a.at[x], ra.at[x]).start()

            @pl.when(jnp.logical_not(mine))
            def _():
                pltpu.make_async_remote_copy(
                    msg_a.at[k, e], got_a.at[x], sa.at[i, e], ra.at[x],
                    device_id=to_a[i][e], device_id_type=MESH,
                ).start()

            pltpu.make_async_remote_copy(
                msg_b.at[k, e], got_b.at[x], sb.at[i, e], rb.at[x],
                device_id=to_b[i][e], device_id_type=MESH,
            ).start()

    own = tp[head * 2 + yh] // (REL_HEADS * 16) == head

    def remote(src, dst, send, recv, to):
        return pltpu.make_async_remote_copy(
            src, dst, send, recv, device_id=to, device_id_type=MESH
        )

    def place(i, zz, c):
        return out.at[order[i], zz, c]

    sends = []
    lane = lax.broadcasted_iota(jnp.int32, (ROWS // 2, 128), 1)
    order = [x, (x + 1) % 4, (x + 3) % 4, (x + 2) % 4]
    for i, xs in enumerate(order):
        pltpu.make_async_copy(msg_a.at[0, 0], got_a.at[xs], ra.at[xs]).wait()
        pltpu.make_async_copy(msg_b.at[0, 0], got_b.at[xs], rb.at[xs]).wait()
        b = got_b[xs]
        b_roll = jnp.concatenate([b[:, W:], b[:, :W]], axis=1)
        keep = jnp.logical_or(own, lane >= W)
        chunk[i, 0 : ROWS // 2] = jnp.where(keep, got_a[xs, 0 : ROWS // 2], b)
        chunk[i, ROWS // 2 : ROWS] = jnp.where(keep, got_a[xs, ROWS // 2 : ROWS], b_roll)
        chunk[i, ROWS:PIECE] = got_a[xs, ROWS:PIECE]
        for copy in (
            remote(chunk.at[i], place(i, z, doc), s_up.at[i], r_dn.at[i], up),
            remote(chunk.at[i], place(i, z, doc), s_dn.at[i], r_up.at[i], down),
            remote(chunk.at[i], place(i, z, doc), s_core.at[i], r_core.at[i], core),
        ):
            copy.start()
            sends.append(copy)
        local = pltpu.make_async_copy(chunk.at[i], place(i, z, doc), s_own.at[i])
        local.start()
        sends.append(local)

    below, above, across = (z + 3) % 4, (z + 1) % 4, (z + 2) % 4

    def forward(src, send, recv, to):
        copy = remote(src, src, send, recv, to)
        copy.start()
        sends.append(copy)

    def arrived(ref, sem):
        pltpu.make_async_copy(ref, ref, sem).wait()

    for i in range(4):
        lo = place(i, below, doc)
        arrived(lo, r_dn.at[i])
        if i < 2:
            forward(lo, s_up.at[4 + i], r_dn.at[4 + i], up)
        forward(lo, s_core.at[4 + i], r_core.at[4 + i], core)
        hi = place(i, above, doc)
        arrived(hi, r_up.at[i])
        if i >= 2:
            forward(hi, s_dn.at[2 + i], r_up.at[2 + i], down)
        forward(hi, s_core.at[8 + i], r_core.at[8 + i], core)
    for i in range(4):
        far = place(i, across, doc)
        arrived(far, r_dn.at[4 + i] if i < 2 else r_up.at[2 + i])
        forward(far, s_core.at[12 + i], r_core.at[12 + i], core)
    for i in range(4):
        arrived(place(i, z, 1 - doc), r_core.at[i])
        arrived(place(i, below, 1 - doc), r_core.at[4 + i])
        arrived(place(i, above, 1 - doc), r_core.at[8 + i])
        arrived(place(i, across, 1 - doc), r_core.at[12 + i])
    for copy in sends:
        if hasattr(copy, "wait_send") and copy.is_remote:
            copy.wait_send()
        else:
            copy.wait()
    for i, k in enumerate(kinds):
        for e in range(2):

            @pl.when(jnp.logical_not(same(to_a[i][e], me)))
            def _():
                remote(msg_a.at[k, e], got_a.at[x], sa.at[i, e], ra.at[x], to_a[i][e]).wait_send()

            remote(msg_b.at[k, e], got_b.at[x], sb.at[i, e], rb.at[x], to_b[i][e]).wait_send()


def gather(tp, msg_a, msg_b):
    dma = pltpu.SemaphoreType.DMA
    vmem = pl.BlockSpec(memory_space=VMEM)
    return pl.pallas_call(
        gather_kernel,
        out_shape=jax.ShapeDtypeStruct((4, 4, 2, PIECE, 128), BF16),
        in_specs=[pl.BlockSpec(memory_space=pltpu.SMEM), vmem, vmem],
        out_specs=pl.BlockSpec(memory_space=ANY),
        scratch_shapes=[
            VMEM((4, PIECE, 128), BF16),
            VMEM((4, ROWS // 2, 128), BF16),
            VMEM((4, PIECE, 128), BF16),
            dma((2, 2)), dma((2, 2)), dma((4,)), dma((4,)),
            dma((4,)), dma((16,)), dma((6,)), dma((6,)), dma((16,)), dma((6,)), dma((6,)),
        ],
        compiler_params=params(collective_id=0, has_side_effects=True),
    )(tp, msg_a, msg_b)


def live_count(feats):
    total = jnp.zeros((16, 128), F32)
    for i in range(4):
        for zz in range(4):
            for c in range(2):
                total = total + feats[i, zz, c, ROWS:PIECE, :].astype(F32)
    return jnp.sum(total).astype(jnp.int32)


def block(feats, b):
    return feats[b // 8, (b // 2) % 4, b % 2, 0:ROWS, :]


def tile_scores(feats, b, count, rows):
    parts = [jnp.dot(block(feats, b + i), rows, preferred_element_type=F32) for i in range(count)]
    return jnp.concatenate(parts, axis=0)


def own_rows(feats, d, own):
    for m in range(16):
        b = 2 * m + d // 4
        part = feats[b // 8, (b // 2) % 4, b % 2, pl.ds(pl.multiple_of((d % 4) * 128, 128), 128), :]
        own[:, m * 128 : (m + 1) * 128] = part.T


def self_scores(feat):
    f = feat.astype(F32)
    return jnp.sum(f * f, axis=0, keepdims=True) * 0.125


def row_shift(own_score):
    room = 75.0 - (jnp.sqrt(own_score * TOP_BOUND) - own_score)
    k = jnp.floor(jnp.maximum(jnp.minimum(room, own_score), 0.0) * LOG2E)
    return own_score * LOG2E - k, k


def fill_rows(own, xi, yi, shifts):
    zero = jnp.zeros((W, OWN), BF16)
    xi[0:W, :] = own[0:W, :] * jnp.asarray(0.125, BF16)
    xi[W:, :] = zero
    yi[0:W, :] = zero
    yi[W:, :] = own[W:, :] * jnp.asarray(0.125, BF16)
    shifts[0:1, :] = row_shift(self_scores(own[0:W, :]))[0]
    shifts[1:2, :] = row_shift(self_scores(own[W:, :]))[0]


def own_live(n, d):
    lane = lax.broadcasted_iota(jnp.int32, (1, OWN), 1)
    token = ((lane // 128) * 8 + d) * 128 + lane % 128
    return token < n


def row_tiles(n, d, tile):
    blocks = jnp.clip((n - d * 128 + 1023) // 1024, 0, 16)
    need = jnp.maximum((blocks + 1) // 2, 4)
    for width in range(4, 9):

        @pl.when(need == width)
        def _():
            def half(i, _):
                tile(pl.multiple_of(i * width * 128, 128), width * 128)
                return 0

            lax.fori_loop(0, 2, half, 0)


def sums_kernel(feats, out, own, xi, yi, shifts, acc_t, acc_s):
    doc, _, _, z, _ = coords()
    d = doc * 4 + z
    n = live_count(feats)
    own_rows(feats, d, own)
    fill_rows(own, xi, yi, shifts)
    acc_t[...] = jnp.ones_like(acc_t)
    acc_s[...] = jnp.ones_like(acc_s)
    steps = n // STEP
    rest = n - steps * STEP

    def tile(start, width):
        at = pl.ds(start, width)

        def step(j, carry, size=STEP, mask=False):
            b = j * (STEP // ROWS)
            t = jnp.exp2(tile_scores(feats, b, size // ROWS, xi[:, at]) * LOG2E - shifts[0:1, at])
            s = jnp.exp2(tile_scores(feats, b, size // ROWS, yi[:, at]) * LOG2E - shifts[1:2, at])
            if mask:
                alive = lax.broadcasted_iota(jnp.int32, (size, width), 0) < rest
                t = jnp.where(alive, t, 0.0)
                s = jnp.where(alive, s, 0.0)
            add_t = jnp.sum(t.reshape(size // 8, 8, width), axis=0)
            add_s = jnp.sum(s.reshape(size // 8, 8, width), axis=0)
            return carry[0] + add_t, carry[1] + add_s

        zero = jnp.zeros((8, width), F32)
        t, s = lax.fori_loop(0, steps, step, (zero, zero))
        acc_t[:, at] = t
        acc_s[:, at] = s

        def last(size):
            t, s = step(steps, (acc_t[:, at], acc_s[:, at]), size, True)
            acc_t[:, at] = t
            acc_s[:, at] = s

        @pl.when(rest > STEP // 2)
        def _():
            last(STEP)

        @pl.when((rest > 0) & (rest <= STEP // 2))
        def _():
            last(STEP // 2)

    row_tiles(n, d, tile)
    live = own_live(n, d)
    st = self_scores(own[0:W, :])
    ss = self_scores(own[W:, :])
    lt = shifts[0:1, :] * LN2 + jnp.log(jnp.sum(acc_t[...], axis=0, keepdims=True))
    ls = shifts[1:2, :] * LN2 + jnp.log(jnp.sum(acc_s[...], axis=0, keepdims=True))
    top = jnp.max(jnp.where(live, jnp.maximum(st, ss), 0.0))
    lt = jnp.where(live, lt, 0.0)
    ls = jnp.where(live, ls, 0.0)
    for m in range(16):
        out[m : m + 1, :] = lt[:, m * 128 : (m + 1) * 128]
        out[16 + m : 17 + m, :] = ls[:, m * 128 : (m + 1) * 128]
    at = lax.broadcasted_iota(jnp.int32, (8, 128), 0)
    out[32:40, :] = jnp.where(at == 0, top, jnp.where(at == 1, n.astype(F32), 0.0))


def sums(feats):
    return pl.pallas_call(
        sums_kernel,
        out_shape=jax.ShapeDtypeStruct((40, 128), F32),
        in_specs=[pl.BlockSpec(memory_space=VMEM)],
        out_specs=pl.BlockSpec(memory_space=VMEM),
        scratch_shapes=[
            VMEM((128, OWN), BF16),
            VMEM((128, OWN), BF16),
            VMEM((128, OWN), BF16),
            VMEM((8, OWN), F32),
            VMEM((8, OWN), F32),
            VMEM((8, OWN), F32),
        ],
        compiler_params=params(),
    )(feats)


def share_kernel(mine, out, flag, s_own, send, recv):
    doc, head, x, z, yh = coords()
    me = device(doc, head, x, z, yh)
    d = doc * 4 + z
    peers = []
    for step in range(1, 8):
        p = (d + step) % 8
        peers.append(device(p // 4, head, x, p % 4, yh))
    greet(peers, me)
    copies = []
    for step in range(1, 8):
        copy = pltpu.make_async_remote_copy(
            mine, out.at[d], send.at[step - 1], recv.at[step - 1],
            device_id=peers[step - 1], device_id_type=MESH,
        )
        copy.start()
        copies.append(copy)
    local = pltpu.make_async_copy(mine, out.at[d], s_own)
    local.start()
    for step in range(1, 8):
        p = (d + 8 - step) % 8
        pltpu.make_async_copy(mine, out.at[p], recv.at[step - 1]).wait()
    local.wait()
    flag[0] = (jnp.max(out[:, 32:33, :]) <= FAST_TOP).astype(jnp.int32)
    for copy in copies:
        copy.wait_send()


def share(mine):
    dma = pltpu.SemaphoreType.DMA
    vmem = pl.BlockSpec(memory_space=VMEM)
    return pl.pallas_call(
        share_kernel,
        out_shape=(jax.ShapeDtypeStruct((8, 40, 128), F32), jax.ShapeDtypeStruct((1,), jnp.int32)),
        in_specs=[vmem],
        out_specs=(vmem, pl.BlockSpec(memory_space=pltpu.SMEM)),
        scratch_shapes=[dma, dma((7,)), dma((7,))],
        compiler_params=params(collective_id=1, has_side_effects=True),
    )(mine)


def grads_kernel(feats, lse, grad, kl, own, xi, yi, shifts, v, ot, os_):
    doc, _, _, z, _ = coords()
    d = doc * 4 + z
    n = jnp.max(lse[0, 33:34, :]).astype(jnp.int32)
    own_rows(feats, d, own)
    fill_rows(own, xi, yi, shifts)
    rest = n % STEP
    steps = n // STEP + (rest > STEP // 2).astype(jnp.int32)
    more = (rest > 0) & (rest <= STEP // 2)

    def weigh(b, _):
        f = block(feats, b).T
        x, y = f[:W, :], f[W:, :]
        yf = y.astype(F32)
        at = pl.ds(pl.multiple_of(b * ROWS, ROWS), ROWS)
        lt, ls = [], []
        for q in range(4):
            m = (b * 4 + q) // 8
            dd = (b * 4 + q) % 8
            lt.append(lse[dd, pl.ds(m, 1), :])
            ls.append(lse[dd, pl.ds(16 + m, 1), :])
        live = lax.broadcasted_iota(jnp.int32, (1, ROWS), 1) + b * ROWS < n
        wt = jnp.where(live, jnp.exp(SHIFT - jnp.concatenate(lt, axis=1)), 0.0)
        ws = jnp.where(live, jnp.exp(SHIFT - jnp.concatenate(ls, axis=1)), 0.0)
        keep = jnp.where(live, 1.0, 0.0).astype(BF16)
        v[0:W, at] = x * keep
        v[W : 2 * W, at] = (yf * wt).astype(BF16)
        v[2 * W : 3 * W, at] = y * keep
        v[3 * W :, at] = (yf * ws).astype(BF16)
        return 0

    lax.fori_loop(0, steps * (STEP // ROWS) + jnp.where(more, STEP // ROWS // 2, 0), weigh, 0)
    ot[...] = jnp.zeros_like(ot)
    os_[...] = jnp.zeros_like(os_)

    def tile(start, width):
        at = pl.ds(start, width)

        def step(j, _, size=STEP):
            js = pl.ds(pl.multiple_of(j * STEP, STEP), size)
            b = j * (STEP // ROWS)
            t = jnp.exp2(tile_scores(feats, b, size // ROWS, xi[:, at]) * LOG2E - shifts[0:1, at]).astype(BF16)
            s = jnp.exp2(tile_scores(feats, b, size // ROWS, yi[:, at]) * LOG2E - shifts[1:2, at]).astype(BF16)
            ot[:, at] += jnp.dot(v[0 : 3 * W, js], t, preferred_element_type=F32)
            os_[:, at] += jnp.dot(v[2 * W :, js], s, preferred_element_type=F32)
            return 0

        lax.fori_loop(0, steps, step, 0)

        @pl.when(more)
        def _():
            step(steps, 0, STEP // 2)

    row_tiles(n, d, tile)
    live = own_live(n, d)
    x = own[0:W, :].astype(F32)
    y = own[W:, :].astype(F32)
    mine = lse[d]
    lt = jnp.concatenate([mine[m : m + 1, :] for m in range(16)], axis=1)
    ls = jnp.concatenate([mine[16 + m : 17 + m, :] for m in range(16)], axis=1)

    def finish(by_row_sum, by_col_sum, feat, l):
        shift, k = row_shift(self_scores(feat))
        by_row = jnp.exp(shift * LN2 - l)
        by_col = jnp.exp((shift * LN2 - SHIFT) * 0.5)
        exact = y * jnp.exp(SHIFT - l)
        missing = (exact - exact.astype(BF16).astype(F32)) * jnp.exp2(k)
        return by_row_sum * by_row + (by_col_sum + missing) * by_col * by_col, by_row

    gs, _ = finish(os_[0:W, :], os_[W:, :], own[W:, :], ls)
    gt, by_row = finish(ot[2 * W :, :], ot[W : 2 * W, :], own[0:W, :], lt)
    grad[...] = jnp.where(live, (gs - gt) * 0.125, 0.0)
    moved = jnp.sum(x * ot[0:W, :] - y * ot[2 * W :, :], axis=0, keepdims=True)
    rows = jnp.where(live, moved * by_row * 0.125 - lt + ls, 0.0)
    acc = rows[:, 0:128]
    for m in range(1, 16):
        acc = acc + rows[:, m * 128 : (m + 1) * 128]
    at = lax.broadcasted_iota(jnp.int32, (8, 128), 0)
    kl[...] = jnp.where(at == 0, acc, jnp.where(at == 1, n.astype(F32), 0.0))


def grads(feats, lse):
    vmem = pl.BlockSpec(memory_space=VMEM)
    return pl.pallas_call(
        grads_kernel,
        out_shape=(jax.ShapeDtypeStruct((W, OWN), F32), jax.ShapeDtypeStruct((8, 128), F32)),
        in_specs=[vmem, vmem],
        out_specs=(vmem, vmem),
        scratch_shapes=[
            VMEM((128, OWN), BF16),
            VMEM((128, OWN), BF16),
            VMEM((128, OWN), BF16),
            VMEM((8, OWN), F32),
            VMEM((4 * W, LEN), BF16),
            VMEM((3 * W, OWN), F32),
            VMEM((2 * W, OWN), F32),
        ],
        compiler_params=params(),
    )(feats, lse)


def grads_wide(feats, lse):
    doc, _, _, z, _ = coords()
    d = doc * 4 + z
    n = lse[0, 33, 0].astype(jnp.int32)
    f = feats[:, :, :, :ROWS, :].reshape(LEN // 1024, 8, 128, 128)
    mine = lax.dynamic_index_in_dim(f, d, 1, keepdims=False).reshape(OWN, 128)
    cols = f.reshape(LEN // 1024, 1024, 128)
    col_lse = jnp.transpose(lse[:, :32].reshape(8, 2, 16, 128), (2, 1, 0, 3)).reshape(16, 2, 1024)
    own_lse = lax.dynamic_index_in_dim(lse, d, 0, keepdims=False)[:32].reshape(2, OWN)
    lt, ls = own_lse[0][:, None], own_lse[1][:, None]
    lane = jnp.arange(OWN)
    live = (((lane // 128) * 8 + d) * 128 + lane % 128 < n)[:, None]

    def step(j, carry):
        grad, kl = carry
        c = lax.dynamic_index_in_dim(cols, j, 0, keepdims=False)
        cl = lax.dynamic_index_in_dim(col_lse, j, 0, keepdims=False)
        both = live & (j * 1024 + jnp.arange(1024) < n)[None, :]
        t = jnp.dot(mine[:, :W], c[:, :W].T, preferred_element_type=F32) * 0.125
        s = jnp.dot(mine[:, W:], c[:, W:].T, preferred_element_type=F32) * 0.125
        pt = jnp.where(both, jnp.exp(t - lt), 0.0)
        rows = jnp.where(both, jnp.exp(s - ls), 0.0) - pt
        columns = jnp.where(both, jnp.exp(s - cl[1:2]) - jnp.exp(t - cl[0:1]), 0.0)
        w = (rows + columns).astype(BF16)
        grad = grad + jnp.dot(w, c[:, W:], preferred_element_type=F32) * 0.125
        return grad, kl + jnp.sum(pt * (t - s), axis=1, keepdims=True)

    zero = (jnp.zeros((OWN, W), F32), jnp.zeros((OWN, 1), F32))
    grad, kl = lax.fori_loop(0, 16, step, zero)
    rows = jnp.where(live, kl - lt + ls, 0.0).reshape(16, 128)
    tile = jnp.concatenate(
        [jnp.sum(rows, axis=0, keepdims=True), jnp.full((1, 128), n.astype(F32)), jnp.zeros((6, 128), F32)]
    )
    return grad.T, tile


def give_kernel(grad, kl, got, loss, got_kl, sums, got_sum, sg, rg, sk, rk, ss, rs):
    doc, head, x, z, yh = coords()
    me = device(doc, head, x, z, yh)
    to = [device(x // 2, head, m // 4, m % 4, doc) for m in range(16)]
    sources = [device(yh, head, 2 * doc + k, q, e) for k in range(2) for e in range(2) for q in range(4)]
    ring = [device(doc, 1 - head, x, z, yh), device(doc, head, x, z, 1 - yh), device(doc, 1 - head, x, z, 1 - yh)]
    greet(to + sources + ring, me)
    kind, part, q = x % 2, yh, z
    slot = (kind * 2 + part) * 4 + q
    where = pl.ds(pl.multiple_of(part * W, W), W)
    for m in range(16):
        mine = same(to[m], me)
        src = grad.at[:, m * 128 : (m + 1) * 128]

        @pl.when(mine)
        def _():
            pltpu.make_async_copy(src, got.at[kind, q, where], rg.at[slot]).start()
            pltpu.make_async_copy(kl, got_kl.at[slot], rk.at[slot]).start()

        @pl.when(jnp.logical_not(mine))
        def _():
            pltpu.make_async_remote_copy(
                src, got.at[kind, q, where], sg.at[m], rg.at[slot], device_id=to[m], device_id_type=MESH
            ).start()
            pltpu.make_async_remote_copy(
                kl, got_kl.at[slot], sk.at[m], rk.at[slot], device_id=to[m], device_id_type=MESH
            ).start()

    total = jnp.zeros((8, 128), F32)
    for i in range(16):
        pltpu.make_async_copy(kl, got_kl.at[i], rk.at[i]).wait()
        total = total + got_kl[i]
    sums[...] = total
    swaps = []
    for i in range(3):
        copy = pltpu.make_async_remote_copy(
            sums, got_sum.at[i], ss.at[i], rs.at[i], device_id=ring[i], device_id_type=MESH
        )
        copy.start()
        swaps.append(copy)
    for i in range(3):
        swaps[i].wait_recv()
        total = total + got_sum[i]
    for i in range(3):
        swaps[i].wait_send()
    kl_sum = jnp.sum(total[0:1, :], axis=1, keepdims=True)
    count = total[1:2, 0:1] * (1.0 / 64.0)
    loss[...] = jnp.broadcast_to(kl_sum / (count * (2.0 * REL_HEADS)), (8, 128))
    for k in range(2):
        for q_ in range(4):
            for e in range(2):
                part_ref = got.at[k, q_, pl.ds(e * W, W)]
                pltpu.make_async_copy(part_ref, part_ref, rg.at[(k * 2 + e) * 4 + q_]).wait()
    for m in range(16):
        src = grad.at[:, m * 128 : (m + 1) * 128]

        @pl.when(jnp.logical_not(same(to[m], me)))
        def _():
            pltpu.make_async_remote_copy(
                src, got.at[kind, q, where], sg.at[m], rg.at[slot], device_id=to[m], device_id_type=MESH
            ).wait_send()
            pltpu.make_async_remote_copy(
                kl, got_kl.at[slot], sk.at[m], rk.at[slot], device_id=to[m], device_id_type=MESH
            ).wait_send()


def give(grad, kl):
    dma = pltpu.SemaphoreType.DMA
    vmem = pl.BlockSpec(memory_space=VMEM)
    return pl.pallas_call(
        give_kernel,
        out_shape=(jax.ShapeDtypeStruct((2, 4, 128, 128), F32), jax.ShapeDtypeStruct((8, 128), F32)),
        in_specs=[vmem, vmem],
        out_specs=(vmem, vmem),
        scratch_shapes=[
            VMEM((16, 8, 128), F32),
            VMEM((8, 128), F32),
            VMEM((3, 8, 128), F32),
            dma((16,)), dma((16,)), dma((16,)), dma((16,)), dma((3,)), dma((3,)),
        ],
        compiler_params=params(collective_id=2, has_side_effects=True),
    )(grad, kl)


def turn_kernel(got, tile, gq, gv, loss):
    for k, out in ((0, gq), (1, gv)):
        for q in range(4):
            out[0, q * 128 : (q + 1) * 128, :] = got[k, q].T
    loss[0] = jnp.max(tile[...])


def turn(got, tile):
    vmem = pl.BlockSpec(memory_space=VMEM)
    out = jax.ShapeDtypeStruct((1, ROWS, 128), F32)
    return pl.pallas_call(
        turn_kernel,
        out_shape=(out, out, jax.ShapeDtypeStruct((1,), F32)),
        in_specs=[vmem, vmem],
        out_specs=(vmem, vmem, pl.BlockSpec(memory_space=pltpu.SMEM)),
        compiler_params=params(),
    )(got, tile)


def shards(token_ids, teacher_query, teacher_value, student_query, student_value, teacher_pick, student_pick):
    msg_a, msg_b = pick(
        teacher_pick, student_pick, token_ids.reshape(4, 128),
        teacher_query[0], teacher_value[0], student_query[0], student_value[0],
    )
    feats = gather(teacher_pick, msg_a, msg_b)
    lse, fast = share(sums(feats))
    grad, kl = lax.cond(fast[0] > 0, grads, grads_wide, feats, lse)
    return turn(*give(grad, kl))


def solution(mesh):
    return jax.shard_map(
        shards,
        mesh=mesh,
        in_specs=(
            P("doc", "seq"),
            P("doc", "seq", "head"),
            P("doc", "seq", "head"),
            P("doc", "seq", None),
            P("doc", "seq", None),
            P(),
            P(),
        ),
        out_specs=(P("doc", "seq", "head"), P("doc", "seq", "head"), P("doc")),
        check_vma=False,
    )
```

```python
import functools

import jax
import jax.numpy as jnp
from jax import lax
from jax.experimental import pallas as pl
from jax.experimental.pallas import tpu as pltpu
from jax.sharding import PartitionSpec as P

HEAD_DIM = 128
W = 64
PER_HEAD = HEAD_DIM // W
T_GROUP = 8
S_GROUP = 7
REL_HEADS = 4
LEN = 16384
ROWS = 512
PIECE = ROWS + 16
OWN = 2048
TOP_BOUND = 162.0
LN2 = 0.6931471805599453
LOG2E = 1.4426950408889634
SHIFT = 74.0
FAST_TOP = 130.0
STEP = 2048
F32 = jnp.float32
BF16 = jnp.bfloat16
MESH = pl.DeviceIdType.MESH
VMEM = pltpu.VMEM
ANY = pl.ANY


def coords():
    doc = lax.axis_index("doc")
    head = lax.axis_index("head")
    seq = lax.axis_index("seq")
    return doc, head, seq // 8, (seq // 2) % 4, seq % 2


def device(doc, head, x, z, yh):
    return (doc, head, (x * 4 + z) * 2 + yh)


def same(a, b):
    return (a[0] == b[0]) & (a[1] == b[1]) & (a[2] == b[2])


def params(**kw):
    return pltpu.CompilerParams(vmem_limit_bytes=56 * 2**20, **kw)


def pick_kernel(tp, sp, ids, tq, tv, sq, sv, msg_a, msg_b, tw, sw, sem):
    head = lax.axis_index("head")
    copies = []

    def fetch(src, block, dst):
        start = pl.multiple_of((block // 2) * 128, 128)
        copy = pltpu.make_async_copy(src.at[:, pl.ds(start, 128)], dst, sem.at[len(copies)])
        copy.start()
        copies.append(copy)

    q_blocks = tq.shape[1] // W
    v_blocks = tv.shape[1] // W
    for r in range(REL_HEADS):
        b = tp[r]
        vb = (b // PER_HEAD) // T_GROUP * PER_HEAD + b % PER_HEAD
        fetch(tq, b % q_blocks, tw.at[0, r])
        fetch(tv, vb % v_blocks, tw.at[1, r])
    for e in range(2):
        b = sp[head * 2 + e]
        vb = (b // PER_HEAD) // S_GROUP * PER_HEAD + b % PER_HEAD
        fetch(sq, b, sw.at[0, e])
        fetch(sv, vb, sw.at[1, e])
    for copy in copies:
        copy.wait()

    def half(w, b):
        return jnp.where(b % 2 == 0, w[:, :W], w[:, W:])

    live = (ids[...] != 0).astype(F32)
    tail = jnp.concatenate([live, jnp.zeros((12, 128), F32)], axis=0).astype(BF16)
    for k in range(2):
        for e in range(2):
            r = head * 2 + e
            t = half(tw[k, r], tp[r])
            s = half(sw[k, e], sp[r])
            msg_a[k, e, 0:ROWS, :] = jnp.concatenate([t, s], axis=1)
            msg_a[k, e, ROWS:PIECE, :] = tail
            r = (1 - head) * 2 + e
            t = half(tw[k, r], tp[r])
            msg_b[k, e] = jnp.concatenate([t[: ROWS // 2], t[ROWS // 2 :]], axis=1)


def pick(tp, sp, ids, tq, tv, sq, sv):
    smem = pl.BlockSpec(memory_space=pltpu.SMEM)
    vmem = pl.BlockSpec(memory_space=VMEM)
    hbm = pl.BlockSpec(memory_space=ANY)
    return pl.pallas_call(
        pick_kernel,
        out_shape=(
            jax.ShapeDtypeStruct((2, 2, PIECE, 128), BF16),
            jax.ShapeDtypeStruct((2, 2, ROWS // 2, 128), BF16),
        ),
        in_specs=[smem, smem, vmem, hbm, hbm, hbm, hbm],
        out_specs=(vmem, vmem),
        scratch_shapes=[
            VMEM((2, 4, ROWS, 128), BF16),
            VMEM((2, 2, ROWS, 128), BF16),
            pltpu.SemaphoreType.DMA((12,)),
        ],
        compiler_params=params(),
    )(tp, sp, ids, tq, tv, sq, sv)


def live_count(feats):
    total = jnp.zeros((16, 128), F32)
    for i in range(4):
        for zz in range(4):
            for c in range(2):
                total = total + feats[i, zz, c, ROWS:PIECE, :].astype(F32)
    return jnp.sum(total).astype(jnp.int32)


def block(feats, b):
    return feats[b // 8, (b // 2) % 4, b % 2, 0:ROWS, :]


def tile_scores(feats, b, count, rows):
    parts = [jnp.dot(block(feats, b + i), rows, preferred_element_type=F32) for i in range(count)]
    return jnp.concatenate(parts, axis=0)


def own_rows(feats, d, own):
    for m in range(own.shape[1] // 128):
        b = 2 * m + d // 4
        part = feats[b // 8, (b // 2) % 4, b % 2, pl.ds(pl.multiple_of((d % 4) * 128, 128), 128), :]
        own[:, m * 128 : (m + 1) * 128] = part.T


def self_scores(feat):
    f = feat.astype(F32)
    return jnp.sum(f * f, axis=0, keepdims=True) * 0.125


def row_shift(own_score):
    room = 75.0 - (jnp.sqrt(own_score * TOP_BOUND) - own_score)
    k = jnp.floor(jnp.maximum(jnp.minimum(room, own_score), 0.0) * LOG2E)
    return own_score * LOG2E - k, k


def fill_rows(own, xi, yi, shifts):
    zero = jnp.zeros((W, own.shape[1]), BF16)
    xi[0:W, :] = own[0:W, :] * jnp.asarray(0.125, BF16)
    xi[W:, :] = zero
    yi[0:W, :] = zero
    yi[W:, :] = own[W:, :] * jnp.asarray(0.125, BF16)
    shifts[0:1, :] = row_shift(self_scores(own[0:W, :]))[0]
    shifts[1:2, :] = row_shift(self_scores(own[W:, :]))[0]


def own_live(n, d):
    lane = lax.broadcasted_iota(jnp.int32, (1, OWN), 1)
    token = ((lane // 128) * 8 + d) * 128 + lane % 128
    return token < n


def column_sums(feats, b, count, xi, yi, shift_t, shift_s, carry, alive=None):
    out = []
    for rows, shift, total in ((xi, shift_t, carry[0]), (yi, shift_s, carry[1])):
        e = jnp.exp2(tile_scores(feats, b, count, rows) * LOG2E - shift)
        if alive is not None:
            e = jnp.where(alive, e, 0.0)
        out.append(total + jnp.sum(e.reshape(count * ROWS // 8, 8, e.shape[1]), axis=0))
    return tuple(out)


def row_tiles(n, d, tile):
    blocks = jnp.clip((n - d * 128 + 1023) // 1024, 0, 16)
    need = jnp.maximum((blocks + 1) // 2, 4)
    for width in range(4, 9):

        @pl.when(need == width)
        def _():
            def half(i, _):
                tile(pl.multiple_of(i * width * 128, 128), width * 128)
                return 0

            lax.fori_loop(0, 2, half, 0)


def greet(peers, me):
    barrier = pltpu.get_barrier_semaphore()
    count = 0
    for peer in peers:
        other = jnp.logical_not(same(peer, me))

        @pl.when(other)
        def _():
            pl.semaphore_signal(barrier, inc=1, device_id=peer, device_id_type=MESH)

        count = count + other.astype(jnp.int32)
    pl.semaphore_wait(barrier, count)


def gather_kernel(
    tp, msg_a, msg_b, out, part, got_a, got_b, chunk, rows, xi, yi, shifts,
    sa, sb, ra, rb, s_own, s_core, s_up, s_dn, r_core, r_up, r_dn,
):
    doc, head, x, z, yh = coords()
    me = device(doc, head, x, z, yh)
    core = device(1 - doc, head, x, z, yh)
    up = device(doc, head, x, (z + 1) % 4, yh)
    down = device(doc, head, x, (z + 3) % 4, yh)
    kinds = [((x == 2 * doc + 1) | (x == (2 * doc + 2) % 4)).astype(jnp.int32)]
    kinds.append(1 - kinds[0])
    to_a = [[device(yh, head, 2 * doc + k, z, e) for e in range(2)] for k in kinds]
    to_b = [[device(yh, 1 - head, 2 * doc + k, z, e) for e in range(2)] for k in kinds]
    from_doc = x // 2
    sources = [device(from_doc, h, xs, z, doc) for h in range(2) for xs in range(4)]
    greet(to_a[0] + to_a[1] + to_b[0] + to_b[1] + sources + [core, up, down], me)

    for i, k in enumerate(kinds):
        for e in range(2):
            mine = same(to_a[i][e], me)

            @pl.when(mine)
            def _():
                pltpu.make_async_copy(msg_a.at[k, e], got_a.at[x], ra.at[x]).start()

            @pl.when(jnp.logical_not(mine))
            def _():
                pltpu.make_async_remote_copy(
                    msg_a.at[k, e], got_a.at[x], sa.at[i, e], ra.at[x],
                    device_id=to_a[i][e], device_id_type=MESH,
                ).start()

            pltpu.make_async_remote_copy(
                msg_b.at[k, e], got_b.at[x], sb.at[i, e], rb.at[x],
                device_id=to_b[i][e], device_id_type=MESH,
            ).start()

    own = tp[head * 2 + yh] // (REL_HEADS * 16) == head

    def remote(src, dst, send, recv, to):
        return pltpu.make_async_remote_copy(
            src, dst, send, recv, device_id=to, device_id_type=MESH
        )

    def place(i, zz, c):
        return out.at[order[i], zz, c]

    sends = []
    lane = lax.broadcasted_iota(jnp.int32, (ROWS // 2, 128), 1)
    low = x < 2
    order = [jnp.where(low, x, 3 - x), jnp.where(low, 1 - x, x - 2)]
    order += [jnp.where(low, 3 - x, x), jnp.where(low, 2 + x, 5 - x)]
    for i, xs in enumerate(order):
        pltpu.make_async_copy(msg_a.at[0, 0], got_a.at[xs], ra.at[xs]).wait()
        pltpu.make_async_copy(msg_b.at[0, 0], got_b.at[xs], rb.at[xs]).wait()
        b = got_b[xs]
        b_roll = jnp.concatenate([b[:, W:], b[:, :W]], axis=1)
        keep = jnp.logical_or(own, lane >= W)
        chunk[i, 0 : ROWS // 2] = jnp.where(keep, got_a[xs, 0 : ROWS // 2], b)
        chunk[i, ROWS // 2 : ROWS] = jnp.where(keep, got_a[xs, ROWS // 2 : ROWS], b_roll)
        chunk[i, ROWS:PIECE] = got_a[xs, ROWS:PIECE]
        for copy in (
            remote(chunk.at[i], place(i, z, doc), s_up.at[i], r_dn.at[i], up),
            remote(chunk.at[i], place(i, z, doc), s_dn.at[i], r_up.at[i], down),
            remote(chunk.at[i], place(i, z, doc), s_core.at[i], r_core.at[i], core),
        ):
            copy.start()
            sends.append(copy)
        local = pltpu.make_async_copy(chunk.at[i], place(i, z, doc), s_own.at[i])
        local.start()
        if i >= 2:
            sends.append(local)

    below, above, across = (z + 3) % 4, (z + 1) % 4, (z + 2) % 4

    def forward(src, send, recv, to):
        copy = remote(src, src, send, recv, to)
        copy.start()
        sends.append(copy)

    def arrived(ref, sem):
        pltpu.make_async_copy(ref, ref, sem).wait()

    def pass_on(i):
        lo = place(i, below, doc)
        arrived(lo, r_dn.at[i])
        if i % 2 == 0:
            forward(lo, s_up.at[4 + i // 2], r_dn.at[4 + i // 2], up)
        forward(lo, s_core.at[4 + i], r_core.at[4 + i], core)
        hi = place(i, above, doc)
        arrived(hi, r_up.at[i])
        if i % 2 == 1:
            forward(hi, s_dn.at[4 + i // 2], r_up.at[4 + i // 2], down)
        forward(hi, s_core.at[8 + i], r_core.at[8 + i], core)

    def pass_far(i):
        far = place(i, across, doc)
        arrived(far, r_dn.at[4 + i // 2] if i % 2 == 0 else r_up.at[4 + i // 2])
        forward(far, s_core.at[12 + i], r_core.at[12 + i], core)

    def other_core(i):
        arrived(place(i, z, 1 - doc), r_core.at[i])
        arrived(place(i, below, 1 - doc), r_core.at[4 + i])
        arrived(place(i, above, 1 - doc), r_core.at[8 + i])
        arrived(place(i, across, 1 - doc), r_core.at[12 + i])

    pass_on(0)
    pass_on(1)
    pass_far(0)
    pass_far(1)
    for i in range(2):
        pltpu.make_async_copy(chunk.at[i], place(i, z, doc), s_own.at[i]).wait()

    own_rows(out, doc * 4 + z, rows)
    fill_rows(rows, xi, yi, shifts)

    def add(first, last, core_index, carry):
        def step(i, carry):
            xs, zz = i // 2, (i % 2) * 2
            for half in range(2):
                b = (xs * 4 + zz + half) * 2 + core_index
                carry = column_sums(out, b, 1, xi[...], yi[...], shifts[0:1, :], shifts[1:2, :], carry)
            return carry

        return lax.fori_loop(first, last, step, carry)

    zero = jnp.zeros((8, OWN // 2), F32)
    carry = add(0, 1, doc, (zero, zero))
    pass_on(2)
    carry = add(1, 2, doc, carry)
    pass_on(3)
    carry = add(2, 4, doc, carry)
    pass_far(2)
    pass_far(3)
    other_core(0)
    other_core(1)
    carry = add(0, 4, 1 - doc, carry)
    part[0:8, :] = carry[0]
    part[8:16, :] = carry[1]
    other_core(2)
    other_core(3)
    for copy in sends:
        if hasattr(copy, "wait_send") and copy.is_remote:
            copy.wait_send()
        else:
            copy.wait()
    for i, k in enumerate(kinds):
        for e in range(2):

            @pl.when(jnp.logical_not(same(to_a[i][e], me)))
            def _():
                remote(msg_a.at[k, e], got_a.at[x], sa.at[i, e], ra.at[x], to_a[i][e]).wait_send()

            remote(msg_b.at[k, e], got_b.at[x], sb.at[i, e], rb.at[x], to_b[i][e]).wait_send()


def gather(tp, msg_a, msg_b):
    dma = pltpu.SemaphoreType.DMA
    vmem = pl.BlockSpec(memory_space=VMEM)
    return pl.pallas_call(
        gather_kernel,
        out_shape=(
            jax.ShapeDtypeStruct((4, 4, 2, PIECE, 128), BF16),
            jax.ShapeDtypeStruct((16, OWN // 2), F32),
        ),
        in_specs=[pl.BlockSpec(memory_space=pltpu.SMEM), vmem, vmem],
        out_specs=(vmem, vmem),
        scratch_shapes=[
            VMEM((4, PIECE, 128), BF16),
            VMEM((4, ROWS // 2, 128), BF16),
            VMEM((4, PIECE, 128), BF16),
            VMEM((128, OWN // 2), BF16),
            VMEM((128, OWN // 2), BF16),
            VMEM((128, OWN // 2), BF16),
            VMEM((8, OWN // 2), F32),
            dma((2, 2)), dma((2, 2)), dma((4,)), dma((4,)),
            dma((4,)), dma((16,)), dma((6,)), dma((6,)), dma((16,)), dma((6,)), dma((6,)),
        ],
        compiler_params=params(collective_id=0, has_side_effects=True),
    )(tp, msg_a, msg_b)


def sums_kernel(feats, part, out, own, xi, yi, shifts, acc_t, acc_s):
    doc, _, _, z, _ = coords()
    d = doc * 4 + z
    n = live_count(feats)
    own_rows(feats, d, own)
    fill_rows(own, xi, yi, shifts)
    acc_t[...] = jnp.ones_like(acc_t)
    acc_s[...] = jnp.ones_like(acc_s)
    steps = n // STEP
    rest = n - steps * STEP

    def tile(start, width, first, carry):
        at = pl.ds(start, width)

        def step(j, carry, size=STEP, mask=False):
            alive = lax.broadcasted_iota(jnp.int32, (size, width), 0) < rest if mask else None
            return column_sums(
                feats, j * (STEP // ROWS), size // ROWS, xi[:, at], yi[:, at],
                shifts[0:1, at], shifts[1:2, at], carry, alive,
            )

        t, s = lax.fori_loop(first, steps, step, carry)
        acc_t[:, at] = t
        acc_s[:, at] = s

        def last(size):
            t, s = step(steps, (acc_t[:, at], acc_s[:, at]), size, True)
            acc_t[:, at] = t
            acc_s[:, at] = s

        @pl.when(rest > STEP // 2)
        def _():
            last(STEP)

        @pl.when((rest > 0) & (rest <= STEP // 2))
        def _():
            last(STEP // 2)

    half = OWN // 2
    tile(0, half, LEN // 2 // STEP, (part[0:8, :], part[8:16, :]))
    blocks = jnp.clip((n - d * 128 + 1023) // 1024, 0, 16) - half // 128
    for width in range(1, 5):

        @pl.when((blocks + 1) // 2 == width)
        def _():
            zero = jnp.zeros((8, width * 256), F32)
            tile(half, width * 256, 0, (zero, zero))

    live = own_live(n, d)
    st = self_scores(own[0:W, :])
    ss = self_scores(own[W:, :])
    lt = shifts[0:1, :] * LN2 + jnp.log(jnp.sum(acc_t[...], axis=0, keepdims=True))
    ls = shifts[1:2, :] * LN2 + jnp.log(jnp.sum(acc_s[...], axis=0, keepdims=True))
    top = jnp.max(jnp.where(live, jnp.maximum(st, ss), 0.0))
    lt = jnp.where(live, lt, 0.0)
    ls = jnp.where(live, ls, 0.0)
    for m in range(16):
        out[m : m + 1, :] = lt[:, m * 128 : (m + 1) * 128]
        out[16 + m : 17 + m, :] = ls[:, m * 128 : (m + 1) * 128]
    at = lax.broadcasted_iota(jnp.int32, (8, 128), 0)
    out[32:40, :] = jnp.where(at == 0, top, jnp.where(at == 1, n.astype(F32), 0.0))


def sums(feats, part):
    return pl.pallas_call(
        sums_kernel,
        out_shape=jax.ShapeDtypeStruct((40, 128), F32),
        in_specs=[pl.BlockSpec(memory_space=VMEM)] * 2,
        out_specs=pl.BlockSpec(memory_space=VMEM),
        scratch_shapes=[
            VMEM((128, OWN), BF16),
            VMEM((128, OWN), BF16),
            VMEM((128, OWN), BF16),
            VMEM((8, OWN), F32),
            VMEM((8, OWN), F32),
            VMEM((8, OWN), F32),
        ],
        compiler_params=params(),
    )(feats, part)


def share_kernel(mine, out, flag, s_own, send, recv):
    doc, head, x, z, yh = coords()
    me = device(doc, head, x, z, yh)
    d = doc * 4 + z
    peers = []
    for step in range(1, 8):
        p = (d + step) % 8
        peers.append(device(p // 4, head, x, p % 4, yh))
    greet(peers, me)
    copies = []
    for step in range(1, 8):
        copy = pltpu.make_async_remote_copy(
            mine, out.at[d], send.at[step - 1], recv.at[step - 1],
            device_id=peers[step - 1], device_id_type=MESH,
        )
        copy.start()
        copies.append(copy)
    local = pltpu.make_async_copy(mine, out.at[d], s_own)
    local.start()
    for step in range(1, 8):
        p = (d + 8 - step) % 8
        pltpu.make_async_copy(mine, out.at[p], recv.at[step - 1]).wait()
    local.wait()
    flag[0] = (jnp.max(out[:, 32:33, :]) <= FAST_TOP).astype(jnp.int32)
    for copy in copies:
        copy.wait_send()


def share(mine):
    dma = pltpu.SemaphoreType.DMA
    vmem = pl.BlockSpec(memory_space=VMEM)
    return pl.pallas_call(
        share_kernel,
        out_shape=(jax.ShapeDtypeStruct((8, 40, 128), F32), jax.ShapeDtypeStruct((1,), jnp.int32)),
        in_specs=[vmem],
        out_specs=(vmem, pl.BlockSpec(memory_space=pltpu.SMEM)),
        scratch_shapes=[dma, dma((7,)), dma((7,))],
        compiler_params=params(collective_id=1, has_side_effects=True),
    )(mine)


def grads_kernel(feats, lse, grad, kl, own, xi, yi, shifts, v, ot, os_):
    doc, _, _, z, _ = coords()
    d = doc * 4 + z
    n = jnp.max(lse[0, 33:34, :]).astype(jnp.int32)
    own_rows(feats, d, own)
    fill_rows(own, xi, yi, shifts)
    rest = n % STEP
    steps = n // STEP + (rest > STEP // 2).astype(jnp.int32)
    more = (rest > 0) & (rest <= STEP // 2)

    def weigh(b, _):
        f = block(feats, b).T
        x, y = f[:W, :], f[W:, :]
        yf = y.astype(F32)
        at = pl.ds(pl.multiple_of(b * ROWS, ROWS), ROWS)
        lt, ls = [], []
        for q in range(4):
            m = (b * 4 + q) // 8
            dd = (b * 4 + q) % 8
            lt.append(lse[dd, pl.ds(m, 1), :])
            ls.append(lse[dd, pl.ds(16 + m, 1), :])
        live = lax.broadcasted_iota(jnp.int32, (1, ROWS), 1) + b * ROWS < n
        wt = jnp.where(live, jnp.exp(SHIFT - jnp.concatenate(lt, axis=1)), 0.0)
        ws = jnp.where(live, jnp.exp(SHIFT - jnp.concatenate(ls, axis=1)), 0.0)
        keep = jnp.where(live, 1.0, 0.0).astype(BF16)
        v[0:W, at] = x * keep
        v[W : 2 * W, at] = (yf * wt).astype(BF16)
        v[2 * W : 3 * W, at] = y * keep
        v[3 * W :, at] = (yf * ws).astype(BF16)
        return 0

    lax.fori_loop(0, steps * (STEP // ROWS) + jnp.where(more, STEP // ROWS // 2, 0), weigh, 0)
    ot[...] = jnp.zeros_like(ot)
    os_[...] = jnp.zeros_like(os_)

    def tile(start, width):
        at = pl.ds(start, width)

        def step(j, _, size=STEP):
            js = pl.ds(pl.multiple_of(j * STEP, STEP), size)
            b = j * (STEP // ROWS)
            t = jnp.exp2(tile_scores(feats, b, size // ROWS, xi[:, at]) * LOG2E - shifts[0:1, at]).astype(BF16)
            s = jnp.exp2(tile_scores(feats, b, size // ROWS, yi[:, at]) * LOG2E - shifts[1:2, at]).astype(BF16)
            ot[:, at] += jnp.dot(v[0 : 3 * W, js], t, preferred_element_type=F32)
            os_[:, at] += jnp.dot(v[2 * W :, js], s, preferred_element_type=F32)
            return 0

        lax.fori_loop(0, steps, step, 0)

        @pl.when(more)
        def _():
            step(steps, 0, STEP // 2)

    row_tiles(n, d, tile)
    live = own_live(n, d)
    x = own[0:W, :].astype(F32)
    y = own[W:, :].astype(F32)
    mine = lse[d]
    lt = jnp.concatenate([mine[m : m + 1, :] for m in range(16)], axis=1)
    ls = jnp.concatenate([mine[16 + m : 17 + m, :] for m in range(16)], axis=1)

    def finish(by_row_sum, by_col_sum, feat, l):
        shift, k = row_shift(self_scores(feat))
        by_row = jnp.exp(shift * LN2 - l)
        by_col = jnp.exp((shift * LN2 - SHIFT) * 0.5)
        exact = y * jnp.exp(SHIFT - l)
        missing = (exact - exact.astype(BF16).astype(F32)) * jnp.exp2(k)
        return by_row_sum * by_row + (by_col_sum + missing) * by_col * by_col, by_row

    gs, _ = finish(os_[0:W, :], os_[W:, :], own[W:, :], ls)
    gt, by_row = finish(ot[2 * W :, :], ot[W : 2 * W, :], own[0:W, :], lt)
    grad[...] = jnp.where(live, (gs - gt) * 0.125, 0.0)
    moved = jnp.sum(x * ot[0:W, :] - y * ot[2 * W :, :], axis=0, keepdims=True)
    rows = jnp.where(live, moved * by_row * 0.125 - lt + ls, 0.0)
    acc = rows[:, 0:128]
    for m in range(1, 16):
        acc = acc + rows[:, m * 128 : (m + 1) * 128]
    at = lax.broadcasted_iota(jnp.int32, (8, 128), 0)
    kl[...] = jnp.where(at == 0, acc, jnp.where(at == 1, n.astype(F32), 0.0))


def grads(feats, lse):
    vmem = pl.BlockSpec(memory_space=VMEM)
    return pl.pallas_call(
        grads_kernel,
        out_shape=(jax.ShapeDtypeStruct((W, OWN), F32), jax.ShapeDtypeStruct((8, 128), F32)),
        in_specs=[vmem, vmem],
        out_specs=(vmem, vmem),
        scratch_shapes=[
            VMEM((128, OWN), BF16),
            VMEM((128, OWN), BF16),
            VMEM((128, OWN), BF16),
            VMEM((8, OWN), F32),
            VMEM((4 * W, LEN), BF16),
            VMEM((3 * W, OWN), F32),
            VMEM((2 * W, OWN), F32),
        ],
        compiler_params=params(),
    )(feats, lse)


def grads_wide(feats, lse):
    doc, _, _, z, _ = coords()
    d = doc * 4 + z
    n = lse[0, 33, 0].astype(jnp.int32)
    f = feats[:, :, :, :ROWS, :].reshape(LEN // 1024, 8, 128, 128)
    mine = lax.dynamic_index_in_dim(f, d, 1, keepdims=False).reshape(OWN, 128)
    cols = f.reshape(LEN // 1024, 1024, 128)
    col_lse = jnp.transpose(lse[:, :32].reshape(8, 2, 16, 128), (2, 1, 0, 3)).reshape(16, 2, 1024)
    own_lse = lax.dynamic_index_in_dim(lse, d, 0, keepdims=False)[:32].reshape(2, OWN)
    lt, ls = own_lse[0][:, None], own_lse[1][:, None]
    lane = jnp.arange(OWN)
    live = (((lane // 128) * 8 + d) * 128 + lane % 128 < n)[:, None]

    def step(j, carry):
        grad, kl = carry
        c = lax.dynamic_index_in_dim(cols, j, 0, keepdims=False)
        cl = lax.dynamic_index_in_dim(col_lse, j, 0, keepdims=False)
        both = live & (j * 1024 + jnp.arange(1024) < n)[None, :]
        t = jnp.dot(mine[:, :W], c[:, :W].T, preferred_element_type=F32) * 0.125
        s = jnp.dot(mine[:, W:], c[:, W:].T, preferred_element_type=F32) * 0.125
        pt = jnp.where(both, jnp.exp(t - lt), 0.0)
        rows = jnp.where(both, jnp.exp(s - ls), 0.0) - pt
        columns = jnp.where(both, jnp.exp(s - cl[1:2]) - jnp.exp(t - cl[0:1]), 0.0)
        w = (rows + columns).astype(BF16)
        grad = grad + jnp.dot(w, c[:, W:], preferred_element_type=F32) * 0.125
        return grad, kl + jnp.sum(pt * (t - s), axis=1, keepdims=True)

    zero = (jnp.zeros((OWN, W), F32), jnp.zeros((OWN, 1), F32))
    grad, kl = lax.fori_loop(0, 16, step, zero)
    rows = jnp.where(live, kl - lt + ls, 0.0).reshape(16, 128)
    tile = jnp.concatenate(
        [jnp.sum(rows, axis=0, keepdims=True), jnp.full((1, 128), n.astype(F32)), jnp.zeros((6, 128), F32)]
    )
    return grad.T, tile


def give_kernel(grad, kl, got, loss, got_kl, sums, got_sum, sg, rg, sk, rk, ss, rs):
    doc, head, x, z, yh = coords()
    me = device(doc, head, x, z, yh)
    to = [device(x // 2, head, m // 4, m % 4, doc) for m in range(16)]
    sources = [device(yh, head, 2 * doc + k, q, e) for k in range(2) for e in range(2) for q in range(4)]
    ring = [device(doc, 1 - head, x, z, yh), device(doc, head, x, z, 1 - yh), device(doc, 1 - head, x, z, 1 - yh)]
    greet(to + sources + ring, me)
    kind, part, q = x % 2, yh, z
    slot = (kind * 2 + part) * 4 + q
    where = pl.ds(pl.multiple_of(part * W, W), W)
    def send(m, src, dst, send_sem, recv_sem):
        mine = same(to[m], me)

        @pl.when(mine)
        def _():
            pltpu.make_async_copy(src, dst, recv_sem).start()

        @pl.when(jnp.logical_not(mine))
        def _():
            pltpu.make_async_remote_copy(
                src, dst, send_sem, recv_sem, device_id=to[m], device_id_type=MESH
            ).start()

    for m in range(16):
        send(m, kl, got_kl.at[slot], sk.at[m], rk.at[slot])
    for m in range(16):
        send(m, grad.at[:, m * 128 : (m + 1) * 128], got.at[kind, q, where], sg.at[m], rg.at[slot])

    total = jnp.zeros((8, 128), F32)
    for i in range(16):
        pltpu.make_async_copy(kl, got_kl.at[i], rk.at[i]).wait()
        total = total + got_kl[i]
    sums[...] = total
    swaps = []
    for i in range(3):
        copy = pltpu.make_async_remote_copy(
            sums, got_sum.at[i], ss.at[i], rs.at[i], device_id=ring[i], device_id_type=MESH
        )
        copy.start()
        swaps.append(copy)
    for i in range(3):
        swaps[i].wait_recv()
        total = total + got_sum[i]
    for i in range(3):
        swaps[i].wait_send()
    kl_sum = jnp.sum(total[0:1, :], axis=1, keepdims=True)
    count = total[1:2, 0:1] * (1.0 / 64.0)
    loss[...] = jnp.broadcast_to(kl_sum / (count * (2.0 * REL_HEADS)), (8, 128))
    for k in range(2):
        for q_ in range(4):
            for e in range(2):
                part_ref = got.at[k, q_, pl.ds(e * W, W)]
                pltpu.make_async_copy(part_ref, part_ref, rg.at[(k * 2 + e) * 4 + q_]).wait()
    for m in range(16):
        src = grad.at[:, m * 128 : (m + 1) * 128]

        @pl.when(jnp.logical_not(same(to[m], me)))
        def _():
            pltpu.make_async_remote_copy(
                src, got.at[kind, q, where], sg.at[m], rg.at[slot], device_id=to[m], device_id_type=MESH
            ).wait_send()
            pltpu.make_async_remote_copy(
                kl, got_kl.at[slot], sk.at[m], rk.at[slot], device_id=to[m], device_id_type=MESH
            ).wait_send()


def give(grad, kl):
    dma = pltpu.SemaphoreType.DMA
    vmem = pl.BlockSpec(memory_space=VMEM)
    return pl.pallas_call(
        give_kernel,
        out_shape=(jax.ShapeDtypeStruct((2, 4, 128, 128), F32), jax.ShapeDtypeStruct((8, 128), F32)),
        in_specs=[vmem, vmem],
        out_specs=(vmem, vmem),
        scratch_shapes=[
            VMEM((16, 8, 128), F32),
            VMEM((8, 128), F32),
            VMEM((3, 8, 128), F32),
            dma((16,)), dma((16,)), dma((16,)), dma((16,)), dma((3,)), dma((3,)),
        ],
        compiler_params=params(collective_id=2, has_side_effects=True),
    )(grad, kl)


def turn_kernel(got, tile, gq, gv, loss):
    for k, out in ((0, gq), (1, gv)):
        for q in range(4):
            out[0, q * 128 : (q + 1) * 128, :] = got[k, q].T
    loss[0] = jnp.max(tile[...])


def turn(got, tile):
    vmem = pl.BlockSpec(memory_space=VMEM)
    out = jax.ShapeDtypeStruct((1, ROWS, 128), F32)
    return pl.pallas_call(
        turn_kernel,
        out_shape=(out, out, jax.ShapeDtypeStruct((1,), F32)),
        in_specs=[vmem, vmem],
        out_specs=(vmem, vmem, pl.BlockSpec(memory_space=pltpu.SMEM)),
        compiler_params=params(),
    )(got, tile)


def shards(token_ids, teacher_query, teacher_value, student_query, student_value, teacher_pick, student_pick):
    msg_a, msg_b = pick(
        teacher_pick, student_pick, token_ids.reshape(4, 128),
        teacher_query[0], teacher_value[0], student_query[0], student_value[0],
    )
    feats, part = gather(teacher_pick, msg_a, msg_b)
    lse, fast = share(sums(feats, part))
    grad, kl = lax.cond(fast[0] > 0, grads, grads_wide, feats, lse)
    return turn(*give(grad, kl))


def solution(mesh):
    return jax.shard_map(
        shards,
        mesh=mesh,
        in_specs=(
            P("doc", "seq"),
            P("doc", "seq", "head"),
            P("doc", "seq", "head"),
            P("doc", "seq", None),
            P("doc", "seq", None),
            P(),
            P(),
        ),
        out_specs=(P("doc", "seq", "head"), P("doc", "seq", "head"), P("doc")),
        check_vma=False,
    )
```

```python
import functools

import jax
import jax.numpy as jnp
from jax import lax
from jax.experimental import pallas as pl
from jax.experimental.pallas import tpu as pltpu
from jax.sharding import PartitionSpec as P

HEAD_DIM = 128
W = 64
PER_HEAD = HEAD_DIM // W
T_GROUP = 8
S_GROUP = 7
REL_HEADS = 4
LEN = 16384
ROWS = 512
PIECE = ROWS + 16
OWN = 2048
TOP_BOUND = 162.0
LN2 = 0.6931471805599453
LOG2E = 1.4426950408889634
SHIFT = 74.0
FAST_TOP = 130.0
STEP = 2048
F32 = jnp.float32
BF16 = jnp.bfloat16
MESH = pl.DeviceIdType.MESH
VMEM = pltpu.VMEM
ANY = pl.ANY


def coords():
    doc = lax.axis_index("doc")
    head = lax.axis_index("head")
    seq = lax.axis_index("seq")
    return doc, head, seq // 8, (seq // 2) % 4, seq % 2


def device(doc, head, x, z, yh):
    return (doc, head, (x * 4 + z) * 2 + yh)


def same(a, b):
    return (a[0] == b[0]) & (a[1] == b[1]) & (a[2] == b[2])


def params(**kw):
    return pltpu.CompilerParams(vmem_limit_bytes=56 * 2**20, **kw)


def pick_kernel(tp, sp, ids, tq, tv, sq, sv, msg_a, msg_b, tw, sw, sem):
    head = lax.axis_index("head")
    copies = []

    def fetch(src, block, dst):
        start = pl.multiple_of((block // 2) * 128, 128)
        copy = pltpu.make_async_copy(src.at[:, pl.ds(start, 128)], dst, sem.at[len(copies)])
        copy.start()
        copies.append(copy)

    q_blocks = tq.shape[1] // W
    v_blocks = tv.shape[1] // W
    for r in range(REL_HEADS):
        b = tp[r]
        vb = (b // PER_HEAD) // T_GROUP * PER_HEAD + b % PER_HEAD
        fetch(tq, b % q_blocks, tw.at[0, r])
        fetch(tv, vb % v_blocks, tw.at[1, r])
    for e in range(2):
        b = sp[head * 2 + e]
        vb = (b // PER_HEAD) // S_GROUP * PER_HEAD + b % PER_HEAD
        fetch(sq, b, sw.at[0, e])
        fetch(sv, vb, sw.at[1, e])
    for copy in copies:
        copy.wait()

    def half(w, b):
        return jnp.where(b % 2 == 0, w[:, :W], w[:, W:])

    live = (ids[...] != 0).astype(F32)
    tail = jnp.concatenate([live, jnp.zeros((12, 128), F32)], axis=0).astype(BF16)
    upright = jnp.concatenate([live, jnp.zeros((4, 128), F32)], axis=0).T
    keep = jnp.concatenate([jnp.broadcast_to(upright[:, i : i + 1], (128, W)) for i in range(4)], axis=0)
    keep = keep.astype(BF16)
    for k in range(2):
        for e in range(2):
            r = head * 2 + e
            t = half(tw[k, r], tp[r]) * keep
            s = half(sw[k, e], sp[r]) * keep
            msg_a[k, e, 0:ROWS, :] = jnp.concatenate([t, s], axis=1)
            msg_a[k, e, ROWS:PIECE, :] = tail
            r = (1 - head) * 2 + e
            t = half(tw[k, r], tp[r]) * keep
            msg_b[k, e] = jnp.concatenate([t[: ROWS // 2], t[ROWS // 2 :]], axis=1)


def pick(tp, sp, ids, tq, tv, sq, sv):
    smem = pl.BlockSpec(memory_space=pltpu.SMEM)
    vmem = pl.BlockSpec(memory_space=VMEM)
    hbm = pl.BlockSpec(memory_space=ANY)
    return pl.pallas_call(
        pick_kernel,
        out_shape=(
            jax.ShapeDtypeStruct((2, 2, PIECE, 128), BF16),
            jax.ShapeDtypeStruct((2, 2, ROWS // 2, 128), BF16),
        ),
        in_specs=[smem, smem, vmem, hbm, hbm, hbm, hbm],
        out_specs=(vmem, vmem),
        scratch_shapes=[
            VMEM((2, 4, ROWS, 128), BF16),
            VMEM((2, 2, ROWS, 128), BF16),
            pltpu.SemaphoreType.DMA((12,)),
        ],
        compiler_params=params(),
    )(tp, sp, ids, tq, tv, sq, sv)


def greet(peers, me):
    barrier = pltpu.get_barrier_semaphore()
    count = 0
    for peer in peers:
        other = jnp.logical_not(same(peer, me))

        @pl.when(other)
        def _():
            pl.semaphore_signal(barrier, inc=1, device_id=peer, device_id_type=MESH)

        count = count + other.astype(jnp.int32)
    pl.semaphore_wait(barrier, count)


def gather_kernel(
    tp, msg_a, msg_b, out, got_a, got_b, chunk,
    sa, sb, ra, rb, s_own, s_core, s_up, s_dn, r_core, r_up, r_dn,
):
    doc, head, x, z, yh = coords()
    me = device(doc, head, x, z, yh)
    core = device(1 - doc, head, x, z, yh)
    up = device(doc, head, x, (z + 1) % 4, yh)
    down = device(doc, head, x, (z + 3) % 4, yh)
    kinds = [((x == 2 * doc + 1) | (x == (2 * doc + 2) % 4)).astype(jnp.int32)]
    kinds.append(1 - kinds[0])
    to_a = [[device(yh, head, 2 * doc + k, z, e) for e in range(2)] for k in kinds]
    to_b = [[device(yh, 1 - head, 2 * doc + k, z, e) for e in range(2)] for k in kinds]
    from_doc = x // 2
    sources = [device(from_doc, h, xs, z, doc) for h in range(2) for xs in range(4)]
    greet(to_a[0] + to_a[1] + to_b[0] + to_b[1] + sources + [core, up, down], me)

    def scatter(i, act):
        k = kinds[i]
        for e in range(2):
            mine = same(to_a[i][e], me)

            if act == "start":

                @pl.when(mine)
                def _():
                    pltpu.make_async_copy(msg_a.at[k, e], got_a.at[x], ra.at[x]).start()

            @pl.when(jnp.logical_not(mine))
            def _():
                copy = pltpu.make_async_remote_copy(
                    msg_a.at[k, e], got_a.at[x], sa.at[i, e], ra.at[x],
                    device_id=to_a[i][e], device_id_type=MESH,
                )
                copy.start() if act == "start" else copy.wait_send()

            copy = pltpu.make_async_remote_copy(
                msg_b.at[k, e], got_b.at[x], sb.at[i, e], rb.at[x],
                device_id=to_b[i][e], device_id_type=MESH,
            )
            copy.start() if act == "start" else copy.wait_send()

    scatter(0, "start")
    scatter(0, "wait")
    scatter(1, "start")

    own = tp[head * 2 + yh] // (REL_HEADS * 16) == head

    def remote(src, dst, send, recv, to):
        return pltpu.make_async_remote_copy(
            src, dst, send, recv, device_id=to, device_id_type=MESH
        )

    def place(i, zz, c):
        return out.at[order[i], zz, c]

    sends = []
    lane = lax.broadcasted_iota(jnp.int32, (ROWS // 2, 128), 1)
    beside = x + 1 - 2 * (x % 2)
    order = [x, 3 - x, beside, 3 - beside]
    for i, xs in enumerate(order):
        pltpu.make_async_copy(msg_a.at[0, 0], got_a.at[xs], ra.at[xs]).wait()
        pltpu.make_async_copy(msg_b.at[0, 0], got_b.at[xs], rb.at[xs]).wait()
        b = got_b[xs]
        b_roll = jnp.concatenate([b[:, W:], b[:, :W]], axis=1)
        keep = jnp.logical_or(own, lane >= W)
        chunk[i, 0 : ROWS // 2] = jnp.where(keep, got_a[xs, 0 : ROWS // 2], b)
        chunk[i, ROWS // 2 : ROWS] = jnp.where(keep, got_a[xs, ROWS // 2 : ROWS], b_roll)
        chunk[i, ROWS:PIECE] = got_a[xs, ROWS:PIECE]
        for copy in (
            remote(chunk.at[i], place(i, z, doc), s_up.at[i], r_dn.at[i], up),
            remote(chunk.at[i], place(i, z, doc), s_dn.at[i], r_up.at[i], down),
            remote(chunk.at[i], place(i, z, doc), s_core.at[i], r_core.at[i], core),
        ):
            copy.start()
            sends.append(copy)
        local = pltpu.make_async_copy(chunk.at[i], place(i, z, doc), s_own.at[i])
        local.start()
        sends.append(local)

    below, above, across = (z + 3) % 4, (z + 1) % 4, (z + 2) % 4

    def forward(src, send, recv, to):
        copy = remote(src, src, send, recv, to)
        copy.start()
        sends.append(copy)

    def arrived(ref, sem):
        pltpu.make_async_copy(ref, ref, sem).wait()

    for i in range(4):
        lo = place(i, below, doc)
        arrived(lo, r_dn.at[i])
        if i < 2:
            forward(lo, s_up.at[4 + i], r_dn.at[4 + i], up)
        forward(lo, s_core.at[4 + i], r_core.at[4 + i], core)
        hi = place(i, above, doc)
        arrived(hi, r_up.at[i])
        if i >= 2:
            forward(hi, s_dn.at[2 + i], r_up.at[2 + i], down)
        forward(hi, s_core.at[8 + i], r_core.at[8 + i], core)
    for i in range(4):
        far = place(i, across, doc)
        arrived(far, r_dn.at[4 + i] if i < 2 else r_up.at[2 + i])
        forward(far, s_core.at[12 + i], r_core.at[12 + i], core)
    for i in range(4):
        arrived(place(i, z, 1 - doc), r_core.at[i])
        arrived(place(i, below, 1 - doc), r_core.at[4 + i])
        arrived(place(i, above, 1 - doc), r_core.at[8 + i])
        arrived(place(i, across, 1 - doc), r_core.at[12 + i])
    for copy in sends:
        if hasattr(copy, "wait_send") and copy.is_remote:
            copy.wait_send()
        else:
            copy.wait()
    scatter(1, "wait")


def gather(tp, msg_a, msg_b):
    dma = pltpu.SemaphoreType.DMA
    vmem = pl.BlockSpec(memory_space=VMEM)
    return pl.pallas_call(
        gather_kernel,
        out_shape=jax.ShapeDtypeStruct((4, 4, 2, PIECE, 128), BF16),
        in_specs=[pl.BlockSpec(memory_space=pltpu.SMEM), vmem, vmem],
        out_specs=pl.BlockSpec(memory_space=ANY),
        scratch_shapes=[
            VMEM((4, PIECE, 128), BF16),
            VMEM((4, ROWS // 2, 128), BF16),
            VMEM((4, PIECE, 128), BF16),
            dma((2, 2)), dma((2, 2)), dma((4,)), dma((4,)),
            dma((4,)), dma((16,)), dma((6,)), dma((6,)), dma((16,)), dma((6,)), dma((6,)),
        ],
        compiler_params=params(collective_id=0, has_side_effects=True),
    )(tp, msg_a, msg_b)


def live_count(feats):
    total = jnp.zeros((16, 128), F32)
    for i in range(4):
        for zz in range(4):
            for c in range(2):
                total = total + feats[i, zz, c, ROWS:PIECE, :].astype(F32)
    return jnp.sum(total).astype(jnp.int32)


def block(feats, b):
    return feats[b // 8, (b // 2) % 4, b % 2, 0:ROWS, :]


def tile_scores(feats, b, count, rows):
    parts = [jnp.dot(block(feats, b + i), rows, preferred_element_type=F32) for i in range(count)]
    return jnp.concatenate(parts, axis=0)


def own_rows(feats, d, own):
    for m in range(16):
        b = 2 * m + d // 4
        part = feats[b // 8, (b // 2) % 4, b % 2, pl.ds(pl.multiple_of((d % 4) * 128, 128), 128), :]
        own[:, m * 128 : (m + 1) * 128] = part.T


def self_scores(feat):
    f = feat.astype(F32)
    return jnp.sum(f * f, axis=0, keepdims=True) * 0.125


def row_shift(own_score):
    room = 75.0 - (jnp.sqrt(own_score * TOP_BOUND) - own_score)
    k = jnp.floor(jnp.maximum(jnp.minimum(room, own_score), 0.0) * LOG2E)
    return own_score * LOG2E - k, k


def fill_rows(own, xi, yi, shifts):
    zero = jnp.zeros((W, OWN), BF16)
    xi[0:W, :] = own[0:W, :] * jnp.asarray(0.125, BF16)
    xi[W:, :] = zero
    yi[0:W, :] = zero
    yi[W:, :] = own[W:, :] * jnp.asarray(0.125, BF16)
    shifts[0:1, :] = row_shift(self_scores(own[0:W, :]))[0]
    shifts[1:2, :] = row_shift(self_scores(own[W:, :]))[0]


def own_live(n, d):
    lane = lax.broadcasted_iota(jnp.int32, (1, OWN), 1)
    token = ((lane // 128) * 8 + d) * 128 + lane % 128
    return token < n


def row_tiles(n, d, tile):
    blocks = jnp.clip((n - d * 128 + 1023) // 1024, 0, 16)
    need = jnp.maximum((blocks + 1) // 2, 4)
    for width in range(4, 9):

        @pl.when(need == width)
        def _():
            def half(i, _):
                tile(pl.multiple_of(i * width * 128, 128), width * 128)
                return 0

            lax.fori_loop(0, 2, half, 0)


def sums_kernel(feats, out, own, xi, yi, shifts, acc_t, acc_s):
    doc, _, _, z, _ = coords()
    d = doc * 4 + z
    n = live_count(feats)
    own_rows(feats, d, own)
    fill_rows(own, xi, yi, shifts)
    acc_t[...] = jnp.ones_like(acc_t)
    acc_s[...] = jnp.ones_like(acc_s)
    steps = (n + STEP - 1) // STEP

    def tile(start, width):
        at = pl.ds(start, width)

        def step(j, carry):
            b = j * (STEP // ROWS)
            t = jnp.exp2(tile_scores(feats, b, STEP // ROWS, xi[:, at]) * LOG2E - shifts[0:1, at])
            s = jnp.exp2(tile_scores(feats, b, STEP // ROWS, yi[:, at]) * LOG2E - shifts[1:2, at])
            add_t = jnp.sum(t.reshape(STEP // 8, 8, width), axis=0)
            add_s = jnp.sum(s.reshape(STEP // 8, 8, width), axis=0)
            return carry[0] + add_t, carry[1] + add_s

        zero = jnp.zeros((8, width), F32)
        t, s = lax.fori_loop(0, steps, step, (zero, zero))
        acc_t[:, at] = t
        acc_s[:, at] = s

    row_tiles(n, d, tile)
    live = own_live(n, d)
    st = self_scores(own[0:W, :])
    ss = self_scores(own[W:, :])
    dead = (steps * STEP - n).astype(F32)
    sum_t = jnp.sum(acc_t[...], axis=0, keepdims=True) - dead * jnp.exp2(-shifts[0:1, :])
    sum_s = jnp.sum(acc_s[...], axis=0, keepdims=True) - dead * jnp.exp2(-shifts[1:2, :])
    lt = shifts[0:1, :] * LN2 + jnp.log(sum_t)
    ls = shifts[1:2, :] * LN2 + jnp.log(sum_s)
    top = jnp.max(jnp.where(live, jnp.maximum(st, ss), 0.0))
    lt = jnp.where(live, lt, 0.0)
    ls = jnp.where(live, ls, 0.0)
    for m in range(16):
        out[m : m + 1, :] = lt[:, m * 128 : (m + 1) * 128]
        out[16 + m : 17 + m, :] = ls[:, m * 128 : (m + 1) * 128]
    at = lax.broadcasted_iota(jnp.int32, (8, 128), 0)
    out[32:40, :] = jnp.where(at == 0, top, jnp.where(at == 1, n.astype(F32), 0.0))


def sums(feats):
    return pl.pallas_call(
        sums_kernel,
        out_shape=jax.ShapeDtypeStruct((40, 128), F32),
        in_specs=[pl.BlockSpec(memory_space=VMEM)],
        out_specs=pl.BlockSpec(memory_space=VMEM),
        scratch_shapes=[
            VMEM((128, OWN), BF16),
            VMEM((128, OWN), BF16),
            VMEM((128, OWN), BF16),
            VMEM((8, OWN), F32),
            VMEM((8, OWN), F32),
            VMEM((8, OWN), F32),
        ],
        compiler_params=params(),
    )(feats)


def share_kernel(mine, out, flag, s_own, send, recv):
    doc, head, x, z, yh = coords()
    me = device(doc, head, x, z, yh)
    d = doc * 4 + z
    peers = []
    for step in range(1, 8):
        p = (d + step) % 8
        peers.append(device(p // 4, head, x, p % 4, yh))
    greet(peers, me)
    copies = []
    for step in range(1, 8):
        copy = pltpu.make_async_remote_copy(
            mine, out.at[d], send.at[step - 1], recv.at[step - 1],
            device_id=peers[step - 1], device_id_type=MESH,
        )
        copy.start()
        copies.append(copy)
    local = pltpu.make_async_copy(mine, out.at[d], s_own)
    local.start()
    for step in range(1, 8):
        p = (d + 8 - step) % 8
        pltpu.make_async_copy(mine, out.at[p], recv.at[step - 1]).wait()
    local.wait()
    flag[0] = (jnp.max(out[:, 32:33, :]) <= FAST_TOP).astype(jnp.int32)
    for copy in copies:
        copy.wait_send()


def share(mine):
    dma = pltpu.SemaphoreType.DMA
    vmem = pl.BlockSpec(memory_space=VMEM)
    return pl.pallas_call(
        share_kernel,
        out_shape=(jax.ShapeDtypeStruct((8, 40, 128), F32), jax.ShapeDtypeStruct((1,), jnp.int32)),
        in_specs=[vmem],
        out_specs=(vmem, pl.BlockSpec(memory_space=pltpu.SMEM)),
        scratch_shapes=[dma, dma((7,)), dma((7,))],
        compiler_params=params(collective_id=1, has_side_effects=True),
    )(mine)


def grads_kernel(feats, lse, grad, kl, own, xi, yi, shifts, v, ot, os_):
    doc, _, _, z, _ = coords()
    d = doc * 4 + z
    n = jnp.max(lse[0, 33:34, :]).astype(jnp.int32)
    own_rows(feats, d, own)
    fill_rows(own, xi, yi, shifts)
    steps = (n + STEP - 1) // STEP

    def weigh(b, _):
        f = block(feats, b).T
        x, y = f[:W, :], f[W:, :]
        yf = y.astype(F32)
        at = pl.ds(pl.multiple_of(b * ROWS, ROWS), ROWS)
        lt, ls = [], []
        for q in range(4):
            m = (b * 4 + q) // 8
            dd = (b * 4 + q) % 8
            lt.append(lse[dd, pl.ds(m, 1), :])
            ls.append(lse[dd, pl.ds(16 + m, 1), :])
        live = lax.broadcasted_iota(jnp.int32, (1, ROWS), 1) + b * ROWS < n
        wt = jnp.where(live, jnp.exp(SHIFT - jnp.concatenate(lt, axis=1)), 0.0)
        ws = jnp.where(live, jnp.exp(SHIFT - jnp.concatenate(ls, axis=1)), 0.0)
        keep = jnp.where(live, 1.0, 0.0).astype(BF16)
        v[0:W, at] = x * keep
        v[W : 2 * W, at] = (yf * wt).astype(BF16)
        v[2 * W : 3 * W, at] = y * keep
        v[3 * W :, at] = (yf * ws).astype(BF16)
        return 0

    lax.fori_loop(0, steps * (STEP // ROWS), weigh, 0)
    ot[...] = jnp.zeros_like(ot)
    os_[...] = jnp.zeros_like(os_)

    def tile(start, width):
        at = pl.ds(start, width)

        def step(j, _):
            js = pl.ds(pl.multiple_of(j * STEP, STEP), STEP)
            b = j * (STEP // ROWS)
            t = jnp.exp2(tile_scores(feats, b, STEP // ROWS, xi[:, at]) * LOG2E - shifts[0:1, at]).astype(BF16)
            s = jnp.exp2(tile_scores(feats, b, STEP // ROWS, yi[:, at]) * LOG2E - shifts[1:2, at]).astype(BF16)
            ot[:, at] += jnp.dot(v[0 : 3 * W, js], t, preferred_element_type=F32)
            os_[:, at] += jnp.dot(v[2 * W :, js], s, preferred_element_type=F32)
            return 0

        lax.fori_loop(0, steps, step, 0)

    row_tiles(n, d, tile)
    live = own_live(n, d)
    x = own[0:W, :].astype(F32)
    y = own[W:, :].astype(F32)
    mine = lse[d]
    lt = jnp.concatenate([mine[m : m + 1, :] for m in range(16)], axis=1)
    ls = jnp.concatenate([mine[16 + m : 17 + m, :] for m in range(16)], axis=1)

    def finish(by_row_sum, by_col_sum, feat, l):
        shift, k = row_shift(self_scores(feat))
        by_row = jnp.exp(shift * LN2 - l)
        by_col = jnp.exp((shift * LN2 - SHIFT) * 0.5)
        exact = y * jnp.exp(SHIFT - l)
        missing = (exact - exact.astype(BF16).astype(F32)) * jnp.exp2(k)
        return by_row_sum * by_row + (by_col_sum + missing) * by_col * by_col, by_row

    gs, _ = finish(os_[0:W, :], os_[W:, :], own[W:, :], ls)
    gt, by_row = finish(ot[2 * W :, :], ot[W : 2 * W, :], own[0:W, :], lt)
    grad[...] = jnp.where(live, (gs - gt) * 0.125, 0.0)
    moved = jnp.sum(x * ot[0:W, :] - y * ot[2 * W :, :], axis=0, keepdims=True)
    rows = jnp.where(live, moved * by_row * 0.125 - lt + ls, 0.0)
    acc = rows[:, 0:128]
    for m in range(1, 16):
        acc = acc + rows[:, m * 128 : (m + 1) * 128]
    at = lax.broadcasted_iota(jnp.int32, (8, 128), 0)
    kl[...] = jnp.where(at == 0, acc, jnp.where(at == 1, n.astype(F32), 0.0))


def grads(feats, lse):
    vmem = pl.BlockSpec(memory_space=VMEM)
    return pl.pallas_call(
        grads_kernel,
        out_shape=(jax.ShapeDtypeStruct((W, OWN), F32), jax.ShapeDtypeStruct((8, 128), F32)),
        in_specs=[vmem, vmem],
        out_specs=(vmem, vmem),
        scratch_shapes=[
            VMEM((128, OWN), BF16),
            VMEM((128, OWN), BF16),
            VMEM((128, OWN), BF16),
            VMEM((8, OWN), F32),
            VMEM((4 * W, LEN), BF16),
            VMEM((3 * W, OWN), F32),
            VMEM((2 * W, OWN), F32),
        ],
        compiler_params=params(),
    )(feats, lse)


def grads_wide(feats, lse):
    doc, _, _, z, _ = coords()
    d = doc * 4 + z
    n = lse[0, 33, 0].astype(jnp.int32)
    f = feats[:, :, :, :ROWS, :].reshape(LEN // 1024, 8, 128, 128)
    mine = lax.dynamic_index_in_dim(f, d, 1, keepdims=False).reshape(OWN, 128)
    cols = f.reshape(LEN // 1024, 1024, 128)
    col_lse = jnp.transpose(lse[:, :32].reshape(8, 2, 16, 128), (2, 1, 0, 3)).reshape(16, 2, 1024)
    own_lse = lax.dynamic_index_in_dim(lse, d, 0, keepdims=False)[:32].reshape(2, OWN)
    lt, ls = own_lse[0][:, None], own_lse[1][:, None]
    lane = jnp.arange(OWN)
    live = (((lane // 128) * 8 + d) * 128 + lane % 128 < n)[:, None]

    def step(j, carry):
        grad, kl = carry
        c = lax.dynamic_index_in_dim(cols, j, 0, keepdims=False)
        cl = lax.dynamic_index_in_dim(col_lse, j, 0, keepdims=False)
        both = live & (j * 1024 + jnp.arange(1024) < n)[None, :]
        t = jnp.dot(mine[:, :W], c[:, :W].T, preferred_element_type=F32) * 0.125
        s = jnp.dot(mine[:, W:], c[:, W:].T, preferred_element_type=F32) * 0.125
        pt = jnp.where(both, jnp.exp(t - lt), 0.0)
        rows = jnp.where(both, jnp.exp(s - ls), 0.0) - pt
        columns = jnp.where(both, jnp.exp(s - cl[1:2]) - jnp.exp(t - cl[0:1]), 0.0)
        w = (rows + columns).astype(BF16)
        grad = grad + jnp.dot(w, c[:, W:], preferred_element_type=F32) * 0.125
        return grad, kl + jnp.sum(pt * (t - s), axis=1, keepdims=True)

    zero = (jnp.zeros((OWN, W), F32), jnp.zeros((OWN, 1), F32))
    grad, kl = lax.fori_loop(0, 16, step, zero)
    rows = jnp.where(live, kl - lt + ls, 0.0).reshape(16, 128)
    tile = jnp.concatenate(
        [jnp.sum(rows, axis=0, keepdims=True), jnp.full((1, 128), n.astype(F32)), jnp.zeros((6, 128), F32)]
    )
    return grad.T, tile


def give_kernel(grad, kl, got, loss, got_kl, sums, got_sum, sg, rg, sk, rk, ss, rs):
    doc, head, x, z, yh = coords()
    me = device(doc, head, x, z, yh)
    to = [device(x // 2, head, m // 4, m % 4, doc) for m in range(16)]
    sources = [device(yh, head, 2 * doc + k, q, e) for k in range(2) for e in range(2) for q in range(4)]
    ring = [device(doc, 1 - head, x, z, yh), device(doc, head, x, z, 1 - yh), device(doc, 1 - head, x, z, 1 - yh)]
    greet(to + sources + ring, me)
    kind, part, q = x % 2, yh, z
    slot = (kind * 2 + part) * 4 + q
    where = pl.ds(pl.multiple_of(part * W, W), W)
    def send(m, src, dst, send_sem, recv_sem):
        mine = same(to[m], me)

        @pl.when(mine)
        def _():
            pltpu.make_async_copy(src, dst, recv_sem).start()

        @pl.when(jnp.logical_not(mine))
        def _():
            pltpu.make_async_remote_copy(
                src, dst, send_sem, recv_sem, device_id=to[m], device_id_type=MESH
            ).start()

    for m in range(16):
        send(m, kl, got_kl.at[slot], sk.at[m], rk.at[slot])
    for m in range(16):
        send(m, grad.at[:, m * 128 : (m + 1) * 128], got.at[kind, q, where], sg.at[m], rg.at[slot])

    total = jnp.zeros((8, 128), F32)
    for i in range(16):
        pltpu.make_async_copy(kl, got_kl.at[i], rk.at[i]).wait()
        total = total + got_kl[i]
    sums[...] = total
    swaps = []
    for i in range(3):
        copy = pltpu.make_async_remote_copy(
            sums, got_sum.at[i], ss.at[i], rs.at[i], device_id=ring[i], device_id_type=MESH
        )
        copy.start()
        swaps.append(copy)
    for i in range(3):
        swaps[i].wait_recv()
        total = total + got_sum[i]
    for i in range(3):
        swaps[i].wait_send()
    kl_sum = jnp.sum(total[0:1, :], axis=1, keepdims=True)
    count = total[1:2, 0:1] * (1.0 / 64.0)
    loss[...] = jnp.broadcast_to(kl_sum / (count * (2.0 * REL_HEADS)), (8, 128))
    for k in range(2):
        for q_ in range(4):
            for e in range(2):
                part_ref = got.at[k, q_, pl.ds(e * W, W)]
                pltpu.make_async_copy(part_ref, part_ref, rg.at[(k * 2 + e) * 4 + q_]).wait()
    for m in range(16):
        src = grad.at[:, m * 128 : (m + 1) * 128]

        @pl.when(jnp.logical_not(same(to[m], me)))
        def _():
            pltpu.make_async_remote_copy(
                src, got.at[kind, q, where], sg.at[m], rg.at[slot], device_id=to[m], device_id_type=MESH
            ).wait_send()
            pltpu.make_async_remote_copy(
                kl, got_kl.at[slot], sk.at[m], rk.at[slot], device_id=to[m], device_id_type=MESH
            ).wait_send()


def give(grad, kl):
    dma = pltpu.SemaphoreType.DMA
    vmem = pl.BlockSpec(memory_space=VMEM)
    return pl.pallas_call(
        give_kernel,
        out_shape=(jax.ShapeDtypeStruct((2, 4, 128, 128), F32), jax.ShapeDtypeStruct((8, 128), F32)),
        in_specs=[vmem, vmem],
        out_specs=(vmem, vmem),
        scratch_shapes=[
            VMEM((16, 8, 128), F32),
            VMEM((8, 128), F32),
            VMEM((3, 8, 128), F32),
            dma((16,)), dma((16,)), dma((16,)), dma((16,)), dma((3,)), dma((3,)),
        ],
        compiler_params=params(collective_id=2, has_side_effects=True),
    )(grad, kl)


def turn_kernel(got, tile, gq, gv, loss):
    for k, out in ((0, gq), (1, gv)):
        for q in range(4):
            out[0, q * 128 : (q + 1) * 128, :] = got[k, q].T
    loss[0] = jnp.max(tile[...])


def turn(got, tile):
    vmem = pl.BlockSpec(memory_space=VMEM)
    out = jax.ShapeDtypeStruct((1, ROWS, 128), F32)
    return pl.pallas_call(
        turn_kernel,
        out_shape=(out, out, jax.ShapeDtypeStruct((1,), F32)),
        in_specs=[vmem, vmem],
        out_specs=(vmem, vmem, pl.BlockSpec(memory_space=pltpu.SMEM)),
        compiler_params=params(),
    )(got, tile)


def shards(token_ids, teacher_query, teacher_value, student_query, student_value, teacher_pick, student_pick):
    msg_a, msg_b = pick(
        teacher_pick, student_pick, token_ids.reshape(4, 128),
        teacher_query[0], teacher_value[0], student_query[0], student_value[0],
    )
    feats = gather(teacher_pick, msg_a, msg_b)
    lse, fast = share(sums(feats))
    grad, kl = lax.cond(fast[0] > 0, grads, grads_wide, feats, lse)
    return turn(*give(grad, kl))


def solution(mesh):
    return jax.shard_map(
        shards,
        mesh=mesh,
        in_specs=(
            P("doc", "seq"),
            P("doc", "seq", "head"),
            P("doc", "seq", "head"),
            P("doc", "seq", None),
            P("doc", "seq", None),
            P(),
            P(),
        ),
        out_specs=(P("doc", "seq", "head"), P("doc", "seq", "head"), P("doc")),
        check_vma=False,
    )
```

```python
import functools

import jax
import jax.numpy as jnp
from jax import lax
from jax.experimental import pallas as pl
from jax.experimental.pallas import tpu as pltpu
from jax.sharding import PartitionSpec as P

HEAD_DIM = 128
W = 64
PER_HEAD = HEAD_DIM // W
T_GROUP = 8
S_GROUP = 7
REL_HEADS = 4
LEN = 16384
ROWS = 512
PIECE = ROWS + 16
OWN = 2048
TOP_BOUND = 162.0
LN2 = 0.6931471805599453
LOG2E = 1.4426950408889634
SHIFT = 74.0
FAST_TOP = 130.0
STEP = 2048
F32 = jnp.float32
BF16 = jnp.bfloat16
MESH = pl.DeviceIdType.MESH
VMEM = pltpu.VMEM
ANY = pl.ANY


def coords():
    doc = lax.axis_index("doc")
    head = lax.axis_index("head")
    seq = lax.axis_index("seq")
    return doc, head, seq // 8, (seq // 2) % 4, seq % 2


def device(doc, head, x, z, yh):
    return (doc, head, (x * 4 + z) * 2 + yh)


def whole_head(head, yh, e):
    return jnp.where(yh == e, head, 1 - head)


def same(a, b):
    return (a[0] == b[0]) & (a[1] == b[1]) & (a[2] == b[2])


def params(**kw):
    return pltpu.CompilerParams(vmem_limit_bytes=56 * 2**20, **kw)


def pick_kernel(tp, sp, ids, tq, tv, sq, sv, msg_a, msg_b, tw, sw, sem):
    _, head, _, _, yh = coords()
    copies = []

    def fetch(src, block, dst):
        start = pl.multiple_of((block // 2) * 128, 128)
        copy = pltpu.make_async_copy(src.at[:, pl.ds(start, 128)], dst, sem.at[len(copies)])
        copy.start()
        copies.append(copy)

    q_blocks = tq.shape[1] // W
    v_blocks = tv.shape[1] // W
    for r in range(REL_HEADS):
        b = tp[r]
        vb = (b // PER_HEAD) // T_GROUP * PER_HEAD + b % PER_HEAD
        fetch(tq, b % q_blocks, tw.at[0, r])
        fetch(tv, vb % v_blocks, tw.at[1, r])
    for e in range(2):
        b = sp[whole_head(head, yh, e) * 2 + e]
        vb = (b // PER_HEAD) // S_GROUP * PER_HEAD + b % PER_HEAD
        fetch(sq, b, sw.at[0, e])
        fetch(sv, vb, sw.at[1, e])
    for copy in copies:
        copy.wait()

    def half(w, b):
        return jnp.where(b % 2 == 0, w[:, :W], w[:, W:])

    live = (ids[...] != 0).astype(F32)
    tail = jnp.concatenate([live, jnp.zeros((12, 128), F32)], axis=0).astype(BF16)
    upright = jnp.concatenate([live, jnp.zeros((4, 128), F32)], axis=0).T
    keep = jnp.concatenate([jnp.broadcast_to(upright[:, i : i + 1], (128, W)) for i in range(4)], axis=0)
    keep = keep.astype(BF16)
    for k in range(2):
        for e in range(2):
            r = whole_head(head, yh, e) * 2 + e
            t = half(tw[k, r], tp[r]) * keep
            s = half(sw[k, e], sp[r]) * keep
            msg_a[k, e, 0:ROWS, :] = jnp.concatenate([t, s], axis=1)
            msg_a[k, e, ROWS:PIECE, :] = tail
            r = (1 - whole_head(head, yh, e)) * 2 + e
            t = half(tw[k, r], tp[r]) * keep
            msg_b[k, e] = jnp.concatenate([t[: ROWS // 2], t[ROWS // 2 :]], axis=1)


def pick(tp, sp, ids, tq, tv, sq, sv):
    smem = pl.BlockSpec(memory_space=pltpu.SMEM)
    vmem = pl.BlockSpec(memory_space=VMEM)
    hbm = pl.BlockSpec(memory_space=ANY)
    return pl.pallas_call(
        pick_kernel,
        out_shape=(
            jax.ShapeDtypeStruct((2, 2, PIECE, 128), BF16),
            jax.ShapeDtypeStruct((2, 2, ROWS // 2, 128), BF16),
        ),
        in_specs=[smem, smem, vmem, hbm, hbm, hbm, hbm],
        out_specs=(vmem, vmem),
        scratch_shapes=[
            VMEM((2, 4, ROWS, 128), BF16),
            VMEM((2, 2, ROWS, 128), BF16),
            pltpu.SemaphoreType.DMA((12,)),
        ],
        compiler_params=params(),
    )(tp, sp, ids, tq, tv, sq, sv)


def greet(peers, me):
    barrier = pltpu.get_barrier_semaphore()
    count = 0
    for peer in peers:
        other = jnp.logical_not(same(peer, me))

        @pl.when(other)
        def _():
            pl.semaphore_signal(barrier, inc=1, device_id=peer, device_id_type=MESH)

        count = count + other.astype(jnp.int32)
    pl.semaphore_wait(barrier, count)


def gather_kernel(
    tp, msg_a, msg_b, out, got_a, got_b, chunk,
    sa, sb, ra, rb, s_own, s_core, s_up, s_dn, r_core, r_up, r_dn,
):
    doc, head, x, z, yh = coords()
    me = device(doc, head, x, z, yh)
    core = device(1 - doc, head, x, z, yh)
    up = device(doc, head, x, (z + 1) % 4, yh)
    down = device(doc, head, x, (z + 3) % 4, yh)
    kinds = [((x == 2 * doc + 1) | (x == (2 * doc + 2) % 4)).astype(jnp.int32)]
    kinds.append(1 - kinds[0])
    to_a = [[device(yh, whole_head(head, yh, e), 2 * doc + k, z, e) for e in range(2)] for k in kinds]
    to_b = [[device(yh, 1 - whole_head(head, yh, e), 2 * doc + k, z, e) for e in range(2)] for k in kinds]
    from_doc = x // 2
    sources = [device(from_doc, h, xs, z, doc) for h in range(2) for xs in range(4)]
    greet(to_a[0] + to_a[1] + to_b[0] + to_b[1] + sources + [core, up, down], me)

    def scatter(i, act):
        k = kinds[i]
        for e in range(2):
            mine = same(to_a[i][e], me)

            if act == "start":

                @pl.when(mine)
                def _():
                    pltpu.make_async_copy(msg_a.at[k, e], got_a.at[x], ra.at[x]).start()

            @pl.when(jnp.logical_not(mine))
            def _():
                copy = pltpu.make_async_remote_copy(
                    msg_a.at[k, e], got_a.at[x], sa.at[i, e], ra.at[x],
                    device_id=to_a[i][e], device_id_type=MESH,
                )
                copy.start() if act == "start" else copy.wait_send()

            copy = pltpu.make_async_remote_copy(
                msg_b.at[k, e], got_b.at[x], sb.at[i, e], rb.at[x],
                device_id=to_b[i][e], device_id_type=MESH,
            )
            copy.start() if act == "start" else copy.wait_send()

    scatter(0, "start")
    scatter(0, "wait")
    scatter(1, "start")

    own = tp[head * 2 + yh] // (REL_HEADS * 16) == whole_head(head, doc, yh)

    def remote(src, dst, send, recv, to):
        return pltpu.make_async_remote_copy(
            src, dst, send, recv, device_id=to, device_id_type=MESH
        )

    def place(i, zz, c):
        return out.at[order[i], zz, c]

    sends = []
    lane = lax.broadcasted_iota(jnp.int32, (ROWS // 2, 128), 1)
    beside = x + 1 - 2 * (x % 2)
    order = [x, 3 - x, beside, 3 - beside]
    for i, xs in enumerate(order):
        pltpu.make_async_copy(msg_a.at[0, 0], got_a.at[xs], ra.at[xs]).wait()
        pltpu.make_async_copy(msg_b.at[0, 0], got_b.at[xs], rb.at[xs]).wait()
        b = got_b[xs]
        b_roll = jnp.concatenate([b[:, W:], b[:, :W]], axis=1)
        keep = jnp.logical_or(own, lane >= W)
        chunk[i, 0 : ROWS // 2] = jnp.where(keep, got_a[xs, 0 : ROWS // 2], b)
        chunk[i, ROWS // 2 : ROWS] = jnp.where(keep, got_a[xs, ROWS // 2 : ROWS], b_roll)
        chunk[i, ROWS:PIECE] = got_a[xs, ROWS:PIECE]
        for copy in (
            remote(chunk.at[i], place(i, z, doc), s_up.at[i], r_dn.at[i], up),
            remote(chunk.at[i], place(i, z, doc), s_dn.at[i], r_up.at[i], down),
            remote(chunk.at[i], place(i, z, doc), s_core.at[i], r_core.at[i], core),
        ):
            copy.start()
            sends.append(copy)
        local = pltpu.make_async_copy(chunk.at[i], place(i, z, doc), s_own.at[i])
        local.start()
        sends.append(local)

    below, above, across = (z + 3) % 4, (z + 1) % 4, (z + 2) % 4

    def forward(src, send, recv, to):
        copy = remote(src, src, send, recv, to)
        copy.start()
        sends.append(copy)

    def arrived(ref, sem):
        pltpu.make_async_copy(ref, ref, sem).wait()

    for i in range(4):
        lo = place(i, below, doc)
        arrived(lo, r_dn.at[i])
        if i < 2:
            forward(lo, s_up.at[4 + i], r_dn.at[4 + i], up)
        forward(lo, s_core.at[4 + i], r_core.at[4 + i], core)
        hi = place(i, above, doc)
        arrived(hi, r_up.at[i])
        if i >= 2:
            forward(hi, s_dn.at[2 + i], r_up.at[2 + i], down)
        forward(hi, s_core.at[8 + i], r_core.at[8 + i], core)
    for i in range(4):
        far = place(i, across, doc)
        arrived(far, r_dn.at[4 + i] if i < 2 else r_up.at[2 + i])
        forward(far, s_core.at[12 + i], r_core.at[12 + i], core)
    for i in range(4):
        arrived(place(i, z, 1 - doc), r_core.at[i])
        arrived(place(i, below, 1 - doc), r_core.at[4 + i])
        arrived(place(i, above, 1 - doc), r_core.at[8 + i])
        arrived(place(i, across, 1 - doc), r_core.at[12 + i])
    for copy in sends:
        if hasattr(copy, "wait_send") and copy.is_remote:
            copy.wait_send()
        else:
            copy.wait()
    scatter(1, "wait")


def gather(tp, msg_a, msg_b):
    dma = pltpu.SemaphoreType.DMA
    vmem = pl.BlockSpec(memory_space=VMEM)
    return pl.pallas_call(
        gather_kernel,
        out_shape=jax.ShapeDtypeStruct((4, 4, 2, PIECE, 128), BF16),
        in_specs=[pl.BlockSpec(memory_space=pltpu.SMEM), vmem, vmem],
        out_specs=pl.BlockSpec(memory_space=ANY),
        scratch_shapes=[
            VMEM((4, PIECE, 128), BF16),
            VMEM((4, ROWS // 2, 128), BF16),
            VMEM((4, PIECE, 128), BF16),
            dma((2, 2)), dma((2, 2)), dma((4,)), dma((4,)),
            dma((4,)), dma((16,)), dma((6,)), dma((6,)), dma((16,)), dma((6,)), dma((6,)),
        ],
        compiler_params=params(collective_id=0, has_side_effects=True),
    )(tp, msg_a, msg_b)


def live_count(feats):
    total = jnp.zeros((16, 128), F32)
    for i in range(4):
        for zz in range(4):
            for c in range(2):
                total = total + feats[i, zz, c, ROWS:PIECE, :].astype(F32)
    return jnp.sum(total).astype(jnp.int32)


def block(feats, b):
    return feats[b // 8, (b // 2) % 4, b % 2, 0:ROWS, :]


def tile_scores(feats, b, count, rows):
    parts = [jnp.dot(block(feats, b + i), rows, preferred_element_type=F32) for i in range(count)]
    return jnp.concatenate(parts, axis=0)


def own_rows(feats, d, own):
    for m in range(16):
        b = 2 * m + d // 4
        part = feats[b // 8, (b // 2) % 4, b % 2, pl.ds(pl.multiple_of((d % 4) * 128, 128), 128), :]
        own[:, m * 128 : (m + 1) * 128] = part.T


def self_scores(feat):
    f = feat.astype(F32)
    return jnp.sum(f * f, axis=0, keepdims=True) * 0.125


def row_shift(own_score):
    room = 75.0 - (jnp.sqrt(own_score * TOP_BOUND) - own_score)
    k = jnp.floor(jnp.maximum(jnp.minimum(room, own_score), 0.0) * LOG2E)
    return own_score * LOG2E - k, k


def fill_rows(own, xi, yi, shifts):
    zero = jnp.zeros((W, OWN), BF16)
    xi[0:W, :] = own[0:W, :] * jnp.asarray(0.125, BF16)
    xi[W:, :] = zero
    yi[0:W, :] = zero
    yi[W:, :] = own[W:, :] * jnp.asarray(0.125, BF16)
    shifts[0:1, :] = row_shift(self_scores(own[0:W, :]))[0]
    shifts[1:2, :] = row_shift(self_scores(own[W:, :]))[0]


def own_live(n, d):
    lane = lax.broadcasted_iota(jnp.int32, (1, OWN), 1)
    token = ((lane // 128) * 8 + d) * 128 + lane % 128
    return token < n


def row_tiles(n, d, tile):
    blocks = jnp.clip((n - d * 128 + 1023) // 1024, 0, 16)
    need = jnp.maximum((blocks + 1) // 2, 4)
    for width in range(4, 9):

        @pl.when(need == width)
        def _():
            def half(i, _):
                tile(pl.multiple_of(i * width * 128, 128), width * 128)
                return 0

            lax.fori_loop(0, 2, half, 0)


def sums_kernel(feats, out, own, xi, yi, shifts, acc_t, acc_s):
    doc, _, _, z, _ = coords()
    d = doc * 4 + z
    n = live_count(feats)
    own_rows(feats, d, own)
    fill_rows(own, xi, yi, shifts)
    acc_t[...] = jnp.ones_like(acc_t)
    acc_s[...] = jnp.ones_like(acc_s)
    steps = (n + STEP - 1) // STEP

    def tile(start, width):
        at = pl.ds(start, width)

        def step(j, carry):
            b = j * (STEP // ROWS)
            t = jnp.exp2(tile_scores(feats, b, STEP // ROWS, xi[:, at]) * LOG2E - shifts[0:1, at])
            s = jnp.exp2(tile_scores(feats, b, STEP // ROWS, yi[:, at]) * LOG2E - shifts[1:2, at])
            add_t = jnp.sum(t.reshape(STEP // 8, 8, width), axis=0)
            add_s = jnp.sum(s.reshape(STEP // 8, 8, width), axis=0)
            return carry[0] + add_t, carry[1] + add_s

        zero = jnp.zeros((8, width), F32)
        t, s = lax.fori_loop(0, steps, step, (zero, zero))
        acc_t[:, at] = t
        acc_s[:, at] = s

    row_tiles(n, d, tile)
    live = own_live(n, d)
    st = self_scores(own[0:W, :])
    ss = self_scores(own[W:, :])
    dead = (steps * STEP - n).astype(F32)
    sum_t = jnp.sum(acc_t[...], axis=0, keepdims=True) - dead * jnp.exp2(-shifts[0:1, :])
    sum_s = jnp.sum(acc_s[...], axis=0, keepdims=True) - dead * jnp.exp2(-shifts[1:2, :])
    lt = shifts[0:1, :] * LN2 + jnp.log(sum_t)
    ls = shifts[1:2, :] * LN2 + jnp.log(sum_s)
    top = jnp.max(jnp.where(live, jnp.maximum(st, ss), 0.0))
    lt = jnp.where(live, lt, 0.0)
    ls = jnp.where(live, ls, 0.0)
    for m in range(16):
        out[m : m + 1, :] = lt[:, m * 128 : (m + 1) * 128]
        out[16 + m : 17 + m, :] = ls[:, m * 128 : (m + 1) * 128]
    at = lax.broadcasted_iota(jnp.int32, (8, 128), 0)
    out[32:40, :] = jnp.where(at == 0, top, jnp.where(at == 1, n.astype(F32), 0.0))


def sums(feats):
    return pl.pallas_call(
        sums_kernel,
        out_shape=jax.ShapeDtypeStruct((40, 128), F32),
        in_specs=[pl.BlockSpec(memory_space=VMEM)],
        out_specs=pl.BlockSpec(memory_space=VMEM),
        scratch_shapes=[
            VMEM((128, OWN), BF16),
            VMEM((128, OWN), BF16),
            VMEM((128, OWN), BF16),
            VMEM((8, OWN), F32),
            VMEM((8, OWN), F32),
            VMEM((8, OWN), F32),
        ],
        compiler_params=params(),
    )(feats)


def share_kernel(mine, out, flag, s_own, send, recv):
    doc, head, x, z, yh = coords()
    me = device(doc, head, x, z, yh)
    d = doc * 4 + z
    peers = []
    for step in range(1, 8):
        p = (d + step) % 8
        peers.append(device(p // 4, head, x, p % 4, yh))
    greet(peers, me)
    copies = []
    for step in range(1, 8):
        copy = pltpu.make_async_remote_copy(
            mine, out.at[d], send.at[step - 1], recv.at[step - 1],
            device_id=peers[step - 1], device_id_type=MESH,
        )
        copy.start()
        copies.append(copy)
    local = pltpu.make_async_copy(mine, out.at[d], s_own)
    local.start()
    for step in range(1, 8):
        p = (d + 8 - step) % 8
        pltpu.make_async_copy(mine, out.at[p], recv.at[step - 1]).wait()
    local.wait()
    flag[0] = (jnp.max(out[:, 32:33, :]) <= FAST_TOP).astype(jnp.int32)
    for copy in copies:
        copy.wait_send()


def share(mine):
    dma = pltpu.SemaphoreType.DMA
    vmem = pl.BlockSpec(memory_space=VMEM)
    return pl.pallas_call(
        share_kernel,
        out_shape=(jax.ShapeDtypeStruct((8, 40, 128), F32), jax.ShapeDtypeStruct((1,), jnp.int32)),
        in_specs=[vmem],
        out_specs=(vmem, pl.BlockSpec(memory_space=pltpu.SMEM)),
        scratch_shapes=[dma, dma((7,)), dma((7,))],
        compiler_params=params(collective_id=1, has_side_effects=True),
    )(mine)


def grads_kernel(feats, lse, grad, kl, own, xi, yi, shifts, v, ot, os_):
    doc, _, _, z, _ = coords()
    d = doc * 4 + z
    n = jnp.max(lse[0, 33:34, :]).astype(jnp.int32)
    own_rows(feats, d, own)
    fill_rows(own, xi, yi, shifts)
    steps = (n + STEP - 1) // STEP

    def weigh(b, _):
        f = block(feats, b).T
        x, y = f[:W, :], f[W:, :]
        yf = y.astype(F32)
        at = pl.ds(pl.multiple_of(b * ROWS, ROWS), ROWS)
        lt, ls = [], []
        for q in range(4):
            m = (b * 4 + q) // 8
            dd = (b * 4 + q) % 8
            lt.append(lse[dd, pl.ds(m, 1), :])
            ls.append(lse[dd, pl.ds(16 + m, 1), :])
        live = lax.broadcasted_iota(jnp.int32, (1, ROWS), 1) + b * ROWS < n
        wt = jnp.where(live, jnp.exp(SHIFT - jnp.concatenate(lt, axis=1)), 0.0)
        ws = jnp.where(live, jnp.exp(SHIFT - jnp.concatenate(ls, axis=1)), 0.0)
        keep = jnp.where(live, 1.0, 0.0).astype(BF16)
        v[0:W, at] = x * keep
        v[W : 2 * W, at] = (yf * wt).astype(BF16)
        v[2 * W : 3 * W, at] = y * keep
        v[3 * W :, at] = (yf * ws).astype(BF16)
        return 0

    lax.fori_loop(0, steps * (STEP // ROWS), weigh, 0)
    ot[...] = jnp.zeros_like(ot)
    os_[...] = jnp.zeros_like(os_)

    def tile(start, width):
        at = pl.ds(start, width)

        def step(j, _):
            js = pl.ds(pl.multiple_of(j * STEP, STEP), STEP)
            b = j * (STEP // ROWS)
            t = jnp.exp2(tile_scores(feats, b, STEP // ROWS, xi[:, at]) * LOG2E - shifts[0:1, at]).astype(BF16)
            s = jnp.exp2(tile_scores(feats, b, STEP // ROWS, yi[:, at]) * LOG2E - shifts[1:2, at]).astype(BF16)
            ot[:, at] += jnp.dot(v[0 : 3 * W, js], t, preferred_element_type=F32)
            os_[:, at] += jnp.dot(v[2 * W :, js], s, preferred_element_type=F32)
            return 0

        lax.fori_loop(0, steps, step, 0)

    row_tiles(n, d, tile)
    live = own_live(n, d)
    x = own[0:W, :].astype(F32)
    y = own[W:, :].astype(F32)
    mine = lse[d]
    lt = jnp.concatenate([mine[m : m + 1, :] for m in range(16)], axis=1)
    ls = jnp.concatenate([mine[16 + m : 17 + m, :] for m in range(16)], axis=1)

    def finish(by_row_sum, by_col_sum, feat, l):
        shift, k = row_shift(self_scores(feat))
        by_row = jnp.exp(shift * LN2 - l)
        by_col = jnp.exp((shift * LN2 - SHIFT) * 0.5)
        exact = y * jnp.exp(SHIFT - l)
        missing = (exact - exact.astype(BF16).astype(F32)) * jnp.exp2(k)
        return by_row_sum * by_row + (by_col_sum + missing) * by_col * by_col, by_row

    gs, _ = finish(os_[0:W, :], os_[W:, :], own[W:, :], ls)
    gt, by_row = finish(ot[2 * W :, :], ot[W : 2 * W, :], own[0:W, :], lt)
    grad[...] = jnp.where(live, (gs - gt) * 0.125, 0.0)
    moved = jnp.sum(x * ot[0:W, :] - y * ot[2 * W :, :], axis=0, keepdims=True)
    rows = jnp.where(live, moved * by_row * 0.125 - lt + ls, 0.0)
    acc = rows[:, 0:128]
    for m in range(1, 16):
        acc = acc + rows[:, m * 128 : (m + 1) * 128]
    at = lax.broadcasted_iota(jnp.int32, (8, 128), 0)
    kl[...] = jnp.where(at == 0, acc, jnp.where(at == 1, n.astype(F32), 0.0))


def grads(feats, lse):
    vmem = pl.BlockSpec(memory_space=VMEM)
    return pl.pallas_call(
        grads_kernel,
        out_shape=(jax.ShapeDtypeStruct((W, OWN), F32), jax.ShapeDtypeStruct((8, 128), F32)),
        in_specs=[vmem, vmem],
        out_specs=(vmem, vmem),
        scratch_shapes=[
            VMEM((128, OWN), BF16),
            VMEM((128, OWN), BF16),
            VMEM((128, OWN), BF16),
            VMEM((8, OWN), F32),
            VMEM((4 * W, LEN), BF16),
            VMEM((3 * W, OWN), F32),
            VMEM((2 * W, OWN), F32),
        ],
        compiler_params=params(),
    )(feats, lse)


def grads_wide(feats, lse):
    doc, _, _, z, _ = coords()
    d = doc * 4 + z
    n = lse[0, 33, 0].astype(jnp.int32)
    f = feats[:, :, :, :ROWS, :].reshape(LEN // 1024, 8, 128, 128)
    mine = lax.dynamic_index_in_dim(f, d, 1, keepdims=False).reshape(OWN, 128)
    cols = f.reshape(LEN // 1024, 1024, 128)
    col_lse = jnp.transpose(lse[:, :32].reshape(8, 2, 16, 128), (2, 1, 0, 3)).reshape(16, 2, 1024)
    own_lse = lax.dynamic_index_in_dim(lse, d, 0, keepdims=False)[:32].reshape(2, OWN)
    lt, ls = own_lse[0][:, None], own_lse[1][:, None]
    lane = jnp.arange(OWN)
    live = (((lane // 128) * 8 + d) * 128 + lane % 128 < n)[:, None]

    def step(j, carry):
        grad, kl = carry
        c = lax.dynamic_index_in_dim(cols, j, 0, keepdims=False)
        cl = lax.dynamic_index_in_dim(col_lse, j, 0, keepdims=False)
        both = live & (j * 1024 + jnp.arange(1024) < n)[None, :]
        t = jnp.dot(mine[:, :W], c[:, :W].T, preferred_element_type=F32) * 0.125
        s = jnp.dot(mine[:, W:], c[:, W:].T, preferred_element_type=F32) * 0.125
        pt = jnp.where(both, jnp.exp(t - lt), 0.0)
        rows = jnp.where(both, jnp.exp(s - ls), 0.0) - pt
        columns = jnp.where(both, jnp.exp(s - cl[1:2]) - jnp.exp(t - cl[0:1]), 0.0)
        w = (rows + columns).astype(BF16)
        grad = grad + jnp.dot(w, c[:, W:], preferred_element_type=F32) * 0.125
        return grad, kl + jnp.sum(pt * (t - s), axis=1, keepdims=True)

    zero = (jnp.zeros((OWN, W), F32), jnp.zeros((OWN, 1), F32))
    grad, kl = lax.fori_loop(0, 16, step, zero)
    rows = jnp.where(live, kl - lt + ls, 0.0).reshape(16, 128)
    tile = jnp.concatenate(
        [jnp.sum(rows, axis=0, keepdims=True), jnp.full((1, 128), n.astype(F32)), jnp.zeros((6, 128), F32)]
    )
    return grad.T, tile


def give_kernel(grad, kl, got, loss, got_kl, sums, got_sum, sg, rg, sk, rk, ss, rs):
    doc, head, x, z, yh = coords()
    me = device(doc, head, x, z, yh)
    to = [device(x // 2, head, m // 4, m % 4, doc) for m in range(16)]
    sources = [device(yh, head, 2 * doc + k, q, e) for k in range(2) for e in range(2) for q in range(4)]
    ring = [device(doc, 1 - head, x, z, yh), device(doc, head, x, z, 1 - yh), device(doc, 1 - head, x, z, 1 - yh)]
    greet(to + sources + ring, me)
    kind, part, q = x % 2, yh, z
    slot = (kind * 2 + part) * 4 + q
    where = pl.ds(pl.multiple_of(part * W, W), W)
    def send(m, src, dst, send_sem, recv_sem):
        mine = same(to[m], me)

        @pl.when(mine)
        def _():
            pltpu.make_async_copy(src, dst, recv_sem).start()

        @pl.when(jnp.logical_not(mine))
        def _():
            pltpu.make_async_remote_copy(
                src, dst, send_sem, recv_sem, device_id=to[m], device_id_type=MESH
            ).start()

    for m in range(16):
        send(m, kl, got_kl.at[slot], sk.at[m], rk.at[slot])
    for m in range(16):
        send(m, grad.at[:, m * 128 : (m + 1) * 128], got.at[kind, q, where], sg.at[m], rg.at[slot])

    total = jnp.zeros((8, 128), F32)
    for i in range(16):
        pltpu.make_async_copy(kl, got_kl.at[i], rk.at[i]).wait()
        total = total + got_kl[i]
    sums[...] = total
    swaps = []
    for i in range(3):
        copy = pltpu.make_async_remote_copy(
            sums, got_sum.at[i], ss.at[i], rs.at[i], device_id=ring[i], device_id_type=MESH
        )
        copy.start()
        swaps.append(copy)
    for i in range(3):
        swaps[i].wait_recv()
        total = total + got_sum[i]
    for i in range(3):
        swaps[i].wait_send()
    kl_sum = jnp.sum(total[0:1, :], axis=1, keepdims=True)
    count = total[1:2, 0:1] * (1.0 / 64.0)
    loss[...] = jnp.broadcast_to(kl_sum / (count * (2.0 * REL_HEADS)), (8, 128))
    for k in range(2):
        for q_ in range(4):
            for e in range(2):
                part_ref = got.at[k, q_, pl.ds(e * W, W)]
                pltpu.make_async_copy(part_ref, part_ref, rg.at[(k * 2 + e) * 4 + q_]).wait()
    for m in range(16):
        src = grad.at[:, m * 128 : (m + 1) * 128]

        @pl.when(jnp.logical_not(same(to[m], me)))
        def _():
            pltpu.make_async_remote_copy(
                src, got.at[kind, q, where], sg.at[m], rg.at[slot], device_id=to[m], device_id_type=MESH
            ).wait_send()
            pltpu.make_async_remote_copy(
                kl, got_kl.at[slot], sk.at[m], rk.at[slot], device_id=to[m], device_id_type=MESH
            ).wait_send()


def give(grad, kl):
    dma = pltpu.SemaphoreType.DMA
    vmem = pl.BlockSpec(memory_space=VMEM)
    return pl.pallas_call(
        give_kernel,
        out_shape=(jax.ShapeDtypeStruct((2, 4, 128, 128), F32), jax.ShapeDtypeStruct((8, 128), F32)),
        in_specs=[vmem, vmem],
        out_specs=(vmem, vmem),
        scratch_shapes=[
            VMEM((16, 8, 128), F32),
            VMEM((8, 128), F32),
            VMEM((3, 8, 128), F32),
            dma((16,)), dma((16,)), dma((16,)), dma((16,)), dma((3,)), dma((3,)),
        ],
        compiler_params=params(collective_id=2, has_side_effects=True),
    )(grad, kl)


def turn_kernel(got, tile, gq, gv, loss):
    for k, out in ((0, gq), (1, gv)):
        for q in range(4):
            out[0, q * 128 : (q + 1) * 128, :] = got[k, q].T
    loss[0] = jnp.max(tile[...])


def turn(got, tile):
    vmem = pl.BlockSpec(memory_space=VMEM)
    out = jax.ShapeDtypeStruct((1, ROWS, 128), F32)
    return pl.pallas_call(
        turn_kernel,
        out_shape=(out, out, jax.ShapeDtypeStruct((1,), F32)),
        in_specs=[vmem, vmem],
        out_specs=(vmem, vmem, pl.BlockSpec(memory_space=pltpu.SMEM)),
        compiler_params=params(),
    )(got, tile)


def shards(token_ids, teacher_query, teacher_value, student_query, student_value, teacher_pick, student_pick):
    msg_a, msg_b = pick(
        teacher_pick, student_pick, token_ids.reshape(4, 128),
        teacher_query[0], teacher_value[0], student_query[0], student_value[0],
    )
    feats = gather(teacher_pick, msg_a, msg_b)
    lse, fast = share(sums(feats))
    grad, kl = lax.cond(fast[0] > 0, grads, grads_wide, feats, lse)
    return turn(*give(grad, kl))


def solution(mesh):
    return jax.shard_map(
        shards,
        mesh=mesh,
        in_specs=(
            P("doc", "seq"),
            P("doc", "seq", "head"),
            P("doc", "seq", "head"),
            P("doc", "seq", None),
            P("doc", "seq", None),
            P(),
            P(),
        ),
        out_specs=(P("doc", "seq", "head"), P("doc", "seq", "head"), P("doc")),
        check_vma=False,
    )
```

```python
import functools

import jax
import jax.numpy as jnp
from jax import lax
from jax.experimental import pallas as pl
from jax.experimental.pallas import tpu as pltpu
from jax.sharding import PartitionSpec as P

HEAD_DIM = 128
W = 64
PER_HEAD = HEAD_DIM // W
T_GROUP = 8
S_GROUP = 7
REL_HEADS = 4
LEN = 16384
ROWS = 512
PIECE = ROWS + 16
OWN = 2048
TOP_BOUND = 162.0
LN2 = 0.6931471805599453
LOG2E = 1.4426950408889634
SHIFT = 74.0
FAST_TOP = 130.0
STEP = 2048
F32 = jnp.float32
BF16 = jnp.bfloat16
MESH = pl.DeviceIdType.MESH
VMEM = pltpu.VMEM
ANY = pl.ANY


def coords():
    doc = lax.axis_index("doc")
    head = lax.axis_index("head")
    seq = lax.axis_index("seq")
    return doc, head, seq // 8, (seq // 2) % 4, seq % 2


def device(doc, head, x, z, yh):
    return (doc, head, (x * 4 + z) * 2 + yh)


def same(a, b):
    return (a[0] == b[0]) & (a[1] == b[1]) & (a[2] == b[2])


def params(**kw):
    return pltpu.CompilerParams(vmem_limit_bytes=56 * 2**20, **kw)


def pick_kernel(tp, sp, ids, tq, tv, sq, sv, msg_a, msg_b, tw, sw, sem):
    head = lax.axis_index("head")
    copies = []

    def fetch(src, block, dst):
        start = pl.multiple_of((block // 2) * 128, 128)
        copy = pltpu.make_async_copy(src.at[:, pl.ds(start, 128)], dst, sem.at[len(copies)])
        copy.start()
        copies.append(copy)

    q_blocks = tq.shape[1] // W
    v_blocks = tv.shape[1] // W
    for r in range(REL_HEADS):
        b = tp[r]
        vb = (b // PER_HEAD) // T_GROUP * PER_HEAD + b % PER_HEAD
        fetch(tq, b % q_blocks, tw.at[0, r])
        fetch(tv, vb % v_blocks, tw.at[1, r])
    for e in range(2):
        b = sp[head * 2 + e]
        vb = (b // PER_HEAD) // S_GROUP * PER_HEAD + b % PER_HEAD
        fetch(sq, b, sw.at[0, e])
        fetch(sv, vb, sw.at[1, e])
    for copy in copies:
        copy.wait()

    def half(w, b):
        return jnp.where(b % 2 == 0, w[:, :W], w[:, W:])

    live = (ids[...] != 0).astype(F32)
    tail = jnp.concatenate([live, jnp.zeros((12, 128), F32)], axis=0).astype(BF16)
    upright = jnp.concatenate([live, jnp.zeros((4, 128), F32)], axis=0).T
    keep = jnp.concatenate([jnp.broadcast_to(upright[:, i : i + 1], (128, W)) for i in range(4)], axis=0)
    keep = keep.astype(BF16)
    for k in range(2):
        for e in range(2):
            r = head * 2 + e
            t = half(tw[k, r], tp[r]) * keep
            s = half(sw[k, e], sp[r]) * keep
            msg_a[k, e, 0:ROWS, :] = jnp.concatenate([t, s], axis=1)
            msg_a[k, e, ROWS:PIECE, :] = tail
            r = (1 - head) * 2 + e
            t = half(tw[k, r], tp[r]) * keep
            msg_b[k, e] = jnp.concatenate([t[: ROWS // 2], t[ROWS // 2 :]], axis=1)


def pick(tp, sp, ids, tq, tv, sq, sv):
    smem = pl.BlockSpec(memory_space=pltpu.SMEM)
    vmem = pl.BlockSpec(memory_space=VMEM)
    hbm = pl.BlockSpec(memory_space=ANY)
    return pl.pallas_call(
        pick_kernel,
        out_shape=(
            jax.ShapeDtypeStruct((2, 2, PIECE, 128), BF16),
            jax.ShapeDtypeStruct((2, 2, ROWS // 2, 128), BF16),
        ),
        in_specs=[smem, smem, vmem, hbm, hbm, hbm, hbm],
        out_specs=(vmem, vmem),
        scratch_shapes=[
            VMEM((2, 4, ROWS, 128), BF16),
            VMEM((2, 2, ROWS, 128), BF16),
            pltpu.SemaphoreType.DMA((12,)),
        ],
        compiler_params=params(),
    )(tp, sp, ids, tq, tv, sq, sv)


def greet(peers, me):
    barrier = pltpu.get_barrier_semaphore()
    count = 0
    for peer in peers:
        other = jnp.logical_not(same(peer, me))

        @pl.when(other)
        def _():
            pl.semaphore_signal(barrier, inc=1, device_id=peer, device_id_type=MESH)

        count = count + other.astype(jnp.int32)
    pl.semaphore_wait(barrier, count)


def gather_kernel(
    tp, msg_a, msg_b, out, got_a, got_b, chunk,
    sa, sb, ra, rb, s_own, s_core, s_up, s_dn, r_core, r_up, r_dn,
):
    doc, head, x, z, yh = coords()
    me = device(doc, head, x, z, yh)
    core = device(1 - doc, head, x, z, yh)
    up = device(doc, head, x, (z + 1) % 4, yh)
    down = device(doc, head, x, (z + 3) % 4, yh)
    kinds = [((x == 2 * doc + 1) | (x == (2 * doc + 2) % 4)).astype(jnp.int32)]
    kinds.append(1 - kinds[0])
    to_a = [[device(yh, head, 2 * doc + k, z, e) for e in range(2)] for k in kinds]
    to_b = [[device(yh, 1 - head, 2 * doc + k, z, e) for e in range(2)] for k in kinds]
    from_doc = x // 2
    sources = [device(from_doc, h, xs, z, doc) for h in range(2) for xs in range(4)]
    greet(to_a[0] + to_a[1] + to_b[0] + to_b[1] + sources + [core, up, down], me)

    def scatter(i, act):
        k = kinds[i]
        for e in range(2):
            mine = same(to_a[i][e], me)

            if act == "start":

                @pl.when(mine)
                def _():
                    pltpu.make_async_copy(msg_a.at[k, e], got_a.at[x], ra.at[x]).start()

            @pl.when(jnp.logical_not(mine))
            def _():
                copy = pltpu.make_async_remote_copy(
                    msg_a.at[k, e], got_a.at[x], sa.at[i, e], ra.at[x],
                    device_id=to_a[i][e], device_id_type=MESH,
                )
                copy.start() if act == "start" else copy.wait_send()

            copy = pltpu.make_async_remote_copy(
                msg_b.at[k, e], got_b.at[x], sb.at[i, e], rb.at[x],
                device_id=to_b[i][e], device_id_type=MESH,
            )
            copy.start() if act == "start" else copy.wait_send()

    scatter(0, "start")
    scatter(0, "wait")
    scatter(1, "start")

    own = tp[head * 2 + yh] // (REL_HEADS * 16) == head

    def remote(src, dst, send, recv, to):
        return pltpu.make_async_remote_copy(
            src, dst, send, recv, device_id=to, device_id_type=MESH
        )

    def place(i, zz, c):
        return out.at[order[i], zz, c]

    sends = []
    lane = lax.broadcasted_iota(jnp.int32, (ROWS // 2, 128), 1)
    beside = x + 1 - 2 * (x % 2)
    order = [x, 3 - x, beside, 3 - beside]
    for i, xs in enumerate(order):
        pltpu.make_async_copy(msg_a.at[0, 0], got_a.at[xs], ra.at[xs]).wait()
        pltpu.make_async_copy(msg_b.at[0, 0], got_b.at[xs], rb.at[xs]).wait()
        b = got_b[xs]
        b_roll = jnp.concatenate([b[:, W:], b[:, :W]], axis=1)
        keep = jnp.logical_or(own, lane >= W)
        chunk[i, 0 : ROWS // 2] = jnp.where(keep, got_a[xs, 0 : ROWS // 2], b)
        chunk[i, ROWS // 2 : ROWS] = jnp.where(keep, got_a[xs, ROWS // 2 : ROWS], b_roll)
        chunk[i, ROWS:PIECE] = got_a[xs, ROWS:PIECE]
        for copy in (
            remote(chunk.at[i], place(i, z, doc), s_up.at[i], r_dn.at[i], up),
            remote(chunk.at[i], place(i, z, doc), s_dn.at[i], r_up.at[i], down),
            remote(chunk.at[i], place(i, z, doc), s_core.at[i], r_core.at[i], core),
        ):
            copy.start()
            sends.append(copy)
        local = pltpu.make_async_copy(chunk.at[i], place(i, z, doc), s_own.at[i])
        local.start()
        sends.append(local)

    below, above, across = (z + 3) % 4, (z + 1) % 4, (z + 2) % 4

    def forward(src, send, recv, to):
        copy = remote(src, src, send, recv, to)
        copy.start()
        sends.append(copy)

    def arrived(ref, sem):
        pltpu.make_async_copy(ref, ref, sem).wait()

    for i in range(4):
        lo = place(i, below, doc)
        arrived(lo, r_dn.at[i])
        if i % 2 == 0:
            forward(lo, s_up.at[4 + i // 2], r_dn.at[4 + i // 2], up)
        forward(lo, s_core.at[4 + i], r_core.at[4 + i], core)
        hi = place(i, above, doc)
        arrived(hi, r_up.at[i])
        if i % 2 == 1:
            forward(hi, s_dn.at[4 + i // 2], r_up.at[4 + i // 2], down)
        forward(hi, s_core.at[8 + i], r_core.at[8 + i], core)
    for i in range(4):
        far = place(i, across, doc)
        arrived(far, r_dn.at[4 + i // 2] if i % 2 == 0 else r_up.at[4 + i // 2])
        forward(far, s_core.at[12 + i], r_core.at[12 + i], core)
    for i in range(4):
        arrived(place(i, z, 1 - doc), r_core.at[i])
        arrived(place(i, below, 1 - doc), r_core.at[4 + i])
        arrived(place(i, above, 1 - doc), r_core.at[8 + i])
        arrived(place(i, across, 1 - doc), r_core.at[12 + i])
    for copy in sends:
        if hasattr(copy, "wait_send") and copy.is_remote:
            copy.wait_send()
        else:
            copy.wait()
    scatter(1, "wait")


def gather(tp, msg_a, msg_b):
    dma = pltpu.SemaphoreType.DMA
    vmem = pl.BlockSpec(memory_space=VMEM)
    return pl.pallas_call(
        gather_kernel,
        out_shape=jax.ShapeDtypeStruct((4, 4, 2, PIECE, 128), BF16),
        in_specs=[pl.BlockSpec(memory_space=pltpu.SMEM), vmem, vmem],
        out_specs=pl.BlockSpec(memory_space=ANY),
        scratch_shapes=[
            VMEM((4, PIECE, 128), BF16),
            VMEM((4, ROWS // 2, 128), BF16),
            VMEM((4, PIECE, 128), BF16),
            dma((2, 2)), dma((2, 2)), dma((4,)), dma((4,)),
            dma((4,)), dma((16,)), dma((6,)), dma((6,)), dma((16,)), dma((6,)), dma((6,)),
        ],
        compiler_params=params(collective_id=0, has_side_effects=True),
    )(tp, msg_a, msg_b)


def live_count(feats):
    total = jnp.zeros((16, 128), F32)
    for i in range(4):
        for zz in range(4):
            for c in range(2):
                total = total + feats[i, zz, c, ROWS:PIECE, :].astype(F32)
    return jnp.sum(total).astype(jnp.int32)


def block(feats, b):
    return feats[b // 8, (b // 2) % 4, b % 2, 0:ROWS, :]


def tile_scores(feats, b, count, rows):
    parts = [jnp.dot(block(feats, b + i), rows, preferred_element_type=F32) for i in range(count)]
    return jnp.concatenate(parts, axis=0)


def own_rows(feats, d, own):
    for m in range(16):
        b = 2 * m + d // 4
        part = feats[b // 8, (b // 2) % 4, b % 2, pl.ds(pl.multiple_of((d % 4) * 128, 128), 128), :]
        own[:, m * 128 : (m + 1) * 128] = part.T


def self_scores(feat):
    f = feat.astype(F32)
    return jnp.sum(f * f, axis=0, keepdims=True) * 0.125


def row_shift(own_score):
    room = 75.0 - (jnp.sqrt(own_score * TOP_BOUND) - own_score)
    k = jnp.floor(jnp.maximum(jnp.minimum(room, own_score), 0.0) * LOG2E)
    return own_score * LOG2E - k, k


def fill_rows(own, xi, yi, shifts):
    zero = jnp.zeros((W, OWN), BF16)
    xi[0:W, :] = own[0:W, :] * jnp.asarray(0.125, BF16)
    xi[W:, :] = zero
    yi[0:W, :] = zero
    yi[W:, :] = own[W:, :] * jnp.asarray(0.125, BF16)
    shifts[0:1, :] = row_shift(self_scores(own[0:W, :]))[0]
    shifts[1:2, :] = row_shift(self_scores(own[W:, :]))[0]


def own_live(n, d):
    lane = lax.broadcasted_iota(jnp.int32, (1, OWN), 1)
    token = ((lane // 128) * 8 + d) * 128 + lane % 128
    return token < n


def row_tiles(n, d, tile):
    blocks = jnp.clip((n - d * 128 + 1023) // 1024, 0, 16)
    need = jnp.maximum((blocks + 1) // 2, 4)
    for width in range(4, 9):

        @pl.when(need == width)
        def _():
            def half(i, _):
                tile(pl.multiple_of(i * width * 128, 128), width * 128)
                return 0

            lax.fori_loop(0, 2, half, 0)


def sums_kernel(feats, out, own, xi, yi, shifts, acc_t, acc_s):
    doc, _, _, z, _ = coords()
    d = doc * 4 + z
    n = live_count(feats)
    own_rows(feats, d, own)
    fill_rows(own, xi, yi, shifts)
    acc_t[...] = jnp.ones_like(acc_t)
    acc_s[...] = jnp.ones_like(acc_s)
    steps = (n + STEP - 1) // STEP

    def tile(start, width):
        at = pl.ds(start, width)

        def step(j, carry):
            b = j * (STEP // ROWS)
            t = jnp.exp2(tile_scores(feats, b, STEP // ROWS, xi[:, at]) * LOG2E - shifts[0:1, at])
            s = jnp.exp2(tile_scores(feats, b, STEP // ROWS, yi[:, at]) * LOG2E - shifts[1:2, at])
            add_t = jnp.sum(t.reshape(STEP // 8, 8, width), axis=0)
            add_s = jnp.sum(s.reshape(STEP // 8, 8, width), axis=0)
            return carry[0] + add_t, carry[1] + add_s

        zero = jnp.zeros((8, width), F32)
        t, s = lax.fori_loop(0, steps, step, (zero, zero))
        acc_t[:, at] = t
        acc_s[:, at] = s

    row_tiles(n, d, tile)
    live = own_live(n, d)
    st = self_scores(own[0:W, :])
    ss = self_scores(own[W:, :])
    dead = (steps * STEP - n).astype(F32)
    sum_t = jnp.sum(acc_t[...], axis=0, keepdims=True) - dead * jnp.exp2(-shifts[0:1, :])
    sum_s = jnp.sum(acc_s[...], axis=0, keepdims=True) - dead * jnp.exp2(-shifts[1:2, :])
    lt = shifts[0:1, :] * LN2 + jnp.log(sum_t)
    ls = shifts[1:2, :] * LN2 + jnp.log(sum_s)
    top = jnp.max(jnp.where(live, jnp.maximum(st, ss), 0.0))
    lt = jnp.where(live, lt, 0.0)
    ls = jnp.where(live, ls, 0.0)
    for m in range(16):
        out[m : m + 1, :] = lt[:, m * 128 : (m + 1) * 128]
        out[16 + m : 17 + m, :] = ls[:, m * 128 : (m + 1) * 128]
    at = lax.broadcasted_iota(jnp.int32, (8, 128), 0)
    out[32:40, :] = jnp.where(at == 0, top, jnp.where(at == 1, n.astype(F32), 0.0))


def sums(feats):
    return pl.pallas_call(
        sums_kernel,
        out_shape=jax.ShapeDtypeStruct((40, 128), F32),
        in_specs=[pl.BlockSpec(memory_space=VMEM)],
        out_specs=pl.BlockSpec(memory_space=VMEM),
        scratch_shapes=[
            VMEM((128, OWN), BF16),
            VMEM((128, OWN), BF16),
            VMEM((128, OWN), BF16),
            VMEM((8, OWN), F32),
            VMEM((8, OWN), F32),
            VMEM((8, OWN), F32),
        ],
        compiler_params=params(),
    )(feats)


def share_kernel(mine, out, flag, s_own, send, recv):
    doc, head, x, z, yh = coords()
    me = device(doc, head, x, z, yh)
    d = doc * 4 + z
    peers = []
    for step in range(1, 8):
        p = (d + step) % 8
        peers.append(device(p // 4, head, x, p % 4, yh))
    greet(peers, me)
    copies = []
    for step in range(1, 8):
        copy = pltpu.make_async_remote_copy(
            mine, out.at[d], send.at[step - 1], recv.at[step - 1],
            device_id=peers[step - 1], device_id_type=MESH,
        )
        copy.start()
        copies.append(copy)
    local = pltpu.make_async_copy(mine, out.at[d], s_own)
    local.start()
    for step in range(1, 8):
        p = (d + 8 - step) % 8
        pltpu.make_async_copy(mine, out.at[p], recv.at[step - 1]).wait()
    local.wait()
    flag[0] = (jnp.max(out[:, 32:33, :]) <= FAST_TOP).astype(jnp.int32)
    for copy in copies:
        copy.wait_send()


def share(mine):
    dma = pltpu.SemaphoreType.DMA
    vmem = pl.BlockSpec(memory_space=VMEM)
    return pl.pallas_call(
        share_kernel,
        out_shape=(jax.ShapeDtypeStruct((8, 40, 128), F32), jax.ShapeDtypeStruct((1,), jnp.int32)),
        in_specs=[vmem],
        out_specs=(vmem, pl.BlockSpec(memory_space=pltpu.SMEM)),
        scratch_shapes=[dma, dma((7,)), dma((7,))],
        compiler_params=params(collective_id=1, has_side_effects=True),
    )(mine)


def grads_kernel(feats, lse, grad, kl, own, xi, yi, shifts, v, ot, os_):
    doc, _, _, z, _ = coords()
    d = doc * 4 + z
    n = jnp.max(lse[0, 33:34, :]).astype(jnp.int32)
    own_rows(feats, d, own)
    fill_rows(own, xi, yi, shifts)
    steps = (n + STEP - 1) // STEP

    def weigh(b, _):
        f = block(feats, b).T
        x, y = f[:W, :], f[W:, :]
        yf = y.astype(F32)
        at = pl.ds(pl.multiple_of(b * ROWS, ROWS), ROWS)
        lt, ls = [], []
        for q in range(4):
            m = (b * 4 + q) // 8
            dd = (b * 4 + q) % 8
            lt.append(lse[dd, pl.ds(m, 1), :])
            ls.append(lse[dd, pl.ds(16 + m, 1), :])
        live = lax.broadcasted_iota(jnp.int32, (1, ROWS), 1) + b * ROWS < n
        wt = jnp.where(live, jnp.exp(SHIFT - jnp.concatenate(lt, axis=1)), 0.0)
        ws = jnp.where(live, jnp.exp(SHIFT - jnp.concatenate(ls, axis=1)), 0.0)
        keep = jnp.where(live, 1.0, 0.0).astype(BF16)
        v[0:W, at] = x * keep
        v[W : 2 * W, at] = (yf * wt).astype(BF16)
        v[2 * W : 3 * W, at] = y * keep
        v[3 * W :, at] = (yf * ws).astype(BF16)
        return 0

    lax.fori_loop(0, steps * (STEP // ROWS), weigh, 0)
    ot[...] = jnp.zeros_like(ot)
    os_[...] = jnp.zeros_like(os_)

    def tile(start, width):
        at = pl.ds(start, width)

        def step(j, _):
            js = pl.ds(pl.multiple_of(j * STEP, STEP), STEP)
            b = j * (STEP // ROWS)
            t = jnp.exp2(tile_scores(feats, b, STEP // ROWS, xi[:, at]) * LOG2E - shifts[0:1, at]).astype(BF16)
            s = jnp.exp2(tile_scores(feats, b, STEP // ROWS, yi[:, at]) * LOG2E - shifts[1:2, at]).astype(BF16)
            ot[:, at] += jnp.dot(v[0 : 3 * W, js], t, preferred_element_type=F32)
            os_[:, at] += jnp.dot(v[2 * W :, js], s, preferred_element_type=F32)
            return 0

        lax.fori_loop(0, steps, step, 0)

    row_tiles(n, d, tile)
    live = own_live(n, d)
    x = own[0:W, :].astype(F32)
    y = own[W:, :].astype(F32)
    mine = lse[d]
    lt = jnp.concatenate([mine[m : m + 1, :] for m in range(16)], axis=1)
    ls = jnp.concatenate([mine[16 + m : 17 + m, :] for m in range(16)], axis=1)

    def finish(by_row_sum, by_col_sum, feat, l):
        shift, k = row_shift(self_scores(feat))
        by_row = jnp.exp(shift * LN2 - l)
        by_col = jnp.exp((shift * LN2 - SHIFT) * 0.5)
        exact = y * jnp.exp(SHIFT - l)
        missing = (exact - exact.astype(BF16).astype(F32)) * jnp.exp2(k)
        return by_row_sum * by_row + (by_col_sum + missing) * by_col * by_col, by_row

    gs, _ = finish(os_[0:W, :], os_[W:, :], own[W:, :], ls)
    gt, by_row = finish(ot[2 * W :, :], ot[W : 2 * W, :], own[0:W, :], lt)
    grad[...] = jnp.where(live, (gs - gt) * 0.125, 0.0)
    moved = jnp.sum(x * ot[0:W, :] - y * ot[2 * W :, :], axis=0, keepdims=True)
    rows = jnp.where(live, moved * by_row * 0.125 - lt + ls, 0.0)
    acc = rows[:, 0:128]
    for m in range(1, 16):
        acc = acc + rows[:, m * 128 : (m + 1) * 128]
    at = lax.broadcasted_iota(jnp.int32, (8, 128), 0)
    kl[...] = jnp.where(at == 0, acc, jnp.where(at == 1, n.astype(F32), 0.0))


def grads(feats, lse):
    vmem = pl.BlockSpec(memory_space=VMEM)
    return pl.pallas_call(
        grads_kernel,
        out_shape=(jax.ShapeDtypeStruct((W, OWN), F32), jax.ShapeDtypeStruct((8, 128), F32)),
        in_specs=[vmem, vmem],
        out_specs=(vmem, vmem),
        scratch_shapes=[
            VMEM((128, OWN), BF16),
            VMEM((128, OWN), BF16),
            VMEM((128, OWN), BF16),
            VMEM((8, OWN), F32),
            VMEM((4 * W, LEN), BF16),
            VMEM((3 * W, OWN), F32),
            VMEM((2 * W, OWN), F32),
        ],
        compiler_params=params(),
    )(feats, lse)


def grads_wide(feats, lse):
    doc, _, _, z, _ = coords()
    d = doc * 4 + z
    n = lse[0, 33, 0].astype(jnp.int32)
    f = feats[:, :, :, :ROWS, :].reshape(LEN // 1024, 8, 128, 128)
    mine = lax.dynamic_index_in_dim(f, d, 1, keepdims=False).reshape(OWN, 128)
    cols = f.reshape(LEN // 1024, 1024, 128)
    col_lse = jnp.transpose(lse[:, :32].reshape(8, 2, 16, 128), (2, 1, 0, 3)).reshape(16, 2, 1024)
    own_lse = lax.dynamic_index_in_dim(lse, d, 0, keepdims=False)[:32].reshape(2, OWN)
    lt, ls = own_lse[0][:, None], own_lse[1][:, None]
    lane = jnp.arange(OWN)
    live = (((lane // 128) * 8 + d) * 128 + lane % 128 < n)[:, None]

    def step(j, carry):
        grad, kl = carry
        c = lax.dynamic_index_in_dim(cols, j, 0, keepdims=False)
        cl = lax.dynamic_index_in_dim(col_lse, j, 0, keepdims=False)
        both = live & (j * 1024 + jnp.arange(1024) < n)[None, :]
        t = jnp.dot(mine[:, :W], c[:, :W].T, preferred_element_type=F32) * 0.125
        s = jnp.dot(mine[:, W:], c[:, W:].T, preferred_element_type=F32) * 0.125
        pt = jnp.where(both, jnp.exp(t - lt), 0.0)
        rows = jnp.where(both, jnp.exp(s - ls), 0.0) - pt
        columns = jnp.where(both, jnp.exp(s - cl[1:2]) - jnp.exp(t - cl[0:1]), 0.0)
        w = (rows + columns).astype(BF16)
        grad = grad + jnp.dot(w, c[:, W:], preferred_element_type=F32) * 0.125
        return grad, kl + jnp.sum(pt * (t - s), axis=1, keepdims=True)

    zero = (jnp.zeros((OWN, W), F32), jnp.zeros((OWN, 1), F32))
    grad, kl = lax.fori_loop(0, 16, step, zero)
    rows = jnp.where(live, kl - lt + ls, 0.0).reshape(16, 128)
    tile = jnp.concatenate(
        [jnp.sum(rows, axis=0, keepdims=True), jnp.full((1, 128), n.astype(F32)), jnp.zeros((6, 128), F32)]
    )
    return grad.T, tile


def give_kernel(grad, kl, got, loss, got_kl, sums, got_sum, sg, rg, sk, rk, ss, rs):
    doc, head, x, z, yh = coords()
    me = device(doc, head, x, z, yh)
    to = [device(x // 2, head, m // 4, m % 4, doc) for m in range(16)]
    sources = [device(yh, head, 2 * doc + k, q, e) for k in range(2) for e in range(2) for q in range(4)]
    ring = [device(doc, 1 - head, x, z, yh), device(doc, head, x, z, 1 - yh), device(doc, 1 - head, x, z, 1 - yh)]
    greet(to + sources + ring, me)
    kind, part, q = x % 2, yh, z
    slot = (kind * 2 + part) * 4 + q
    where = pl.ds(pl.multiple_of(part * W, W), W)
    def send(m, src, dst, send_sem, recv_sem):
        mine = same(to[m], me)

        @pl.when(mine)
        def _():
            pltpu.make_async_copy(src, dst, recv_sem).start()

        @pl.when(jnp.logical_not(mine))
        def _():
            pltpu.make_async_remote_copy(
                src, dst, send_sem, recv_sem, device_id=to[m], device_id_type=MESH
            ).start()

    for m in range(16):
        send(m, kl, got_kl.at[slot], sk.at[m], rk.at[slot])
    for m in range(16):
        send(m, grad.at[:, m * 128 : (m + 1) * 128], got.at[kind, q, where], sg.at[m], rg.at[slot])

    total = jnp.zeros((8, 128), F32)
    for i in range(16):
        pltpu.make_async_copy(kl, got_kl.at[i], rk.at[i]).wait()
        total = total + got_kl[i]
    sums[...] = total
    swaps = []
    for i in range(3):
        copy = pltpu.make_async_remote_copy(
            sums, got_sum.at[i], ss.at[i], rs.at[i], device_id=ring[i], device_id_type=MESH
        )
        copy.start()
        swaps.append(copy)
    for i in range(3):
        swaps[i].wait_recv()
        total = total + got_sum[i]
    for i in range(3):
        swaps[i].wait_send()
    kl_sum = jnp.sum(total[0:1, :], axis=1, keepdims=True)
    count = total[1:2, 0:1] * (1.0 / 64.0)
    loss[...] = jnp.broadcast_to(kl_sum / (count * (2.0 * REL_HEADS)), (8, 128))
    for k in range(2):
        for q_ in range(4):
            for e in range(2):
                part_ref = got.at[k, q_, pl.ds(e * W, W)]
                pltpu.make_async_copy(part_ref, part_ref, rg.at[(k * 2 + e) * 4 + q_]).wait()
    for m in range(16):
        src = grad.at[:, m * 128 : (m + 1) * 128]

        @pl.when(jnp.logical_not(same(to[m], me)))
        def _():
            pltpu.make_async_remote_copy(
                src, got.at[kind, q, where], sg.at[m], rg.at[slot], device_id=to[m], device_id_type=MESH
            ).wait_send()
            pltpu.make_async_remote_copy(
                kl, got_kl.at[slot], sk.at[m], rk.at[slot], device_id=to[m], device_id_type=MESH
            ).wait_send()


def give(grad, kl):
    dma = pltpu.SemaphoreType.DMA
    vmem = pl.BlockSpec(memory_space=VMEM)
    return pl.pallas_call(
        give_kernel,
        out_shape=(jax.ShapeDtypeStruct((2, 4, 128, 128), F32), jax.ShapeDtypeStruct((8, 128), F32)),
        in_specs=[vmem, vmem],
        out_specs=(vmem, vmem),
        scratch_shapes=[
            VMEM((16, 8, 128), F32),
            VMEM((8, 128), F32),
            VMEM((3, 8, 128), F32),
            dma((16,)), dma((16,)), dma((16,)), dma((16,)), dma((3,)), dma((3,)),
        ],
        compiler_params=params(collective_id=2, has_side_effects=True),
    )(grad, kl)


def turn_kernel(got, tile, gq, gv, loss):
    for k, out in ((0, gq), (1, gv)):
        for q in range(4):
            out[0, q * 128 : (q + 1) * 128, :] = got[k, q].T
    loss[0] = jnp.max(tile[...])


def turn(got, tile):
    vmem = pl.BlockSpec(memory_space=VMEM)
    out = jax.ShapeDtypeStruct((1, ROWS, 128), F32)
    return pl.pallas_call(
        turn_kernel,
        out_shape=(out, out, jax.ShapeDtypeStruct((1,), F32)),
        in_specs=[vmem, vmem],
        out_specs=(vmem, vmem, pl.BlockSpec(memory_space=pltpu.SMEM)),
        compiler_params=params(),
    )(got, tile)


def shards(token_ids, teacher_query, teacher_value, student_query, student_value, teacher_pick, student_pick):
    msg_a, msg_b = pick(
        teacher_pick, student_pick, token_ids.reshape(4, 128),
        teacher_query[0], teacher_value[0], student_query[0], student_value[0],
    )
    feats = gather(teacher_pick, msg_a, msg_b)
    lse, fast = share(sums(feats))
    grad, kl = lax.cond(fast[0] > 0, grads, grads_wide, feats, lse)
    return turn(*give(grad, kl))


def solution(mesh):
    return jax.shard_map(
        shards,
        mesh=mesh,
        in_specs=(
            P("doc", "seq"),
            P("doc", "seq", "head"),
            P("doc", "seq", "head"),
            P("doc", "seq", None),
            P("doc", "seq", None),
            P(),
            P(),
        ),
        out_specs=(P("doc", "seq", "head"), P("doc", "seq", "head"), P("doc")),
        check_vma=False,
    )
```
